32 devices in a mesh: rep: 8 (over y, x, core), shard: 4 (over z).
Axes of the slice: x: 2, y: 2, z: 4, core: 2. Of those that a mesh axis runs over, the one named last changes fastest.
Arguments:
- prompt_x: bfloat16 [8, 8, 2048, 800], P(None, 'rep', 'shard'), may hold values from -6 to 6
- cont_x: bfloat16 [8, 32, 512, 800], P(None, ('rep', 'shard')), may hold values from -6 to 6
- cont_map: int32 [8, 32, 2], P(None, ('rep', 'shard')), may hold values from 0 to 7
- cont_start: int32 [8, 32, 2], P(None, ('rep', 'shard')), may hold values from 0 to 511, as said below
- w_in: float32 [800, 400], P('shard'), may hold values from -0.21875 to 0.21875
- w_conv: float32 [3, 400, 400], P(None, 'shard'), may hold values from -0.1875 to 0.1875
- w_out: float32 [400, 800], P('shard'), may hold values from -0.4375 to 0.4375
- norm1_gain: float32 [800], replicated, may hold values from 0.1 to 1.9
- norm1_bias: float32 [800], replicated, may hold values from -3 to 3
- bias_in: float32 [400], replicated, may hold values from -3 to 3
- norm2_gain: float32 [400], replicated, may hold values from 0.1 to 1.9
- norm2_bias: float32 [400], replicated, may hold values from -3 to 3
- bias_conv: float32 [400], replicated, may hold values from -3 to 3
- norm3_gain: float32 [400], replicated, may hold values from 0.1 to 1.9
- norm3_bias: float32 [400], replicated, may hold values from -3 to 3
- bias_out: float32 [800], replicated, may hold values from -3 to 3
- prompt_cot: bfloat16 [8, 8, 2048, 800], P(None, 'rep', 'shard'), may hold values from -6 to 6
- cont_cot: bfloat16 [8, 32, 512, 800], P(None, ('rep', 'shard')), may hold values from -6 to 6
Outputs:
- prompt_out: bfloat16 [8, 8, 2048, 800], P(None, 'rep', 'shard')
- cont_out: bfloat16 [8, 32, 512, 800], P(None, ('rep', 'shard'))
- prompt_grad: float32 [8, 8, 2048, 800], P(None, 'rep', 'shard')
- cont_grad: float32 [8, 32, 512, 800], P(None, ('rep', 'shard'))
- grad_w_in: float32 [800, 400], P('shard')
- grad_w_conv: float32 [3, 400, 400], P(None, 'shard')
- grad_w_out: float32 [400, 800], P('shard')
- grad_norm1_gain: float32 [800], replicated
- grad_norm1_bias: float32 [800], replicated
- grad_bias_in: float32 [400], replicated
- grad_norm2_gain: float32 [400], replicated
- grad_norm2_bias: float32 [400], replicated
- grad_bias_conv: float32 [400], replicated
- grad_norm3_gain: float32 [400], replicated
- grad_norm3_bias: float32 [400], replicated
- grad_bias_out: float32 [800], replicated
The draws below stay inside these ranges and needn't reach their ends.
Inputs may be any that keep to these rules, and one draw needn't show every extreme that they name: `cont_start`: in each buffer the 2 starts rise strictly and the first is 0; a continuation runs from its start to the next start or to the buffer's end. In the first buffer of every micro-batch the last start is 511.
All inputs are finite; a program needn't handle non-finite values.
Results may differ from the reference program's by a relative error of at most 0.0099.
Values may be sent and summed in bfloat16 or wider, within the bound.
No kernel may reach another device: no remote copies, remote signals or barrier semaphores. Data moves between devices by JAX's collectives and lax.ppermute only.
A program may use at most 256 MiB of HBM per device.

```python
import jax
import jax.numpy as jnp
from jax import lax

D = 800
INNER = 400
DILATION_STEP = 16
PROMPT_LENGTH = 2048
CONTINUATION_ROWS = 512
MB = 8
NP = 8
NBUF = 32
CONT_DEV = 2


def draw_cont_start(key, part):
    scores = jax.random.randint(key, (MB, NBUF, CONTINUATION_ROWS - 1), 0, 65536)
    scores = scores * CONTINUATION_ROWS + jnp.arange(CONTINUATION_ROWS - 1, dtype=jnp.int32)
    forced = (jnp.arange(NBUF, dtype=jnp.int32)[:, None] == 0) & (jnp.arange(CONTINUATION_ROWS - 1, dtype=jnp.int32)[None, :] == CONTINUATION_ROWS - 2)
    scores = jnp.where(forced[None], jnp.int32(65536 * CONTINUATION_ROWS + CONTINUATION_ROWS), scores)
    chosen = lax.top_k(scores, CONT_DEV - 1)[1].astype(jnp.int32) + 1
    cuts = jnp.sort(chosen, axis=-1)
    firsts = jnp.zeros((MB, NBUF, 1), jnp.int32)
    return jnp.concatenate([firsts, cuts], axis=-1).astype(jnp.int32)


def with_ends(values, rng, smallest, largest):
    extent = values.shape
    spot = [jax.random.randint(jax.random.fold_in(rng, axis), (), 0, extent[axis]) for axis in range(len(extent))]
    values = values.at[tuple(spot)].set(smallest)
    longest = extent.index(max(extent))
    spot[longest] = (spot[longest] + 1) % extent[longest]
    return values.at[tuple(spot)].set(largest)


def block_scale(rng, shape, cuts, low, high):
    factor_of = 1.0
    for dim, parts in cuts:
        steps = jax.random.uniform(jax.random.fold_in(jax.random.fold_in(rng, 6), dim), (parts,), jnp.float32, low / len(cuts), high / len(cuts))
        factor_of = factor_of * jnp.repeat(jnp.exp(steps), shape[dim] // parts).reshape((-1,) + (1,) * (len(shape) - 1 - dim))
    return factor_of


def noise(rng, extent, scale, limit, pieces=(), kind=jnp.bfloat16):
    entries = scale * jax.random.normal(rng, extent, jnp.float32)
    if pieces:
        entries = entries * block_scale(rng, extent, pieces, -0.22, 0.18)
    return jnp.clip(entries, -limit, limit).astype(kind)


def setup_inputs(seed: int = 0) -> dict:
    arg_keys = jax.random.split(jax.random.key(seed), 19)
    return {
        "prompt_x": noise(arg_keys[0], (MB, NP, PROMPT_LENGTH, D), 1.0, 6.0, ((1, 8), (2, 4))),
        "cont_x": noise(arg_keys[1], (MB, NBUF, CONTINUATION_ROWS, D), 1.0, 6.0, ((1, 32),)),
        "cont_map": with_ends(jax.random.randint(arg_keys[2], (MB, NBUF, CONT_DEV), 0, NP), jax.random.fold_in(arg_keys[2], 1), 0, NP - 1).astype(jnp.int32),
        "cont_start": draw_cont_start(jax.random.fold_in(arg_keys[18], 71), 0),
        "w_in": noise(arg_keys[4], (D, INNER), D ** -0.5, 0.21875, ((0, 4),), jnp.float32),
        "w_conv": noise(arg_keys[5], (3, INNER, INNER), (3 * INNER) ** -0.5, 0.1875, ((1, 4),), jnp.float32),
        "w_out": noise(arg_keys[6], (INNER, D), (INNER // 2) ** -0.5, 0.4375, ((0, 4),), jnp.float32),
        "norm1_gain": jnp.clip(1.0 + 0.18 * jax.random.normal(arg_keys[7], (D,), jnp.float32), 0.1, 1.9),
        "norm1_bias": noise(arg_keys[8], (D,), 0.5, 3.0, (), jnp.float32),
        "bias_in": noise(arg_keys[9], (INNER,), 0.5, 3.0, (), jnp.float32),
        "norm2_gain": jnp.clip(1.0 + 0.18 * jax.random.normal(arg_keys[10], (INNER,), jnp.float32), 0.1, 1.9),
        "norm2_bias": noise(arg_keys[11], (INNER,), 0.5, 3.0, (), jnp.float32),
        "bias_conv": noise(arg_keys[12], (INNER,), 0.5, 3.0, (), jnp.float32),
        "norm3_gain": jnp.clip(1.0 + 0.18 * jax.random.normal(arg_keys[13], (INNER,), jnp.float32), 0.1, 1.9),
        "norm3_bias": noise(arg_keys[14], (INNER,), 0.5, 3.0, (), jnp.float32),
        "bias_out": noise(arg_keys[15], (D,), 0.5, 3.0, (), jnp.float32),
        "prompt_cot": noise(arg_keys[16], (MB, NP, PROMPT_LENGTH, D), 1.0, 6.0, ((1, 8), (2, 4))),
        "cont_cot": noise(arg_keys[17], (MB, NBUF, CONTINUATION_ROWS, D), 1.0, 6.0, ((1, 32),)),
    }


@jax.custom_vjp
def low(v):
    return lax.optimization_barrier(v.astype(jnp.bfloat16)).astype(jnp.float32)

@jax.custom_vjp
def low_back(v):
    return v

def low_keep(v):
    return (low(v), None)

def low_pass(kept, grad):
    return (grad,)

def back_keep(v):
    return (v, None)

def back_low(kept, grad):
    return (low(grad),)
low.defvjp(low_keep, low_pass)
low_back.defvjp(back_keep, back_low)
epsilon = 1e-05
highest = lax.Precision.HIGHEST

def layer_norm(values, gain, shift_by):
    center = values - lax.optimization_barrier(jnp.mean(values, axis=-1, keepdims=True))
    spread = lax.optimization_barrier(jnp.mean(center * center, axis=-1, keepdims=True))
    return center * lax.rsqrt(spread + epsilon) * gain + shift_by

def project(left, right):
    return jnp.einsum('...d,de->...e', left, right, precision=highest)

def reference(prompt_x, cont_x, cont_map, cont_start, w_in, w_conv, w_out, norm1_gain, norm1_bias, bias_in, norm2_gain, norm2_bias, bias_conv, norm3_gain, norm3_bias, bias_out, prompt_cot, cont_cot):
    receptive_width = 2 * DILATION_STEP
    starts = cont_start.astype(jnp.int32)
    owners = cont_map.astype(jnp.int32)
    row_ids = jnp.arange(CONTINUATION_ROWS, dtype=jnp.int32)
    member = (lax.optimization_barrier(jnp.sum((row_ids[None, None, :, None] >= starts[:, :, None, :]).astype(jnp.int32), axis=-1)) - 1).astype(jnp.int32)
    begin = jnp.take_along_axis(starts, member, axis=2).astype(jnp.int32)
    row_position = (row_ids[None, None, :] - begin).astype(jnp.int32)
    owning_prompt = jnp.take_along_axis(owners, member, axis=2).astype(jnp.int32)
    batch_ids = jnp.arange(MB, dtype=jnp.int32)[:, None, None]

    def forward(prompt_in, cont_in, weight_in, weight_conv, weight_out, gain_one, shift_one, bias_one, gain_two, shift_two, bias_two, gain_three, shift_three, bias_three):
        low_in = low(weight_in)
        low_conv = low(weight_conv).reshape(3 * INNER, INNER)
        low_out = low(weight_out)

        def front(values):
            act_in = low(jax.nn.silu(layer_norm(values, gain_one, shift_one)))
            hidden_in = low_back(project(act_in, low_in)) + bias_one
            return low(jax.nn.silu(layer_norm(hidden_in, gain_two, shift_two)))

        def finish(values, taps):
            conv_out = low_back(project(taps, low_conv)) + bias_two
            act_conv = low(jax.nn.silu(layer_norm(conv_out, gain_three, shift_three)))
            return values + project(act_conv, low_out) + bias_three
        prompt_act = front(prompt_in)
        cont_act = front(cont_in)
        zero_padded_input = jnp.pad(prompt_act, ((0, 0), (0, 0), (receptive_width, 0), (0, 0)))
        prompt_kernel_taps = jnp.concatenate([zero_padded_input[:, :, receptive_width - kernel_tap_index * DILATION_STEP:receptive_width - kernel_tap_index * DILATION_STEP + PROMPT_LENGTH] for kernel_tap_index in range(3)], axis=-1)
        tails = prompt_act[:, :, PROMPT_LENGTH - receptive_width:].reshape(MB, NP * receptive_width, INNER)
        zero_padded_continuation = jnp.pad(cont_act, ((0, 0), (0, 0), (receptive_width, 0), (0, 0)))
        input_portions = []
        for kernel_tap_index in range(3):
            nearby_rows = zero_padded_continuation[:, :, receptive_width - kernel_tap_index * DILATION_STEP:receptive_width - kernel_tap_index * DILATION_STEP + CONTINUATION_ROWS]
            row_index = (owning_prompt * receptive_width + jnp.clip(receptive_width + row_position - kernel_tap_index * DILATION_STEP, 0, receptive_width - 1)).astype(jnp.int32)
            distant_rows = tails[batch_ids, row_index]
            input_portions.append(jnp.where((row_position >= kernel_tap_index * DILATION_STEP)[..., None], nearby_rows, distant_rows))
        cont_taps = jnp.concatenate(input_portions, axis=-1)
        return (finish(prompt_in, prompt_kernel_taps), finish(cont_in, cont_taps))
    outputs, pullback = jax.vjp(forward, prompt_x.astype(jnp.float32), cont_x.astype(jnp.float32), w_in, w_conv, w_out, norm1_gain, norm1_bias, bias_in, norm2_gain, norm2_bias, bias_conv, norm3_gain, norm3_bias, bias_out)
    grads = pullback((prompt_cot.astype(jnp.float32), cont_cot.astype(jnp.float32)))
    return (outputs[0].astype(jnp.bfloat16), outputs[1].astype(jnp.bfloat16), grads[0], grads[1], grads[2], grads[3], grads[4], grads[5], grads[6], grads[7], grads[8], grads[9], grads[10], grads[11], grads[12], grads[13])
```

```python
import functools

import jax
import jax.numpy as jnp
from jax import lax
from jax.experimental import pallas as pl
from jax.experimental.pallas import tpu as pltpu
from jax.sharding import PartitionSpec as P

STEP = 16
REACH = 2 * STEP
LANES = 128
GROUP = 4
epsilon = 1e-05
bf16 = jnp.bfloat16
f32 = jnp.float32
VMEM_BYTES = 58 * 2**20
WHOLE = pl.BlockSpec(memory_space=pltpu.VMEM)
PARAMS = pltpu.CompilerParams(vmem_limit_bytes=VMEM_BYTES)


def cost(flops, moved):
    return pl.CostEstimate(flops=int(2.5 * flops), bytes_accessed=int(moved), transcendentals=0)


def dot(a, b, ca, cb):
    return lax.dot_general(a, b, (((ca,), (cb,)), ((), ())), preferred_element_type=f32)


def at(column):
    return slice(column * LANES, (column + 1) * LANES)


def where_is(shape, column):
    per = shape[-1] // LANES
    return column // per, at(column % per)


def column_of(ref, column):
    block, lanes = where_is(ref.shape, column)
    return ref[(block,) + (0,) * (len(ref.shape) - 3) + (slice(None), lanes)]


def put_column(ref, column, values):
    block, lanes = where_is(ref.shape, column)
    ref[(block,) + (0,) * (len(ref.shape) - 3) + (slice(None), lanes)] = values


def columns_in(ref):
    return ref.shape[0] * (ref.shape[-1] // LANES)


def mean_over(values):
    return jnp.sum(values, axis=0, keepdims=True) * (1.0 / values.shape[0])


def normed_of(x):
    center = x - mean_over(x)
    scale = lax.rsqrt(mean_over(center * center) + epsilon)
    return center * scale, scale


def silu(y):
    half = 0.5 * y
    return half * jnp.tanh(half) + half


def silu_and_slope(y):
    half = 0.5 * y
    t = jnp.tanh(half)
    value = half * t + half
    sigma = 0.5 * t + 0.5
    return value, sigma + value * (1.0 - sigma)


def norm_backward(g, normed, scale, gain):
    gn = g * normed
    u = g * gain
    return gn, scale * (u - mean_over(u) - normed * mean_over(gn * gain))


def front_kernel(streams, with_rim, *refs):
    x_refs, refs = refs[:streams], refs[streams:]
    (w_in_t, vec1, vec2), refs = refs[:3], refs[3:]
    outs, refs = [refs[3 * s : 3 * s + 3] for s in range(streams)], refs[3 * streams :]
    rim_ref = refs[0] if with_rim else None
    acts = refs[-streams:]
    width = vec1.shape[1]
    for s in range(streams):
        x_ref, act = x_refs[s], acts[s]
        mid_ref, n2_ref, r2_ref = outs[s]
        columns = columns_in(x_ref)
        for c in range(columns):
            normed, _ = normed_of(column_of(x_ref, c).astype(f32))
            act[:, at(c)] = silu(normed * vec1[0] + vec1[1]).astype(bf16)
        hidden = dot(w_in_t[...], act[...], 1, 0)
        rim = []
        for c in range(columns):
            normed, scale = normed_of(hidden[:, at(c)] + vec2[0])
            value = silu(normed * vec2[1] + vec2[2])
            put_column(mid_ref, c, value.astype(bf16))
            put_column(n2_ref, c, normed.astype(bf16))
            put_column(r2_ref, c, scale)
            rim.append(value[:, LANES - REACH :])
        if with_rim:
            rim_ref[...] = jnp.concatenate(rim, axis=1).astype(bf16)


def blocks(shape, lanes, group, first):
    full = (group,) + tuple(shape[1:-1]) + (lanes,)
    return pl.BlockSpec(full, lambda i: (i,) + (0,) * (len(shape) - 2) + (first // lanes,))


def front(xs, parts, w_in_t, vec1, vec2, with_rim=False):
    inner, width = w_in_t.shape
    batches = xs[0].shape[0]
    steps = batches // parts[0][1]
    in_specs, out_specs, out_shape, scratch = [], [], [], []
    for x, (lanes, group, first) in zip(xs, parts):
        in_specs.append(blocks(x.shape, lanes, group, first))
        for depth, kind in ((inner, bf16), (inner, bf16), (1, f32)):
            out_specs.append(blocks((batches, depth, lanes), lanes, group, 0))
            out_shape.append(jax.ShapeDtypeStruct((batches, depth, lanes), kind))
        scratch.append(pltpu.VMEM((width, group * lanes), bf16))
    if with_rim:
        out_specs.append(pl.BlockSpec((inner, GROUP * REACH), lambda i: (0, i)))
        out_shape.append(jax.ShapeDtypeStruct((inner, batches * REACH), bf16))
    return pl.pallas_call(
        functools.partial(front_kernel, len(xs), with_rim),
        grid=(steps,),
        in_specs=in_specs + [WHOLE] * 3,
        out_specs=out_specs,
        out_shape=out_shape,
        scratch_shapes=scratch,
        compiler_params=PARAMS,
        cost_estimate=cost(4 * width * inner * sum(batches * part[0] for part in parts), 0),
        name="front",
    )(*xs, w_in_t, vec1, vec2)


def shifted_right(values, by):
    zeros = jnp.zeros((values.shape[0], by), values.dtype)
    return jnp.concatenate([zeros, values[:, : values.shape[1] - by]], axis=1)


def shifted_left(values, by):
    zeros = jnp.zeros((values.shape[0], by), values.dtype)
    return jnp.concatenate([values[:, by:], zeros], axis=1)


def chosen(base, position, fits, batches):
    one = jnp.where(jnp.logical_and(fits, position < STEP), base + STEP + position, -1)
    two = jnp.where(jnp.logical_and(fits, position < REACH), base + position, -1)
    target = jnp.concatenate([one, two], axis=1)
    row = lax.broadcasted_iota(jnp.int32, (batches * REACH, target.shape[1]), 0)
    return jnp.where(row == target, 1.0, 0.0).astype(bf16)


def middle_kernel(batches, prompts, group, pieces, has_before, has_after, *refs):
    if not prompts:
        (cont_start, cont_map), refs = refs[:2], refs[2:]
    mids, refs = refs[:pieces], refs[pieces:]
    (x_ref, cot_ref, tails), refs = refs[:3], refs[3:]
    (w_conv_t, w_conv, w_out_t, w_out, vec3, bias_out), refs = refs[:6], refs[6:]
    if has_before:
        before, refs = refs[:4], refs[4:]
    out_ref, gs, refs = refs[0], refs[1 : 1 + pieces], refs[1 + pieces :]
    sums, table, refs = refs[:4], refs[4], refs[5:]
    if has_after:
        (out_chunks, conv_chunks), refs = refs[:2], refs[2:]
    gw_out, gw_conv, g_gain3, g_shift3 = sums
    scratch = [refs[4 * q : 4 * q + 4] for q in range(group)]
    width, inner = w_out_t.shape
    step = pl.program_id(0)

    @pl.when(step == 0)
    def _():
        for k, ref in enumerate(sums):
            ref[...] = before[k][...] if has_before else jnp.zeros_like(ref)
        table[...] = jnp.zeros_like(table)
        for taps, act, _, _ in scratch:
            taps[3 * inner :, :] = jnp.ones_like(taps[3 * inner :, :])
            act[inner:, :] = jnp.ones_like(act[inner:, :])

    for q in range(group):
        taps, act, gc, gt = scratch[q]
        m = step * group + q
        base = m * REACH
        length = taps.shape[1]
        columns = length // LANES
        mid = mids[0][q] if pieces == 1 else jnp.concatenate([ref[q] for ref in mids], axis=1)
        lane = lax.broadcasted_iota(jnp.int32, (1, LANES), 1)
        if prompts:
            begin = chosen(base, lane, lane >= 0, batches)
            before_rows = tails[...]
        else:
            start = cont_start[m, 0, 1]
            owners = cont_map[m, 0, 0], cont_map[m, 0, 1]
            at_most = (length // LANES - 2) * LANES
            window = jnp.minimum(lax.shift_right_logical(start, 7) * LANES, at_most)
            window = pl.multiple_of(window, LANES)
            begin = chosen(base, lane, lane < start, batches)
            before_rows = tails[owners[0]]
        first = dot(before_rows, begin, 1, 0).astype(bf16)
        taps[0:inner, :] = mid
        one, two = shifted_right(mid, STEP), shifted_right(mid, REACH)
        if not prompts:
            row = lax.broadcasted_iota(jnp.int32, (1, length), 1)
            since = jnp.where(row < start, row, row - start)
            near_one = jnp.where(since >= STEP, 1.0, 0.0)
            near_two = jnp.where(since >= REACH, 1.0, 0.0)
            full = lambda w: jnp.broadcast_to(w, (inner, length)).astype(bf16)
            one, two = one * full(near_one), two * full(near_two)
        taps[inner : 2 * inner, :] = one
        taps[2 * inner : 3 * inner, :] = two
        taps[inner : 2 * inner, :LANES] += first[:, :LANES]
        taps[2 * inner : 3 * inner, :LANES] += first[:, LANES:]
        if not prompts:
            wide = pl.ds(window, 2 * LANES)
            offset = window + lax.broadcasted_iota(jnp.int32, (1, 2 * LANES), 1) - start
            later = chosen(base, offset, offset >= 0, batches)
            far = dot(tails[owners[1]], later, 1, 0).astype(bf16)
            taps[inner : 2 * inner, wide] += far[:, : 2 * LANES]
            taps[2 * inner : 3 * inner, wide] += far[:, 2 * LANES :]
        cot = cot_ref[q, 0]
        conv = dot(w_conv_t[...], taps[0 : 3 * inner, :], 1, 0)
        g_act = dot(w_out[...], cot, 1, 0)
        for c in range(columns):
            normed, scale = normed_of(conv[:, at(c)] + vec3[0])
            value, slope = silu_and_slope(normed * vec3[1] + vec3[2])
            act[0:inner, at(c)] = value.astype(bf16)
            g = g_act[:, at(c)] * slope
            gn, g_in = norm_backward(g, normed, scale, vec3[1])
            g_gain3[...] += gn
            g_shift3[...] += g
            gc[:, at(c)] = g_in.astype(bf16)
        branch = dot(w_out_t[...], act[0:inner, :], 1, 0)
        for c in range(columns):
            y = x_ref[q, 0, :, at(c)].astype(f32) + (branch[:, at(c)] + bias_out[...])
            out_ref[q, 0, :, at(c)] = y.astype(bf16)
        gw_out[...] += dot(cot, act[...], 1, 1)
        gw_conv[...] += dot(gc[...], taps[...], 1, 1)
        g_taps = dot(w_conv[...], gc[...], 1, 0)
        g0, g1, g2 = (g_taps[k * inner : (k + 1) * inner] for k in range(3))
        both = jnp.concatenate([g1[:, :LANES], g2[:, :LANES]], axis=1).astype(bf16)
        back = dot(both, begin, 1, 1)
        if prompts:
            table[...] += back
        else:
            table[owners[0]] += back
            gt[0] = g1.astype(bf16)
            gt[1] = g2.astype(bf16)
            both = jnp.concatenate([gt[0, :, wide], gt[1, :, wide]], axis=1)
            table[owners[1]] += dot(both, later, 1, 1)
            g1, g2 = g1 * near_one, g2 * near_two
        g_mid = (g0 + shifted_left(g1, STEP) + shifted_left(g2, REACH)).astype(bf16)
        if pieces == 1:
            gs[0][q] = g_mid
        else:
            gs[0][q] = g_mid[:, : length - LANES]
            gs[1][q] = g_mid[:, length - LANES :]

    if has_after:

        @pl.when(step == pl.num_programs(0) - 1)
        def _():
            count, few, _ = conv_chunks.shape
            many = out_chunks.shape[1]
            gw_conv[:, 3 * inner + 1 : 3 * inner + 2] = jnp.sum(g_gain3[...], axis=1, keepdims=True)
            gw_conv[:, 3 * inner + 2 : 3 * inner + 3] = jnp.sum(g_shift3[...], axis=1, keepdims=True)
            for r in range(count):
                out_chunks[r] = gw_out[r * many : (r + 1) * many, : inner + 1]
                conv_chunks[r] = gw_conv[r * few : (r + 1) * few, : 3 * inner + 3]


def middle(prompts, group, scalars, mids, x, cot, tails, weights, before=None, chunks=0):
    batches, _, width, length = x.shape
    inner = mids[0].shape[1]
    block = lambda a: blocks(a.shape, a.shape[-1], group, 0)
    args = list(scalars) + mids + [x, cot, tails] + list(weights) + list(before or ())
    in_specs = [pl.BlockSpec(memory_space=pltpu.SMEM)] * len(scalars)
    in_specs += [block(a) for a in mids + [x, cot]]
    in_specs += [WHOLE] * (len(args) - len(in_specs))
    out_like = [jax.ShapeDtypeStruct(x.shape, bf16)]
    out_like += [jax.ShapeDtypeStruct(mid.shape, bf16) for mid in mids]
    sums = [
        (width, inner + 16),
        (inner, 3 * inner + 16),
        (inner, LANES),
        (inner, LANES),
        tails.shape,
    ]
    if chunks:
        sums += [(chunks, width // chunks, inner + 1), (chunks, inner // chunks, 3 * inner + 3)]
    scratch = []
    for _ in range(group):
        scratch += [
            pltpu.VMEM((3 * inner + 16, length), bf16),
            pltpu.VMEM((inner + 16, length), bf16),
            pltpu.VMEM((inner, length), bf16),
            pltpu.VMEM((2, inner, length), bf16),
        ]
    return pl.pallas_call(
        functools.partial(
            middle_kernel, batches, prompts, group, len(mids), before is not None, chunks > 0
        ),
        grid=(batches // group,),
        in_specs=in_specs,
        out_specs=[block(a) for a in out_like] + [WHOLE] * len(sums),
        out_shape=out_like + [jax.ShapeDtypeStruct(shape, f32) for shape in sums],
        scratch_shapes=scratch,
        compiler_params=PARAMS,
        cost_estimate=cost(batches * length * 9 * inner * width, 3 * x.size * 2),
        name="middle",
    )(*args)


def back_kernel(has_rim, has_before, has_into, has_after, *refs):
    (x_ref, cot_ref, g_ref, n2_ref, r2_ref), refs = refs[:5], refs[5:]
    (w_in, vec1, vec2), refs = refs[:3], refs[3:]
    if has_rim:
        rim, refs = refs[0], refs[1:]
    if has_before:
        before, refs = refs[:5], refs[5:]
    if has_into:
        refs = refs[1:]
    out_ref, sums, refs = refs[0], refs[1:6], refs[6:]
    if has_after:
        (in_chunks, one_chunks), refs = refs[:2], refs[2:]
    act, gh = refs
    gw_in, g_gain2, g_shift2, g_gain1, g_shift1 = sums
    width, inner = w_in.shape
    step = pl.program_id(0)

    @pl.when(step == 0)
    def _():
        for k, ref in enumerate(sums):
            ref[...] = before[k][...] if has_before else jnp.zeros_like(ref)
        act[width:, :] = jnp.ones_like(act[width:, :])

    columns = columns_in(x_ref)
    for c in range(columns):
        normed = column_of(n2_ref, c).astype(f32)
        _, slope = silu_and_slope(normed * vec2[1] + vec2[2])
        g = column_of(g_ref, c).astype(f32)
        if has_rim:
            piece = rim[:, c * REACH : (c + 1) * REACH]
            g += jnp.concatenate([jnp.zeros((inner, LANES - REACH), f32), piece], axis=1)
        g = g * slope
        gn, g_in = norm_backward(g, normed, column_of(r2_ref, c), vec2[1])
        g_gain2[...] += gn
        g_shift2[...] += g
        gh[:, at(c)] = g_in.astype(bf16)
    g_act = dot(w_in[...], gh[...], 1, 0)
    for c in range(columns):
        normed, scale = normed_of(column_of(x_ref, c).astype(f32))
        value, slope = silu_and_slope(normed * vec1[0] + vec1[1])
        act[0:width, at(c)] = value.astype(bf16)
        g = g_act[:, at(c)] * slope
        gn, g_in = norm_backward(g, normed, scale, vec1[0])
        g_gain1[...] += gn
        g_shift1[...] += g
        put_column(out_ref, c, column_of(cot_ref, c).astype(f32) + g_in)
    gw_in[...] += dot(gh[...], act[...], 1, 1)

    if has_after:

        @pl.when(step == pl.num_programs(0) - 1)
        def _():
            count, few, _ = in_chunks.shape
            many = one_chunks.shape[1]
            gw_in[:, width + 1 : width + 2] = jnp.sum(g_gain2[...], axis=1, keepdims=True)
            gw_in[:, width + 2 : width + 3] = jnp.sum(g_shift2[...], axis=1, keepdims=True)
            g_gain1[:, 0:1] = jnp.sum(g_gain1[...], axis=1, keepdims=True)
            g_gain1[:, 1:2] = jnp.sum(g_shift1[...], axis=1, keepdims=True)
            for r in range(count):
                in_chunks[r] = gw_in[r * few : (r + 1) * few, : width + 3]
                one_chunks[r] = g_gain1[r * many : (r + 1) * many, 0:2]


def back(x, cot, g, n2, r2, part, w_in, vec1, vec2, rim=None, before=None, into=None, chunks=0):
    width, inner = w_in.shape
    batches = x.shape[0]
    lanes, group, first = part
    block = blocks(x.shape, lanes, group, first)
    in_specs = [block, block] + [blocks(a.shape, lanes, group, 0) for a in (g, n2, r2)] + [WHOLE] * 3
    args = [x, cot, g, n2, r2, w_in, vec1, vec2]
    if rim is not None:
        args.append(rim)
        in_specs.append(pl.BlockSpec((inner, GROUP * REACH), lambda i: (0, i)))
    if before is not None:
        args += before
        in_specs += [WHOLE] * 5
    aliases = {}
    if into is not None:
        aliases = {len(args): 0}
        args.append(into)
        in_specs.append(pl.BlockSpec(memory_space=pl.ANY))
    sums = [(inner, width + 16), (inner, LANES), (inner, LANES), (width, LANES), (width, LANES)]
    if chunks:
        sums += [(chunks, inner // chunks, width + 3), (chunks, width // chunks, 2)]
    return pl.pallas_call(
        functools.partial(
            back_kernel, rim is not None, before is not None, into is not None, chunks > 0
        ),
        grid=(batches // group,),
        in_specs=in_specs,
        out_specs=[block] + [WHOLE] * len(sums),
        out_shape=[jax.ShapeDtypeStruct(x.shape, f32)]
        + [jax.ShapeDtypeStruct(shape, f32) for shape in sums],
        scratch_shapes=[
            pltpu.VMEM((width + 16, group * lanes), bf16),
            pltpu.VMEM((inner, group * lanes), bf16),
        ],
        input_output_aliases=aliases,
        compiler_params=PARAMS,
        cost_estimate=cost(10 * width * inner * batches * lanes, 0),
        name="back",
    )(*args)


def passed_along(x, axis, by):
    size = lax.axis_size(axis)
    pairs = [(i, i + by) for i in range(size) if 0 <= i + by < size]
    return lax.ppermute(x, axis, pairs)


def gathered(x, axis):
    size = lax.axis_size(axis)
    if size > 4:
        return lax.all_gather(x, axis)
    me = lax.axis_index(axis)
    total = jnp.zeros((size,) + x.shape, x.dtype)
    for k in range(size):
        piece = x if k == 0 else lax.ppermute(x, axis, [(i, i ^ k) for i in range(size)])
        total = lax.dynamic_update_index_in_dim(total, piece, me ^ k, 0)
    return total


def sent_from_last(x, axis):
    size = lax.axis_size(axis)
    me = lax.axis_index(axis)
    value = x
    for j in range(size - 1):
        piece = lax.ppermute(x, axis, [(size - 1, j)])
        value = jnp.where(me == j, piece, value)
    return value


def summed_at_last(x, axis):
    size = lax.axis_size(axis)
    total = x.astype(f32)
    for j in range(size - 1):
        total = total + lax.ppermute(x, axis, [(j, size - 1)]).astype(f32)
    return total


def on_device(
    prompt_x,
    cont_x,
    cont_map,
    cont_start,
    w_in,
    w_conv,
    w_out,
    norm1_gain,
    norm1_bias,
    bias_in,
    norm2_gain,
    norm2_bias,
    bias_conv,
    norm3_gain,
    norm3_bias,
    bias_out,
    prompt_cot,
    cont_cot,
):
    inner = w_conv.shape[2]
    turned = lambda a: jnp.swapaxes(a, 2, 3)
    prompt_x, cont_x, prompt_cot, cont_cot = map(turned, (prompt_x, cont_x, prompt_cot, cont_cot))
    width = prompt_x.shape[2]
    shards, reps = lax.axis_size("shard"), lax.axis_size("rep")
    is_last = lax.axis_index("shard") == shards - 1
    low_in = gathered(w_in.astype(bf16), "shard").reshape(width, inner)
    own = w_out.shape[0]
    packed = jnp.concatenate(
        [w_conv.reshape(3 * own, inner), w_out[:, :inner], w_out[:, inner:]], axis=0
    ).astype(bf16)
    packed = gathered(packed, "shard")
    low_conv = packed[:, : 3 * own].reshape(shards, 3, own, inner).transpose(1, 0, 2, 3)
    low_conv = low_conv.reshape(3 * inner, inner)
    low_out = packed[:, 3 * own :].reshape(shards, 2, own, inner).transpose(0, 2, 1, 3)
    low_out = low_out.reshape(inner, width)
    spread = lambda *v: jnp.broadcast_to(jnp.stack(v)[:, :, None], (len(v), v[0].shape[0], LANES))
    vec1 = spread(norm1_gain, norm1_bias)
    vec2 = spread(bias_in, norm2_gain, norm2_bias)
    vec3 = spread(bias_conv, norm3_gain, norm3_bias)
    vec_out = spread(bias_out)[0]

    rows_p, rows_c = prompt_x.shape[3], cont_x.shape[3]
    last = (LANES, GROUP, rows_p - LANES)
    rest = (rows_p - LANES, 1, 0)
    every = (rows_c, 1, 0)
    have_first = rows_p > LANES
    w_in_t = low_in.T
    mid_l, n2_l, r2_l, rim = front([prompt_x], [last], w_in_t, vec1, vec2, with_rim=True)
    halo = passed_along(rim, "shard", 1)
    tails = lax.all_gather(sent_from_last(rim, "shard"), "rep", axis=0)
    if have_first:
        mid_f, n2_f, r2_f, mid_c, n2_c, r2_c = front(
            [prompt_x, cont_x], [rest, every], w_in_t, vec1, vec2
        )
        mids = [mid_f, mid_l]
    else:
        mid_c, n2_c, r2_c = front([cont_x], [every], w_in_t, vec1, vec2)
        mids = [mid_l]

    weights = (low_conv.T, low_conv, low_out.T, low_out, vec3, vec_out)
    prompt_out, *results = middle(True, 1, [], mids, prompt_x, prompt_cot, halo, weights)
    g_ps, results = results[: len(mids)], results[len(mids) :]
    sums, rim_out = results[:4], results[4]
    cont_out, g_c, *sums, table, out_chunks, conv_chunks = middle(
        False,
        1,
        [cont_start, cont_map],
        [mid_c],
        cont_x,
        cont_cot,
        tails,
        weights,
        before=sums,
        chunks=reps,
    )
    back_rim = passed_along(rim_out.astype(bf16), "shard", -1).astype(f32)
    own_tail = lax.psum_scatter(table, "rep", scatter_dimension=0)
    own_tail = summed_at_last(own_tail.astype(bf16), "shard")
    rim_in = back_rim + jnp.where(is_last, own_tail, 0.0)
    out_chunks = lax.psum_scatter(out_chunks, "rep", scatter_dimension=0)
    conv_chunks = lax.psum_scatter(conv_chunks, "rep", scatter_dimension=0)

    sums = None
    prompt_grad = None
    if have_first:
        prompt_grad, *sums = back(
            prompt_x, prompt_cot, g_ps[0], n2_f, r2_f, rest, low_in, vec1, vec2
        )
    cont_grad, *sums = back(
        cont_x, cont_cot, g_c, n2_c, r2_c, every, low_in, vec1, vec2, before=sums
    )
    prompt_grad, *results = back(
        prompt_x,
        prompt_cot,
        g_ps[-1],
        n2_l,
        r2_l,
        last,
        low_in,
        vec1,
        vec2,
        rim=rim_in,
        before=sums,
        into=prompt_grad,
        chunks=reps,
    )
    in_chunks, one_chunks = results[5:]
    swapped = lambda a, axis: lax.all_to_all(a.astype(bf16), axis, 0, 0, tiled=True).astype(f32)
    in_chunks = jnp.sum(swapped(in_chunks, "rep"), axis=0)
    one_chunks = jnp.sum(swapped(one_chunks, "rep"), axis=0)

    few = inner // reps
    twice = width // inner
    halves = lambda a: jnp.concatenate(jnp.split(a, twice, axis=0), axis=1)
    part_out = halves(out_chunks)
    kept = [part_out[:, h * (inner + 1) + inner][:, None] for h in range(twice)]
    kept += [halves(one_chunks), conv_chunks[:, 3 * inner :], in_chunks[:, width:]]
    kept = jnp.concatenate(kept, axis=1)
    pieces = []
    for j in range(shards):
        wide = width // shards
        parts = [part_out[:, h * (inner + 1) + j * own :][:, :own] for h in range(twice)]
        parts += [conv_chunks[:, k * inner + j * own :][:, :own] for k in range(3)]
        parts += [in_chunks[:, j * wide : (j + 1) * wide], kept]
        pieces.append(jnp.concatenate(parts, axis=1))
    mine = jnp.sum(swapped(jnp.stack(pieces), "shard"), axis=0)
    whole = lax.all_gather(mine, "rep")
    a, b, c = twice * own, (twice + 3) * own, (twice + 3) * own + width // shards
    grad_w_out = whole[:, :, :a].reshape(reps, few, twice, own).transpose(3, 0, 2, 1)
    grad_w_out = grad_w_out.reshape(own, width)
    grad_w_conv = whole[:, :, a:b].reshape(inner, 3, own).transpose(1, 2, 0)
    grad_w_in = whole[:, :, b:c].reshape(inner, width // shards).T
    small = whole[:, :, c:]
    by_width = lambda v: v.transpose(0, 2, 1).reshape(width)
    grad_bias_out = by_width(small[:, :, :twice])
    ones = small[:, :, twice : 3 * twice].reshape(reps, few, twice, 2)
    grad_gain1, grad_shift1 = by_width(ones[..., 0]), by_width(ones[..., 1])
    by_inner = [small[:, :, 3 * twice + k].reshape(inner) for k in range(6)]
    grad_bias_conv, grad_gain3, grad_shift3, grad_bias_in, grad_gain2, grad_shift2 = by_inner
    return (
        turned(prompt_out),
        turned(cont_out),
        turned(prompt_grad),
        turned(cont_grad),
        grad_w_in,
        grad_w_conv,
        grad_w_out,
        grad_gain1,
        grad_shift1,
        grad_bias_in,
        grad_gain2,
        grad_shift2,
        grad_bias_conv,
        grad_gain3,
        grad_shift3,
        grad_bias_out,
    )


def solution(mesh):
    rows = P(None, "rep", "shard", None)
    buffers = P(None, ("rep", "shard"), None, None)
    in_specs = (
        rows,
        buffers,
        P(None, ("rep", "shard"), None),
        P(None, ("rep", "shard"), None),
        P("shard", None),
        P(None, "shard", None),
        P("shard", None),
    ) + (P(),) * 9 + (rows, buffers)
    out_specs = (
        rows,
        buffers,
        rows,
        buffers,
        P("shard", None),
        P(None, "shard", None),
        P("shard", None),
    ) + (P(),) * 9
    return jax.shard_map(
        on_device, mesh=mesh, in_specs=in_specs, out_specs=out_specs, check_vma=False
    )
```

```python
import functools

import jax
import jax.numpy as jnp
from jax import lax
from jax.experimental import pallas as pl
from jax.experimental.pallas import tpu as pltpu
from jax.sharding import PartitionSpec as P

STEP = 16
REACH = 2 * STEP
LANES = 128
GROUP = 4
TILE = 16
epsilon = 1e-05
bf16 = jnp.bfloat16
f32 = jnp.float32
VMEM_BYTES = 58 * 2**20
WHOLE = pl.BlockSpec(memory_space=pltpu.VMEM)
PARAMS = pltpu.CompilerParams(vmem_limit_bytes=VMEM_BYTES)


def cost(flops, moved):
    return pl.CostEstimate(flops=int(2.5 * flops), bytes_accessed=int(moved), transcendentals=0)


def dot(a, b, ca, cb):
    return lax.dot_general(a, b, (((ca,), (cb,)), ((), ())), preferred_element_type=f32)


def at(column):
    return slice(column * LANES, (column + 1) * LANES)


def tiles(depth):
    return [slice(r, r + TILE) for r in range(0, depth, TILE)]


class Columns:
    def __init__(self, ref):
        self.ref = ref
        self.per = ref.shape[-1] // LANES
        self.count = ref.shape[0] * self.per

    def key(self, rows, c):
        return (c // self.per,) + (0,) * (len(self.ref.shape) - 3) + (rows, at(c % self.per))

    def get(self, rows, c):
        return self.ref[self.key(rows, c)].astype(f32)

    def put(self, rows, c, values):
        self.ref[self.key(rows, c)] = values.astype(self.ref.dtype)


ROW = slice(0, 1)


def down(values):
    return jnp.sum(values, axis=0, keepdims=True)


def stats(load, depth, columns):
    zero = jnp.zeros((TILE, LANES), f32)
    sums = [zero] * columns
    for t in tiles(depth):
        sums = [s + load(t, c) for c, s in enumerate(sums)]
    means = [down(s) * (1.0 / depth) for s in sums]
    sums = [zero] * columns
    for t in tiles(depth):
        for c in range(columns):
            center = load(t, c) - means[c]
            sums[c] = sums[c] + center * center
    scales = [lax.rsqrt(down(s) * (1.0 / depth) + epsilon) for s in sums]
    return means, scales


def halved(vec):
    return 0.5 * vec


def backward_pass(columns, depth, normed, g_in, vec, sums, keep, act=None):
    g_gain, g_shift = sums
    zero = jnp.zeros((TILE, LANES), f32)
    totals = [[zero, zero] for _ in range(columns)]
    for t in tiles(depth):
        gain, shift = vec[0, t, :], vec[1, t, :]
        half_gain, half_shift = halved(gain), halved(shift)
        gains = shifts = None
        for c in range(columns):
            n = normed(t, c)
            half = n * half_gain + half_shift
            tan = jnp.tanh(half)
            if act is not None:
                act(t, c, half * tan + half)
            slope = (1.0 + tan) * (1.0 + half * (1.0 - tan))
            g = g_in(t, c) * slope
            gn = g * n
            u = g * gain
            keep(t, c, u)
            totals[c][0] = totals[c][0] + u
            totals[c][1] = totals[c][1] + gn * gain
            gains = gn if gains is None else gains + gn
            shifts = g if shifts is None else shifts + g
        g_gain[t, :] += gains
        g_shift[t, :] += shifts
    return [[down(s) * (1.0 / depth) for s in pair] for pair in totals]


def blocks(shape, lanes, group, first, batch=0):
    full = (group,) + tuple(shape[1:-1]) + (lanes,)
    zeros = (0,) * (len(shape) - 2)
    return pl.BlockSpec(full, lambda i: (i + batch // group,) + zeros + (first // lanes,))


def shape_of(*shape, kind=f32):
    return jax.ShapeDtypeStruct(shape, kind)


def splits(own):
    return 2 if own % 2 == 0 else 1


def sending_kernel(ids, w_in, w_conv_t, w_out, *refs):
    rows, (in_part, rest_part), vecs = refs[:6], refs[6:8], refs[8:]
    own, width = w_out.shape
    inner = w_conv_t.shape[1]
    parts = splits(own)
    few = own // parts
    in_part[...] = w_in[...].astype(bf16)
    conv = [w_conv_t[k].T for k in range(3)]
    for h in range(parts):

        @pl.when(ids[1] % parts == h)
        def _():
            mine = slice(h * few, (h + 1) * few)
            pieces = [turn[mine] for turn in conv]
            pieces += [w_out[mine, q : q + inner] for q in range(0, width, inner)]
            rest_part[...] = jnp.concatenate(pieces, axis=0).astype(bf16)

    for k, row in enumerate(rows):
        wide = jnp.broadcast_to(row[...], (LANES, row.shape[1]))
        vecs[k // 2][k % 2] = wide.T


def sending(ids, w_in, w_conv, w_out, rows):
    own, width = w_out.shape
    inner = w_conv.shape[2]
    parts = splits(own)
    return pl.pallas_call(
        sending_kernel,
        in_specs=[pl.BlockSpec(memory_space=pltpu.SMEM)] + [WHOLE] * 9,
        out_specs=[WHOLE] * 5,
        out_shape=[
            shape_of(*w_in.shape, kind=bf16),
            shape_of((3 + width // inner) * own // parts, inner, kind=bf16),
            shape_of(2, width, LANES),
            shape_of(2, inner, LANES),
            shape_of(2, inner, LANES),
        ],
        compiler_params=PARAMS,
        name="sending",
    )(ids, w_in, jnp.swapaxes(w_conv, 1, 2), w_out, *[row[None] for row in rows])


def with_shift(weights, shift):
    parts = []
    left = shift
    for _ in range(3):
        part = left.astype(bf16).astype(f32)
        parts.append(part)
        left = left - part
    parts.append(jnp.zeros((13, shift.shape[1]), f32))
    return jnp.concatenate([weights.T, jnp.concatenate(parts, axis=0).T], axis=1).astype(bf16)


def taking_in_kernel(ids, pieces, bias, half_in, w_in_t, total):
    shards, some, _ = pieces.shape
    for j in range(shards):
        total[j * some : (j + 1) * some, :] = pieces[ids[0] ^ j].astype(f32)
    half_in[...] = (0.5 * total[...]).astype(bf16)
    w_in_t[...] = with_shift(total[...], bias[...])


def taking_in(ids, pieces, bias):
    shards, some, inner = pieces.shape
    width = shards * some
    return pl.pallas_call(
        taking_in_kernel,
        in_specs=[pl.BlockSpec(memory_space=pltpu.SMEM)] + [WHOLE] * 2,
        out_specs=[WHOLE] * 2,
        out_shape=[shape_of(width, inner, kind=bf16), shape_of(inner, width + 16, kind=bf16)],
        scratch_shapes=[pltpu.VMEM((width, inner), f32)],
        compiler_params=PARAMS,
        name="taking_in",
    )(ids, pieces, bias[None])


def taking_rest_kernel(ids, pieces, bias_conv, bias_out, *refs):
    (w_conv_t, half_conv, w_out_t, half_out), (conv, out) = refs[:4], refs[4:]
    parts, shards, rows, inner = pieces.shape
    width = out.shape[1]
    few = rows // (3 + width // inner)
    for j in range(shards):
        for h in range(parts):
            first = (j * parts + h) * few
            piece = pieces[h ^ (ids[1] % parts), ids[0] ^ j].astype(f32)
            for k in range(3):
                conv[k * inner + first : k * inner + first + few, :] = piece[k * few : (k + 1) * few]
            halves = [piece[k * few : (k + 1) * few] for k in range(3, 3 + width // inner)]
            out[first : first + few, :] = jnp.concatenate(halves, axis=1)
    half_conv[...] = (0.5 * conv[...]).astype(bf16)
    w_conv_t[...] = with_shift(conv[...], bias_conv[...])
    half_out[...] = (0.5 * out[...]).astype(bf16)
    w_out_t[...] = with_shift(out[...], bias_out[...])


def taking_rest(ids, pieces, bias_conv, bias_out):
    inner, width = bias_conv.shape[0], bias_out.shape[0]
    return pl.pallas_call(
        taking_rest_kernel,
        in_specs=[pl.BlockSpec(memory_space=pltpu.SMEM)] + [WHOLE] * 3,
        out_specs=[WHOLE] * 4,
        out_shape=[
            shape_of(inner, 3 * inner + 16, kind=bf16),
            shape_of(3 * inner, inner, kind=bf16),
            shape_of(width, inner + 16, kind=bf16),
            shape_of(inner, width, kind=bf16),
        ],
        scratch_shapes=[pltpu.VMEM((3 * inner, inner), f32), pltpu.VMEM((inner, width), f32)],
        compiler_params=PARAMS,
        name="taking_rest",
    )(ids, pieces, bias_conv[None], bias_out[None])


def lead_kernel(*refs):
    x_refs, vec1, outs = refs[:2], refs[2], refs[3:]
    for s in range(2):
        x, act, mean, scale = (Columns(ref) for ref in (x_refs[s],) + tuple(outs[3 * s : 3 * s + 3]))
        depth = x_refs[s].shape[-2]
        means, scales = stats(x.get, depth, x.count)
        for c in range(x.count):
            mean.put(ROW, c, means[c])
            scale.put(ROW, c, scales[c])
        shifts = [m * v for m, v in zip(means, scales)]
        for t in tiles(depth):
            gain, shift = halved(vec1[0, t, :]), halved(vec1[1, t, :])
            for c in range(x.count):
                half = (x.get(t, c) * scales[c] - shifts[c]) * gain + shift
                act.put(t, c, half * jnp.tanh(half) + half)
        for c in range(x.count):
            act.put(slice(depth, depth + 16), c, jnp.ones((16, LANES), f32))


def lead(xs, vec1):
    batches, _, width, _ = xs[0].shape
    in_specs, out_specs, out_shape = [], [], []
    for x in xs:
        lanes = x.shape[3]
        in_specs.append(blocks(x.shape, lanes, 1, 0))
        for depth, kind in ((width + 16, bf16), (1, f32), (1, f32)):
            out_specs.append(blocks((batches, depth, lanes), lanes, 1, 0))
            out_shape.append(shape_of(batches, depth, lanes, kind=kind))
    return pl.pallas_call(
        lead_kernel,
        grid=(batches,),
        in_specs=in_specs + [WHOLE],
        out_specs=out_specs,
        out_shape=out_shape,
        compiler_params=PARAMS,
        cost_estimate=cost(0, sum(x.size for x in xs) * 4),
        name="lead",
    )(*xs, vec1)


def front_kernel(streams, with_rim, *refs):
    acts, refs = refs[:streams], refs[streams:]
    (w_in_t, vec2), refs = refs[:2], refs[2:]
    outs, refs = [refs[3 * s : 3 * s + 3] for s in range(streams)], refs[3 * streams :]
    rim_ref = refs[0] if with_rim else None
    hiddens = refs[-streams:]
    inner = w_in_t.shape[0]
    for s in range(streams):
        act, hidden = acts[s], hiddens[s]
        mid, n2, r2 = (Columns(ref) for ref in outs[s])
        wide = act.shape[2]
        for q in range(act.shape[0]):
            hidden[:, q * wide : (q + 1) * wide] = dot(w_in_t[...], act[q], 1, 0)
        load = lambda t, c: hidden[t, at(c)]
        means, scales = stats(load, inner, mid.count)
        shifts = [m * v for m, v in zip(means, scales)]
        for c in range(mid.count):
            r2.put(ROW, c, scales[c])
        for t in tiles(inner):
            gain, shift = halved(vec2[0, t, :]), halved(vec2[1, t, :])
            rim = []
            for c in range(mid.count):
                n = load(t, c) * scales[c] - shifts[c]
                half = n * gain + shift
                value = half * jnp.tanh(half) + half
                mid.put(t, c, value)
                n2.put(t, c, n)
                rim.append(value[:, LANES - REACH :])
            if with_rim:
                rim_ref[t, :] = jnp.concatenate(rim, axis=1).astype(bf16)


def front(acts, parts, w_in_t, vec2, with_rim=False):
    inner = w_in_t.shape[0]
    batches = acts[0].shape[0]
    in_specs, out_specs, out_shape, scratch = [], [], [], []
    for act, (lanes, group, first) in zip(acts, parts):
        in_specs.append(blocks(act.shape, lanes, group, first))
        for depth, kind in ((inner, bf16), (inner, bf16), (1, f32)):
            out_specs.append(blocks((batches, depth, lanes), lanes, group, 0))
            out_shape.append(shape_of(batches, depth, lanes, kind=kind))
        scratch.append(pltpu.VMEM((inner, group * lanes), f32))
    if with_rim:
        out_specs.append(pl.BlockSpec((inner, GROUP * REACH), lambda i: (0, i)))
        out_shape.append(shape_of(inner, batches * REACH, kind=bf16))
    return pl.pallas_call(
        functools.partial(front_kernel, len(acts), with_rim),
        grid=(batches // parts[0][1],),
        in_specs=in_specs + [WHOLE] * 2,
        out_specs=out_specs,
        out_shape=out_shape,
        scratch_shapes=scratch,
        compiler_params=PARAMS,
        cost_estimate=cost(4 * w_in_t.size * sum(batches * part[0] for part in parts), 0),
        name="front",
    )(*acts, w_in_t, vec2)


def shifted_right(values, by):
    zeros = jnp.zeros((values.shape[0], by), values.dtype)
    return jnp.concatenate([zeros, values[:, : values.shape[1] - by]], axis=1)


def shifted_left(values, by):
    zeros = jnp.zeros((values.shape[0], by), values.dtype)
    return jnp.concatenate([values[:, by:], zeros], axis=1)


def chosen(base, position, fits, batches):
    one = jnp.where(jnp.logical_and(fits, position < STEP), base + STEP + position, -1)
    two = jnp.where(jnp.logical_and(fits, position < REACH), base + position, -1)
    target = jnp.concatenate([one, two], axis=1)
    row = lax.broadcasted_iota(jnp.int32, (batches * REACH, target.shape[1]), 0)
    return jnp.where(row == target, 1.0, 0.0).astype(bf16)


def middle_kernel(batches, prompts, group, pieces, has_before, has_after, *refs):
    if not prompts:
        (cont_start, cont_map), refs = refs[:2], refs[2:]
    mids, refs = refs[:pieces], refs[pieces:]
    (x_ref, cot_ref, tails), refs = refs[:3], refs[3:]
    (w_conv_t, w_conv, w_out_t, w_out, vec3), refs = refs[:5], refs[5:]
    if has_before:
        before, refs = refs[:4], refs[4:]
    out_ref, gs, refs = refs[0], refs[1 : 1 + pieces], refs[1 + pieces :]
    sums, table_out, refs = refs[:4], refs[4], refs[5:]
    table, refs = refs[-1], refs[:-1]
    if has_after:
        chunks, refs = refs[0], refs[1:]
    gw_out, gw_conv, g_gain3, g_shift3 = sums
    taps, act, gc, gt, conv, g_act, cots = refs
    width = w_out_t.shape[0]
    inner = w_out.shape[0]
    step = pl.program_id(0)
    length = taps.shape[1] // group
    columns = taps.shape[1] // LANES

    @pl.when(step == 0)
    def _():
        for k, ref in enumerate(sums):
            ref[...] = before[k][...] if has_before else jnp.zeros_like(ref)
        table[...] = jnp.zeros_like(table)
        taps[3 * inner :, :] = jnp.ones_like(taps[3 * inner :, :])
        act[inner:, :] = jnp.ones_like(act[inner:, :])

    reads = []
    for q in range(group):
        m = step * group + q
        base = m * REACH
        here = q * length
        span = slice(here, here + length)
        start_span = slice(here, here + LANES)
        cots[:, span] = cot_ref[q, 0]
        mid = mids[0][q] if pieces == 1 else jnp.concatenate([ref[q] for ref in mids], axis=1)
        lane = lax.broadcasted_iota(jnp.int32, (1, LANES), 1)
        if prompts:
            begin = chosen(base, lane, lane >= 0, batches)
            before_rows = tails[...]
            reads.append((begin,))
        else:
            start = cont_start[m, 0, 1]
            owners = cont_map[m, 0, 0], cont_map[m, 0, 1]
            at_most = (length // LANES - 2) * LANES
            window = jnp.minimum(lax.shift_right_logical(start, 7) * LANES, at_most)
            wide = pl.ds(pl.multiple_of(here + window, LANES), 2 * LANES)
            begin = chosen(base, lane, lane < start, batches)
            before_rows = tails[owners[0]]
        first = dot(before_rows, begin, 1, 0).astype(bf16)
        taps[0:inner, span] = mid
        one, two = shifted_right(mid, STEP), shifted_right(mid, REACH)
        if not prompts:
            row = lax.broadcasted_iota(jnp.int32, (1, length), 1)
            since = jnp.where(row < start, row, row - start)
            near_one = jnp.where(since >= STEP, 1.0, 0.0)
            near_two = jnp.where(since >= REACH, 1.0, 0.0)
            full = lambda w: jnp.broadcast_to(w, (inner, length)).astype(bf16)
            one, two = one * full(near_one), two * full(near_two)
        taps[inner : 2 * inner, span] = one
        taps[2 * inner : 3 * inner, span] = two
        taps[inner : 2 * inner, start_span] += first[:, :LANES]
        taps[2 * inner : 3 * inner, start_span] += first[:, LANES:]
        if not prompts:
            offset = window + lax.broadcasted_iota(jnp.int32, (1, 2 * LANES), 1) - start
            later = chosen(base, offset, offset >= 0, batches)
            far = dot(tails[owners[1]], later, 1, 0).astype(bf16)
            taps[inner : 2 * inner, wide] += far[:, : 2 * LANES]
            taps[2 * inner : 3 * inner, wide] += far[:, 2 * LANES :]
            reads.append((begin, owners, wide, later, near_one, near_two))
    conv[...] = dot(w_conv_t[...], taps[...], 1, 0)
    g_act[...] = dot(w_out[...], cots[...], 1, 0)
    load = lambda t, c: conv[t, at(c)]
    means, scales = stats(load, inner, columns)
    shifts = [a * b for a, b in zip(means, scales)]

    def keep(t, c, u):
        g_act[t, at(c)] = u

    def put_act(t, c, value):
        act[t, at(c)] = value.astype(bf16)

    totals = backward_pass(
        columns,
        inner,
        lambda t, c: load(t, c) * scales[c] - shifts[c],
        lambda t, c: g_act[t, at(c)],
        vec3,
        (g_gain3, g_shift3),
        keep,
        put_act,
    )
    for c in range(columns):
        mean_u, mean_un = totals[c]
        by_x = -(scales[c] * scales[c] * mean_un)
        constant = -(scales[c] * mean_u) - means[c] * by_x
        for t in tiles(inner):
            g_in = g_act[t, at(c)] * scales[c] + (load(t, c) * by_x + constant)
            gc[t, at(c)] = g_in.astype(bf16)
    branch = dot(w_out_t[...], act[...], 1, 0)
    for q in range(group):
        span = slice(q * length, (q + 1) * length)
        out_ref[q, 0] = (x_ref[q, 0].astype(f32) + branch[:, span]).astype(bf16)
    gw_out[...] += dot(cots[...], act[...], 1, 1)
    gw_conv[...] += dot(gc[...], taps[...], 1, 1)
    g_taps = dot(w_conv[...], gc[...], 1, 0)
    for q in range(group):
        span = slice(q * length, (q + 1) * length)
        g0, g1, g2 = (g_taps[k * inner : (k + 1) * inner, span] for k in range(3))
        both = jnp.concatenate([g1[:, :LANES], g2[:, :LANES]], axis=1).astype(bf16)
        back = dot(both, reads[q][0], 1, 1)
        if prompts:
            table[...] += back
        else:
            begin, owners, wide, later, near_one, near_two = reads[q]
            table[owners[0]] += back
            gt[0, :, span] = g1.astype(bf16)
            gt[1, :, span] = g2.astype(bf16)
            both = jnp.concatenate([gt[0, :, wide], gt[1, :, wide]], axis=1)
            table[owners[1]] += dot(both, later, 1, 1)
            g1, g2 = g1 * near_one, g2 * near_two
        g_mid = (g0 + shifted_left(g1, STEP) + shifted_left(g2, REACH)).astype(bf16)
        if pieces == 1:
            gs[0][q] = g_mid
        else:
            gs[0][q] = g_mid[:, : length - LANES]
            gs[1][q] = g_mid[:, length - LANES :]

    @pl.when(step == pl.num_programs(0) - 1)
    def _():
        table_out[...] = table[...].astype(bf16)
        if has_after:
            count, few, _ = chunks.shape
            gw_conv[:, 3 * inner + 1 : 3 * inner + 2] = jnp.sum(g_gain3[...], axis=1, keepdims=True)
            gw_conv[:, 3 * inner + 2 : 3 * inner + 3] = jnp.sum(g_shift3[...], axis=1, keepdims=True)
            twice = width // inner
            for r in range(count):
                parts = [gw_conv[r * few : (r + 1) * few, : 3 * inner + 3]]
                for h in range(r * twice, (r + 1) * twice):
                    parts.append(gw_out[h * few : (h + 1) * few, : inner + 1])
                chunks[r] = jnp.concatenate(parts, axis=1).astype(bf16)


def middle(prompts, group, scalars, mids, x, cot, tails, weights, before=None, chunks=0):
    batches, _, width, length = x.shape
    inner = mids[0].shape[1]
    block = lambda a: blocks(a.shape, a.shape[-1], group, 0)
    args = list(scalars) + mids + [x, cot, tails] + list(weights) + list(before or ())
    in_specs = [pl.BlockSpec(memory_space=pltpu.SMEM)] * len(scalars)
    in_specs += [block(a) for a in mids + [x, cot]]
    in_specs += [WHOLE] * (len(args) - len(in_specs))
    out_like = [shape_of(*x.shape, kind=bf16)]
    out_like += [shape_of(*mid.shape, kind=bf16) for mid in mids]
    sums = [
        shape_of(width, inner + 16),
        shape_of(inner, 3 * inner + 16),
        shape_of(inner, LANES),
        shape_of(inner, LANES),
        shape_of(*tails.shape, kind=bf16),
    ]
    if chunks:
        wide = 3 * inner + 3 + (width // inner) * (inner + 1)
        sums.append(shape_of(chunks, inner // chunks, wide, kind=bf16))
    total = group * length
    scratch = [
        pltpu.VMEM((3 * inner + 16, total), bf16),
        pltpu.VMEM((inner + 16, total), bf16),
        pltpu.VMEM((inner, total), bf16),
        pltpu.VMEM((2, inner, total), bf16),
        pltpu.VMEM((inner, total), f32),
        pltpu.VMEM((inner, total), f32),
        pltpu.VMEM((width, total), bf16),
    ]
    scratch.append(pltpu.VMEM(tails.shape, f32))
    return pl.pallas_call(
        functools.partial(
            middle_kernel, batches, prompts, group, len(mids), before is not None, chunks > 0
        ),
        grid=(batches // group,),
        in_specs=in_specs,
        out_specs=[block(a) for a in out_like] + [WHOLE] * len(sums),
        out_shape=out_like + sums,
        scratch_shapes=scratch,
        compiler_params=PARAMS,
        cost_estimate=cost(batches * length * 9 * inner * width, 3 * x.size * 2),
        name="middle",
    )(*args)


def inner_back_kernel(has_rim, has_before, has_after, *refs):
    (act_ref, g_ref, n2_ref, r2_ref, vec2), refs = refs[:5], refs[5:]
    if has_rim:
        rim, refs = refs[0], refs[1:]
    if has_before:
        before, refs = refs[:3], refs[3:]
    gh_ref, sums, refs = refs[0], refs[1:4], refs[4:]
    if has_after:
        in_chunks, refs = refs[0], refs[1:]
    (kept,) = refs
    gw_in, g_gain2, g_shift2 = sums
    inner = vec2.shape[1]
    step = pl.program_id(0)

    @pl.when(step == 0)
    def _():
        for k, ref in enumerate(sums):
            ref[...] = before[k][...] if has_before else jnp.zeros_like(ref)

    g, n2, r2, gh = (Columns(ref) for ref in (g_ref, n2_ref, r2_ref, gh_ref))

    def g_in(t, c):
        value = g.get(t, c)
        if has_rim:
            piece = rim[t, c * REACH : (c + 1) * REACH]
            value += jnp.concatenate([jnp.zeros((TILE, LANES - REACH), f32), piece], axis=1)
        return value

    def keep(t, c, u):
        kept[t, at(c)] = u

    totals = backward_pass(g.count, inner, n2.get, g_in, vec2, (g_gain2, g_shift2), keep)
    for c in range(g.count):
        mean_u, mean_un = totals[c]
        scale = r2.get(ROW, c)
        by_n, constant = -(scale * mean_un), -(scale * mean_u)
        for t in tiles(inner):
            gh.put(t, c, kept[t, at(c)] * scale + (n2.get(t, c) * by_n + constant))
    for q in range(act_ref.shape[0]):
        gw_in[...] += dot(gh_ref[q], act_ref[q], 1, 1)

    if has_after:

        @pl.when(step == pl.num_programs(0) - 1)
        def _():
            count, few, wide = in_chunks.shape
            gw_in[:, wide - 2 : wide - 1] = jnp.sum(g_gain2[...], axis=1, keepdims=True)
            gw_in[:, wide - 1 : wide] = jnp.sum(g_shift2[...], axis=1, keepdims=True)
            for r in range(count):
                in_chunks[r] = gw_in[r * few : (r + 1) * few, :wide].astype(bf16)


def inner_back(act, g, n2, r2, part, vec2, rim=None, before=None, chunks=0):
    inner = vec2.shape[1]
    batches, width = act.shape[0], act.shape[1] - 16
    lanes, group, first = part
    in_specs = [blocks(act.shape, lanes, group, first)]
    in_specs += [blocks(a.shape, lanes, group, 0) for a in (g, n2, r2)] + [WHOLE]
    args = [act, g, n2, r2, vec2]
    if rim is not None:
        args.append(rim)
        in_specs.append(pl.BlockSpec((inner, GROUP * REACH), lambda i: (0, i)))
    if before is not None:
        args += before
        in_specs += [WHOLE] * 3
    sums = [shape_of(inner, width + 16), shape_of(inner, LANES), shape_of(inner, LANES)]
    if chunks:
        sums.append(shape_of(chunks, inner // chunks, width + 3, kind=bf16))
    return pl.pallas_call(
        functools.partial(inner_back_kernel, rim is not None, before is not None, chunks > 0),
        grid=(batches // group,),
        in_specs=in_specs,
        out_specs=[blocks(g.shape, lanes, group, 0)] + [WHOLE] * len(sums),
        out_shape=[shape_of(*g.shape, kind=bf16)] + sums,
        scratch_shapes=[pltpu.VMEM((inner, group * lanes), f32)],
        compiler_params=PARAMS,
        cost_estimate=cost(4 * width * inner * batches * lanes, 0),
        name="inner_back",
    )(*args)


def outer_back_kernel(pieces, has_before, has_into, has_after, *refs):
    (x_ref, cot_ref, mean_ref, scale_ref), refs = refs[:4], refs[4:]
    ghs, refs = refs[:pieces], refs[pieces:]
    (w_in, vec1), refs = refs[:2], refs[2:]
    if has_before:
        before, refs = refs[:2], refs[2:]
    if has_into:
        refs = refs[1:]
    out_ref, sums, refs = refs[0], refs[1:3], refs[3:]
    if has_after:
        small, refs = refs[0], refs[1:]
    (g_act,) = refs
    width = w_in.shape[0]
    step = pl.program_id(0)

    @pl.when(step == 0)
    def _():
        for k, ref in enumerate(sums):
            ref[...] = before[k][...] if has_before else jnp.zeros_like(ref)

    first = 0
    for gh in ghs:
        length = gh.shape[-1]
        g_act[:, first : first + length] = dot(w_in[...], gh[0], 1, 0)
        first += length
    x, cot, mean, scale, out = (Columns(r) for r in (x_ref, cot_ref, mean_ref, scale_ref, out_ref))
    scales = [scale.get(ROW, c) for c in range(x.count)]
    means = [mean.get(ROW, c) for c in range(x.count)]
    shifts = [a * b for a, b in zip(means, scales)]

    def keep(t, c, u):
        g_act[t, at(c)] = u

    totals = backward_pass(
        x.count,
        width,
        lambda t, c: x.get(t, c) * scales[c] - shifts[c],
        lambda t, c: g_act[t, at(c)],
        vec1,
        sums,
        keep,
    )
    for c in range(x.count):
        mean_u, mean_un = totals[c]
        by_x = -(scales[c] * scales[c] * mean_un)
        constant = -(scales[c] * mean_u) - means[c] * by_x
        for t in tiles(width):
            change = g_act[t, at(c)] * scales[c] + (x.get(t, c) * by_x + constant)
            out.put(t, c, cot.get(t, c) + change)

    if has_after:

        @pl.when(step == pl.num_programs(0) - 1)
        def _():
            for k in range(2):
                small[:, k * width : (k + 1) * width] = down(sums[k][...].T)


def outer_back(
    x, cot, mean, scale, ghs, w_in, vec1, batches, before=None, into=None, last=False
):
    first, count = batches
    width, lanes = x.shape[2:]
    block = lambda a: blocks(a.shape, a.shape[-1], 1, 0, first)
    args = [x, cot, mean, scale] + ghs
    in_specs = [block(a) for a in args] + [WHOLE] * 2
    args += [w_in, vec1]
    if before is not None:
        args += before
        in_specs += [WHOLE] * 2
    aliases = {}
    if into is not None:
        aliases = {len(args): 0}
        args.append(into)
        in_specs.append(pl.BlockSpec(memory_space=pl.ANY))
    sums = [shape_of(width, LANES), shape_of(width, LANES)]
    if last:
        sums.append(shape_of(1, 2 * width))
    return pl.pallas_call(
        functools.partial(
            outer_back_kernel, len(ghs), before is not None, into is not None, last
        ),
        grid=(count,),
        in_specs=in_specs,
        out_specs=[block(x)] + [WHOLE] * len(sums),
        out_shape=[shape_of(*x.shape)] + sums,
        scratch_shapes=[pltpu.VMEM((width, lanes), f32)],
        input_output_aliases=aliases,
        compiler_params=PARAMS,
        cost_estimate=cost(8 * w_in.size * count * lanes, 0),
        name="outer_back",
    )(*args)


def packing_kernel(inner, ids, early_ref, late_ref, *refs):
    pieces, packed = refs[:-1], refs[-1]
    total = lambda ref: jnp.sum(ref[...].astype(f32), axis=0)
    early, late = total(early_ref), total(late_ref)
    shards = len(pieces)
    width = late.shape[1] - 3
    own, wide = inner // shards, width // shards
    conv_end = 3 * inner + 3
    firsts = range(conv_end, early.shape[1], inner + 1)
    kept = [early[:, first + inner : first + inner + 1] for first in firsts]
    kept += [early[:, 3 * inner : conv_end], late[:, width:]]
    starts = list(firsts) + [k * inner for k in range(3)]
    for j in range(shards):
        parts = [early[:, first + j * own : first + (j + 1) * own] for first in starts]
        parts += [late[:, j * wide : (j + 1) * wide]]
        packed[ids[0] ^ j] = jnp.concatenate(parts + kept, axis=1)
    for k in range(shards):
        pieces[k][...] = packed[k].astype(pieces[k].dtype)


def packing(ids, shards, inner, early, late):
    few, width = early.shape[1], late.shape[2] - 3
    wide = (2 * width + 3 * inner) // shards + width // inner + 6
    kinds = [f32] + [bf16] * (shards - 1)
    return pl.pallas_call(
        functools.partial(packing_kernel, inner),
        in_specs=[pl.BlockSpec(memory_space=pltpu.SMEM)] + [WHOLE] * 2,
        out_specs=[WHOLE] * shards,
        out_shape=[shape_of(few, wide, kind=kind) for kind in kinds],
        scratch_shapes=[pltpu.VMEM((shards, few, wide), f32)],
        compiler_params=PARAMS,
        name="packing",
    )(ids, early, late)


def unpacking_kernel(whole, by_out, by_conv, by_in, by_width, by_inner, tall, tall_in):
    reps, few, _ = whole.shape
    own, width = by_out.shape
    inner = by_conv.shape[1]
    wide = by_in.shape[0]
    twice = width // inner
    first_in = (twice + 3) * own
    small = first_in + wide
    for r in range(reps):
        piece = whole[r].astype(f32)
        for h in range(twice):
            rows = slice((r * twice + h) * few, (r * twice + h + 1) * few)
            tall[rows, :own] = piece[:, h * own : (h + 1) * own]
            tall[rows, own : own + 1] = piece[:, small + h : small + h + 1]
        rows = slice(r * few, (r + 1) * few)
        for k in range(3):
            by_conv[k, rows, :] = piece[:, (twice + k) * own : (twice + k + 1) * own]
        tall_in[rows, :wide] = piece[:, first_in : first_in + wide]
        tall_in[rows, wide : wide + 6] = piece[:, small + twice : small + twice + 6]
    turned = tall[...].T
    by_out[...] = turned[:own]
    by_width[...] = turned[own : own + 1]
    turned = tall_in[...].T
    by_in[...] = turned[:wide]
    by_inner[...] = turned[wide : wide + 6]


def unpacking(whole, shards, inner, width):
    own, wide = inner // shards, width // shards
    up = lambda n: -(-n // LANES) * LANES
    return pl.pallas_call(
        unpacking_kernel,
        in_specs=[WHOLE],
        out_specs=[WHOLE] * 5,
        out_shape=[
            shape_of(own, width),
            shape_of(3, inner, own),
            shape_of(wide, inner),
            shape_of(1, width),
            shape_of(6, inner),
        ],
        scratch_shapes=[
            pltpu.VMEM((width, up(own + 1)), f32),
            pltpu.VMEM((inner, up(wide + 6)), f32),
        ],
        compiler_params=PARAMS,
        name="unpacking",
    )(whole)


def passed_along(x, axis, by):
    size = lax.axis_size(axis)
    pairs = [(i, i + by) for i in range(size) if 0 <= i + by < size]
    return lax.ppermute(x, axis, pairs)


def swapped(x, axis, k):
    return lax.ppermute(x, axis, [(i, i ^ k) for i in range(lax.axis_size(axis))])


def gathered(x):
    size = lax.axis_size("shard")
    return jnp.stack([x] + [swapped(x, "shard", k) for k in range(1, size)])


def after(value, *others):
    return lax.optimization_barrier((value,) + others)[0]


def sent_from_last(x, axis):
    size = lax.axis_size(axis)
    me = lax.axis_index(axis)
    value = x
    for j in range(size - 1):
        piece = lax.ppermute(x, axis, [(size - 1, j)])
        value = jnp.where(me == j, piece, value)
    return value


def summed_at_last(x, axis):
    size = lax.axis_size(axis)
    total = x.astype(f32)
    for j in range(size - 1):
        total = total + lax.ppermute(x, axis, [(j, size - 1)]).astype(f32)
    return total


def dealt(x, axis):
    return lax.all_to_all(x, axis, 0, 0, tiled=True)


def summed_everywhere(x):
    x = jnp.sum(lax.optimization_barrier(lax.all_gather(x, "rep")), axis=0)
    size = lax.axis_size("shard")
    if size > 4:
        return lax.psum(x, "shard")
    return x + sum(swapped(x, "shard", k) for k in range(1, size))


def on_device(
    prompt_x,
    cont_x,
    cont_map,
    cont_start,
    w_in,
    w_conv,
    w_out,
    norm1_gain,
    norm1_bias,
    bias_in,
    norm2_gain,
    norm2_bias,
    bias_conv,
    norm3_gain,
    norm3_bias,
    bias_out,
    prompt_cot,
    cont_cot,
):
    inner = w_conv.shape[2]
    turned = lambda a: jnp.swapaxes(a, 2, 3)
    prompt_x, cont_x, prompt_cot, cont_cot = map(turned, (prompt_x, cont_x, prompt_cot, cont_cot))
    width = prompt_x.shape[2]
    shards, reps = lax.axis_size("shard"), lax.axis_size("rep")
    is_last = lax.axis_index("shard") == shards - 1
    own = w_out.shape[0]
    parts = splits(own)
    ids = jnp.stack([lax.axis_index("shard"), lax.axis_index("rep") % 2]).astype(jnp.int32)
    rows = (norm1_gain, norm1_bias, norm2_gain, norm2_bias, norm3_gain, norm3_bias)
    in_part, rest_part, vec1, vec2, vec3 = sending(ids, w_in, w_conv, w_out, rows)
    rows_p, rows_c = prompt_x.shape[3], cont_x.shape[3]
    last = (LANES, GROUP, rows_p - LANES)
    rest = (rows_p - LANES, 1, 0)
    every = (rows_c, 1, 0)
    have_first = rows_p > LANES
    act_p, mean_p, scale_p, act_c, mean_c, scale_c = lead([prompt_x, cont_x], vec1)
    in_pieces, rest_part, act_p = lax.optimization_barrier((gathered(in_part), rest_part, act_p))
    half_in, w_in_t = taking_in(ids, in_pieces, bias_in)
    rest_pieces = gathered(rest_part)
    mid_l, n2_l, r2_l, rim = front([act_p], [last], w_in_t, vec2, with_rim=True)
    halo = passed_along(rim, "shard", 1)
    own_tail = sent_from_last(rim, "shard")
    mids = [mid_l]
    if have_first:
        mid_f, n2_f, r2_f = front([act_p], [rest], w_in_t, vec2)
        mids = [mid_f, mid_l]
    rest_pieces, act_c, _ = lax.optimization_barrier((rest_pieces, act_c, mids[0]))
    if parts == 2:
        rest_pieces = jnp.stack([rest_pieces, swapped(rest_pieces, "rep", 1)])
    else:
        rest_pieces = rest_pieces[None]
    mid_c, n2_c, r2_c = front([act_c], [every], w_in_t, vec2)
    rest_pieces, own_tail, mid_c = lax.optimization_barrier((rest_pieces, own_tail, mid_c))
    tails = lax.all_gather(own_tail, "rep", axis=0)

    weights = (*taking_rest(ids, rest_pieces, bias_conv, bias_out), vec3)
    prompt_out, *results = middle(True, 1, [], mids, prompt_x, prompt_cot, halo, weights)
    g_ps, results = results[: len(mids)], results[len(mids) :]
    sums, rim_out = results[:4], results[4]
    back_rim = passed_along(rim_out, "shard", -1)
    cont_out, g_c, *results = middle(
        False,
        1,
        [cont_start, cont_map],
        [mid_c],
        cont_x,
        cont_cot,
        tails,
        weights,
        before=sums,
        chunks=reps,
    )
    table, early = results[4:]
    table = dealt(table, "rep")

    sums = None
    gh_ps = []
    if have_first:
        gh_f, *sums = inner_back(act_p, g_ps[0], n2_f, r2_f, rest, vec2)
        gh_ps.append(gh_f)
    gh_c, *sums = inner_back(act_c, g_c, n2_c, r2_c, every, vec2, before=sums)
    table, gh_c = lax.optimization_barrier((table, gh_c))
    own_tail = jnp.sum(table.astype(f32), axis=0).astype(bf16)
    own_tail, early = lax.optimization_barrier((own_tail, early))
    own_tail = summed_at_last(own_tail, "shard")
    early = dealt(early, "rep")
    batches = prompt_x.shape[0]
    one, two = (0, batches // 2), (batches // 2, batches // 2)
    outer_c = functools.partial(
        outer_back, cont_x, cont_cot, mean_c, scale_c, [gh_c], half_in, vec1
    )
    cont_grad, *sums1 = outer_c(one)
    cont_grad, own_tail = lax.optimization_barrier((cont_grad, own_tail))
    rim_in = back_rim.astype(f32) + jnp.where(is_last, own_tail, 0.0)
    gh_l, *results = inner_back(
        act_p, g_ps[-1], n2_l, r2_l, last, vec2, rim=rim_in, before=sums, chunks=reps
    )
    late, early, gh_l = lax.optimization_barrier((results[3], early, gh_l))
    late = dealt(late, "rep")
    gh_ps.append(gh_l)
    cont_grad, *sums1 = outer_c(two, before=sums1, into=after(cont_grad, gh_l))
    late, cont_grad = lax.optimization_barrier((late, cont_grad))

    mine, *others = packing(ids, shards, inner, early, late)
    others = [swapped(other, "shard", k + 1) for k, other in enumerate(others)]
    outer_p = functools.partial(
        outer_back, prompt_x, prompt_cot, mean_p, scale_p, gh_ps, half_in, vec1
    )
    prompt_grad, *sums1 = outer_p(one, before=[after(sums1[0], mine), sums1[1]])
    *others, prompt_grad = lax.optimization_barrier((*others, prompt_grad))
    mine = mine + sum(other.astype(f32) for other in others)
    whole = lax.all_gather(mine, "rep")
    prompt_grad, *results = outer_p(two, before=sums1, into=after(prompt_grad, mine), last=True)
    ones = summed_everywhere(results[2])[0]
    whole = after(whole, ones)
    grad_w_out, grad_w_conv, grad_w_in, grad_bias_out, small = unpacking(whole, shards, inner, width)
    grad_bias_conv, grad_gain3, grad_shift3, grad_bias_in, grad_gain2, grad_shift2 = small
    return (
        turned(prompt_out),
        turned(cont_out),
        turned(prompt_grad),
        turned(cont_grad),
        grad_w_in,
        jnp.swapaxes(grad_w_conv, 1, 2),
        grad_w_out,
        ones[:width],
        ones[width:],
        grad_bias_in,
        grad_gain2,
        grad_shift2,
        grad_bias_conv,
        grad_gain3,
        grad_shift3,
        grad_bias_out[0],
    )


def solution(mesh):
    rows = P(None, "rep", "shard", None)
    buffers = P(None, ("rep", "shard"), None, None)
    in_specs = (
        rows,
        buffers,
        P(None, ("rep", "shard"), None),
        P(None, ("rep", "shard"), None),
        P("shard", None),
        P(None, "shard", None),
        P("shard", None),
    ) + (P(),) * 9 + (rows, buffers)
    out_specs = (
        rows,
        buffers,
        rows,
        buffers,
        P("shard", None),
        P(None, "shard", None),
        P("shard", None),
    ) + (P(),) * 9
    return jax.shard_map(
        on_device, mesh=mesh, in_specs=in_specs, out_specs=out_specs, check_vma=False
    )
```

```python
import functools

import jax
import jax.numpy as jnp
from jax import lax
from jax.experimental import pallas as pl
from jax.experimental.pallas import tpu as pltpu
from jax.sharding import PartitionSpec as P

STEP = 16
REACH = 2 * STEP
LANES = 128
GROUP = 4
TILE = 16
epsilon = 1e-05
bf16 = jnp.bfloat16
f32 = jnp.float32
VMEM_BYTES = 58 * 2**20
WHOLE = pl.BlockSpec(memory_space=pltpu.VMEM)
PARAMS = pltpu.CompilerParams(vmem_limit_bytes=VMEM_BYTES)


def cost(flops, moved):
    return pl.CostEstimate(flops=int(2.5 * flops), bytes_accessed=int(moved), transcendentals=0)


def dot(a, b, ca, cb):
    return lax.dot_general(a, b, (((ca,), (cb,)), ((), ())), preferred_element_type=f32)


def at(column):
    return slice(column * LANES, (column + 1) * LANES)


def tiles(depth):
    return [slice(r, r + TILE) for r in range(0, depth, TILE)]


class Columns:
    def __init__(self, ref):
        self.ref = ref
        self.per = ref.shape[-1] // LANES
        self.count = ref.shape[0] * self.per

    def key(self, rows, c):
        return (c // self.per,) + (0,) * (len(self.ref.shape) - 3) + (rows, at(c % self.per))

    def get(self, rows, c):
        return self.ref[self.key(rows, c)].astype(f32)

    def put(self, rows, c, values):
        self.ref[self.key(rows, c)] = values.astype(self.ref.dtype)


ROW = slice(0, 1)


def down(values):
    return jnp.sum(values, axis=0, keepdims=True)


def stats(load, depth, columns):
    zero = jnp.zeros((TILE, LANES), f32)
    sums = [zero] * columns
    for t in tiles(depth):
        sums = [s + load(t, c) for c, s in enumerate(sums)]
    means = [down(s) * (1.0 / depth) for s in sums]
    sums = [zero] * columns
    for t in tiles(depth):
        for c in range(columns):
            center = load(t, c) - means[c]
            sums[c] = sums[c] + center * center
    scales = [lax.rsqrt(down(s) * (1.0 / depth) + epsilon) for s in sums]
    return means, scales


def halved(vec):
    return 0.5 * vec


def backward_pass(columns, depth, normed, g_in, vec, sums, keep, act=None):
    g_gain, g_shift = sums
    zero = jnp.zeros((TILE, LANES), f32)
    totals = [[zero, zero] for _ in range(columns)]
    for t in tiles(depth):
        gain, shift = vec[0, t, :], vec[1, t, :]
        half_gain, half_shift = halved(gain), halved(shift)
        gains = shifts = None
        for c in range(columns):
            n = normed(t, c)
            half = n * half_gain + half_shift
            tan = jnp.tanh(half)
            if act is not None:
                act(t, c, half * tan + half)
            slope = (1.0 + tan) * (1.0 + half * (1.0 - tan))
            g = g_in(t, c) * slope
            gn = g * n
            u = g * gain
            keep(t, c, u)
            totals[c][0] = totals[c][0] + u
            totals[c][1] = totals[c][1] + gn * gain
            gains = gn if gains is None else gains + gn
            shifts = g if shifts is None else shifts + g
        g_gain[t, :] += gains
        g_shift[t, :] += shifts
    return [[down(s) * (1.0 / depth) for s in pair] for pair in totals]


def blocks(shape, lanes, group, first, batch=0):
    full = (group,) + tuple(shape[1:-1]) + (lanes,)
    zeros = (0,) * (len(shape) - 2)
    return pl.BlockSpec(full, lambda i: (i + batch // group,) + zeros + (first // lanes,))


def shape_of(*shape, kind=f32):
    return jax.ShapeDtypeStruct(shape, kind)


def splits(own):
    return 2 if own % 2 == 0 else 1


def sending_kernel(ids, w_in, w_conv_t, w_out, *refs):
    rows, (in_part, rest_part), vecs = refs[:6], refs[6:8], refs[8:]
    own, width = w_out.shape
    inner = w_conv_t.shape[1]
    parts = splits(own)
    few = own // parts
    in_part[...] = w_in[...].astype(bf16)
    conv = [w_conv_t[k].T for k in range(3)]
    for h in range(parts):

        @pl.when(ids[1] % parts == h)
        def _():
            mine = slice(h * few, (h + 1) * few)
            pieces = [turn[mine] for turn in conv]
            pieces += [w_out[mine, q : q + inner] for q in range(0, width, inner)]
            rest_part[...] = jnp.concatenate(pieces, axis=0).astype(bf16)

    for k, row in enumerate(rows):
        wide = jnp.broadcast_to(row[...][None], (LANES, row.shape[0]))
        vecs[k // 2][k % 2] = wide.T


def sending(ids, w_in, w_conv, w_out, rows):
    own, width = w_out.shape
    inner = w_conv.shape[2]
    parts = splits(own)
    return pl.pallas_call(
        sending_kernel,
        in_specs=[pl.BlockSpec(memory_space=pltpu.SMEM)] + [WHOLE] * 9,
        out_specs=[WHOLE] * 5,
        out_shape=[
            shape_of(*w_in.shape, kind=bf16),
            shape_of((3 + width // inner) * own // parts, inner, kind=bf16),
            shape_of(2, width, LANES),
            shape_of(2, inner, LANES),
            shape_of(2, inner, LANES),
        ],
        compiler_params=PARAMS,
        name="sending",
    )(ids, w_in, jnp.swapaxes(w_conv, 1, 2), w_out, *rows)


def with_shift(weights, shift):
    parts = []
    left = shift
    for _ in range(3):
        part = left.astype(bf16).astype(f32)
        parts.append(part)
        left = left - part
    parts.append(jnp.zeros((13, shift.shape[1]), f32))
    return jnp.concatenate([weights.T, jnp.concatenate(parts, axis=0).T], axis=1).astype(bf16)


def taking_in_kernel(ids, pieces, bias, half_in, w_in_t, total):
    shards, some, _ = pieces.shape
    for j in range(shards):
        total[j * some : (j + 1) * some, :] = pieces[ids[0] ^ j].astype(f32)
    half_in[...] = (0.5 * total[...]).astype(bf16)
    w_in_t[...] = with_shift(total[...], bias[...])


def taking_in(ids, pieces, bias):
    shards, some, inner = pieces.shape
    width = shards * some
    return pl.pallas_call(
        taking_in_kernel,
        in_specs=[pl.BlockSpec(memory_space=pltpu.SMEM)] + [WHOLE] * 2,
        out_specs=[WHOLE] * 2,
        out_shape=[shape_of(width, inner, kind=bf16), shape_of(inner, width + 16, kind=bf16)],
        scratch_shapes=[pltpu.VMEM((width, inner), f32)],
        compiler_params=PARAMS,
        name="taking_in",
    )(ids, pieces, bias[None])


def taking_rest_kernel(ids, pieces, bias_conv, bias_out, *refs):
    (w_conv_t, half_conv, w_out_t, half_out), (conv, out) = refs[:4], refs[4:]
    parts, shards, rows, inner = pieces.shape
    width = out.shape[1]
    few = rows // (3 + width // inner)
    for j in range(shards):
        for h in range(parts):
            first = (j * parts + h) * few
            piece = pieces[h ^ (ids[1] % parts), ids[0] ^ j].astype(f32)
            for k in range(3):
                conv[k * inner + first : k * inner + first + few, :] = piece[k * few : (k + 1) * few]
            halves = [piece[k * few : (k + 1) * few] for k in range(3, 3 + width // inner)]
            out[first : first + few, :] = jnp.concatenate(halves, axis=1)
    half_conv[...] = (0.5 * conv[...]).astype(bf16)
    w_conv_t[...] = with_shift(conv[...], bias_conv[...])
    half_out[...] = (0.5 * out[...]).astype(bf16)
    w_out_t[...] = with_shift(out[...], bias_out[...])


def taking_rest(ids, pieces, bias_conv, bias_out):
    inner, width = bias_conv.shape[0], bias_out.shape[0]
    return pl.pallas_call(
        taking_rest_kernel,
        in_specs=[pl.BlockSpec(memory_space=pltpu.SMEM)] + [WHOLE] * 3,
        out_specs=[WHOLE] * 4,
        out_shape=[
            shape_of(inner, 3 * inner + 16, kind=bf16),
            shape_of(3 * inner, inner, kind=bf16),
            shape_of(width, inner + 16, kind=bf16),
            shape_of(inner, width, kind=bf16),
        ],
        scratch_shapes=[pltpu.VMEM((3 * inner, inner), f32), pltpu.VMEM((inner, width), f32)],
        compiler_params=PARAMS,
        name="taking_rest",
    )(ids, pieces, bias_conv[None], bias_out[None])


def lead_kernel(*refs):
    x_refs, vec1, outs = refs[:2], refs[2], refs[3:]
    for s in range(2):
        x, act, mean, scale = (Columns(ref) for ref in (x_refs[s],) + tuple(outs[3 * s : 3 * s + 3]))
        depth = x_refs[s].shape[-2]
        means, scales = stats(x.get, depth, x.count)
        for c in range(x.count):
            mean.put(ROW, c, means[c])
            scale.put(ROW, c, scales[c])
        shifts = [m * v for m, v in zip(means, scales)]
        for t in tiles(depth):
            gain, shift = halved(vec1[0, t, :]), halved(vec1[1, t, :])
            for c in range(x.count):
                half = (x.get(t, c) * scales[c] - shifts[c]) * gain + shift
                act.put(t, c, half * jnp.tanh(half) + half)
        for c in range(x.count):
            act.put(slice(depth, depth + 16), c, jnp.ones((16, LANES), f32))


def lead(xs, vec1):
    batches, _, width, _ = xs[0].shape
    in_specs, out_specs, out_shape = [], [], []
    for x in xs:
        lanes = x.shape[3]
        in_specs.append(blocks(x.shape, lanes, 1, 0))
        for depth, kind in ((width + 16, bf16), (1, f32), (1, f32)):
            out_specs.append(blocks((batches, depth, lanes), lanes, 1, 0))
            out_shape.append(shape_of(batches, depth, lanes, kind=kind))
    return pl.pallas_call(
        lead_kernel,
        grid=(batches,),
        in_specs=in_specs + [WHOLE],
        out_specs=out_specs,
        out_shape=out_shape,
        compiler_params=PARAMS,
        cost_estimate=cost(0, sum(x.size for x in xs) * 4),
        name="lead",
    )(*xs, vec1)


def front_kernel(streams, with_rim, *refs):
    acts, refs = refs[:streams], refs[streams:]
    (w_in_t, vec2), refs = refs[:2], refs[2:]
    outs, refs = [refs[3 * s : 3 * s + 3] for s in range(streams)], refs[3 * streams :]
    rim_ref = refs[0] if with_rim else None
    hiddens = refs[-streams:]
    inner = w_in_t.shape[0]
    for s in range(streams):
        act, hidden = acts[s], hiddens[s]
        mid, n2, r2 = (Columns(ref) for ref in outs[s])
        wide = act.shape[2]
        for q in range(act.shape[0]):
            hidden[:, q * wide : (q + 1) * wide] = dot(w_in_t[...], act[q], 1, 0)
        load = lambda t, c: hidden[t, at(c)]
        means, scales = stats(load, inner, mid.count)
        shifts = [m * v for m, v in zip(means, scales)]
        for c in range(mid.count):
            r2.put(ROW, c, scales[c])
        for t in tiles(inner):
            gain, shift = halved(vec2[0, t, :]), halved(vec2[1, t, :])
            rim = []
            for c in range(mid.count):
                n = load(t, c) * scales[c] - shifts[c]
                half = n * gain + shift
                value = half * jnp.tanh(half) + half
                mid.put(t, c, value)
                n2.put(t, c, n)
                rim.append(value[:, LANES - REACH :])
            if with_rim:
                rim_ref[t, :] = jnp.concatenate(rim, axis=1).astype(bf16)


def front(acts, parts, w_in_t, vec2, with_rim=False):
    inner = w_in_t.shape[0]
    batches = acts[0].shape[0]
    in_specs, out_specs, out_shape, scratch = [], [], [], []
    for act, (lanes, group, first) in zip(acts, parts):
        in_specs.append(blocks(act.shape, lanes, group, first))
        for depth, kind in ((inner, bf16), (inner, bf16), (1, f32)):
            out_specs.append(blocks((batches, depth, lanes), lanes, group, 0))
            out_shape.append(shape_of(batches, depth, lanes, kind=kind))
        scratch.append(pltpu.VMEM((inner, group * lanes), f32))
    if with_rim:
        out_specs.append(pl.BlockSpec((inner, GROUP * REACH), lambda i: (0, i)))
        out_shape.append(shape_of(inner, batches * REACH, kind=bf16))
    return pl.pallas_call(
        functools.partial(front_kernel, len(acts), with_rim),
        grid=(batches // parts[0][1],),
        in_specs=in_specs + [WHOLE] * 2,
        out_specs=out_specs,
        out_shape=out_shape,
        scratch_shapes=scratch,
        compiler_params=PARAMS,
        cost_estimate=cost(4 * w_in_t.size * sum(batches * part[0] for part in parts), 0),
        name="front",
    )(*acts, w_in_t, vec2)


def shifted_right(values, by):
    zeros = jnp.zeros((values.shape[0], by), values.dtype)
    return jnp.concatenate([zeros, values[:, : values.shape[1] - by]], axis=1)


def shifted_left(values, by):
    zeros = jnp.zeros((values.shape[0], by), values.dtype)
    return jnp.concatenate([values[:, by:], zeros], axis=1)


def chosen(base, position, fits, batches):
    one = jnp.where(jnp.logical_and(fits, position < STEP), base + STEP + position, -1)
    two = jnp.where(jnp.logical_and(fits, position < REACH), base + position, -1)
    target = jnp.concatenate([one, two], axis=1)
    row = lax.broadcasted_iota(jnp.int32, (batches * REACH, target.shape[1]), 0)
    return jnp.where(row == target, 1.0, 0.0).astype(bf16)


def middle_kernel(batches, prompts, group, pieces, has_before, has_after, *refs):
    if not prompts:
        (cont_start, cont_map), refs = refs[:2], refs[2:]
    mids, refs = refs[:pieces], refs[pieces:]
    (x_ref, cot_ref, tails), refs = refs[:3], refs[3:]
    (w_conv_t, w_conv, w_out_t, w_out, vec3), refs = refs[:5], refs[5:]
    if has_before:
        before, refs = refs[:4], refs[4:]
    out_ref, gs, refs = refs[0], refs[1 : 1 + pieces], refs[1 + pieces :]
    sums, table_out, refs = refs[:4], refs[4], refs[5:]
    table, refs = refs[-1], refs[:-1]
    if has_after:
        chunks, refs = refs[0], refs[1:]
    gw_out, gw_conv, g_gain3, g_shift3 = sums
    taps, act, gc, gt, conv, g_act, cots = refs
    width = w_out_t.shape[0]
    inner = w_out.shape[0]
    step = pl.program_id(0)
    length = taps.shape[1] // group
    columns = taps.shape[1] // LANES

    @pl.when(step == 0)
    def _():
        for k, ref in enumerate(sums):
            ref[...] = before[k][...] if has_before else jnp.zeros_like(ref)
        table[...] = jnp.zeros_like(table)
        taps[3 * inner :, :] = jnp.ones_like(taps[3 * inner :, :])
        act[inner:, :] = jnp.ones_like(act[inner:, :])

    reads = []
    for q in range(group):
        m = step * group + q
        base = m * REACH
        here = q * length
        span = slice(here, here + length)
        start_span = slice(here, here + LANES)
        cots[:, span] = cot_ref[q, 0]
        mid = mids[0][q] if pieces == 1 else jnp.concatenate([ref[q] for ref in mids], axis=1)
        lane = lax.broadcasted_iota(jnp.int32, (1, LANES), 1)
        if prompts:
            begin = chosen(base, lane, lane >= 0, batches)
            before_rows = tails[...]
            reads.append((begin,))
        else:
            start = cont_start[m, 0, 1]
            owners = cont_map[m, 0, 0], cont_map[m, 0, 1]
            at_most = (length // LANES - 2) * LANES
            window = jnp.minimum(lax.shift_right_logical(start, 7) * LANES, at_most)
            wide = pl.ds(pl.multiple_of(here + window, LANES), 2 * LANES)
            begin = chosen(base, lane, lane < start, batches)
            before_rows = tails[owners[0]]
        first = dot(before_rows, begin, 1, 0).astype(bf16)
        taps[0:inner, span] = mid
        one, two = shifted_right(mid, STEP), shifted_right(mid, REACH)
        if not prompts:
            row = lax.broadcasted_iota(jnp.int32, (1, length), 1)
            since = jnp.where(row < start, row, row - start)
            near_one = jnp.where(since >= STEP, 1.0, 0.0)
            near_two = jnp.where(since >= REACH, 1.0, 0.0)
            full = lambda w: jnp.broadcast_to(w, (inner, length)).astype(bf16)
            one, two = one * full(near_one), two * full(near_two)
        taps[inner : 2 * inner, span] = one
        taps[2 * inner : 3 * inner, span] = two
        taps[inner : 2 * inner, start_span] += first[:, :LANES]
        taps[2 * inner : 3 * inner, start_span] += first[:, LANES:]
        if not prompts:
            offset = window + lax.broadcasted_iota(jnp.int32, (1, 2 * LANES), 1) - start
            later = chosen(base, offset, offset >= 0, batches)
            far = dot(tails[owners[1]], later, 1, 0).astype(bf16)
            taps[inner : 2 * inner, wide] += far[:, : 2 * LANES]
            taps[2 * inner : 3 * inner, wide] += far[:, 2 * LANES :]
            reads.append((begin, owners, wide, later, near_one, near_two))
    conv[...] = dot(w_conv_t[...], taps[...], 1, 0)
    g_act[...] = dot(w_out[...], cots[...], 1, 0)
    load = lambda t, c: conv[t, at(c)]
    means, scales = stats(load, inner, columns)
    shifts = [a * b for a, b in zip(means, scales)]

    def keep(t, c, u):
        g_act[t, at(c)] = u

    def put_act(t, c, value):
        act[t, at(c)] = value.astype(bf16)

    totals = backward_pass(
        columns,
        inner,
        lambda t, c: load(t, c) * scales[c] - shifts[c],
        lambda t, c: g_act[t, at(c)],
        vec3,
        (g_gain3, g_shift3),
        keep,
        put_act,
    )
    for c in range(columns):
        mean_u, mean_un = totals[c]
        by_x = -(scales[c] * scales[c] * mean_un)
        constant = -(scales[c] * mean_u) - means[c] * by_x
        for t in tiles(inner):
            g_in = g_act[t, at(c)] * scales[c] + (load(t, c) * by_x + constant)
            gc[t, at(c)] = g_in.astype(bf16)
    branch = dot(w_out_t[...], act[...], 1, 0)
    for q in range(group):
        span = slice(q * length, (q + 1) * length)
        out_ref[q, 0] = (x_ref[q, 0].astype(f32) + branch[:, span]).astype(bf16)
    gw_out[...] += dot(cots[...], act[...], 1, 1)
    gw_conv[...] += dot(gc[...], taps[...], 1, 1)
    g_taps = dot(w_conv[...], gc[...], 1, 0)
    for q in range(group):
        span = slice(q * length, (q + 1) * length)
        g0, g1, g2 = (g_taps[k * inner : (k + 1) * inner, span] for k in range(3))
        both = jnp.concatenate([g1[:, :LANES], g2[:, :LANES]], axis=1).astype(bf16)
        back = dot(both, reads[q][0], 1, 1)
        if prompts:
            table[...] += back
        else:
            begin, owners, wide, later, near_one, near_two = reads[q]
            table[owners[0]] += back
            gt[0, :, span] = g1.astype(bf16)
            gt[1, :, span] = g2.astype(bf16)
            both = jnp.concatenate([gt[0, :, wide], gt[1, :, wide]], axis=1)
            table[owners[1]] += dot(both, later, 1, 1)
            g1, g2 = g1 * near_one, g2 * near_two
        g_mid = (g0 + shifted_left(g1, STEP) + shifted_left(g2, REACH)).astype(bf16)
        if pieces == 1:
            gs[0][q] = g_mid
        else:
            gs[0][q] = g_mid[:, : length - LANES]
            gs[1][q] = g_mid[:, length - LANES :]

    @pl.when(step == pl.num_programs(0) - 1)
    def _():
        table_out[...] = table[...].astype(bf16)
        if has_after:
            count, few, _ = chunks.shape
            gw_conv[:, 3 * inner + 1 : 3 * inner + 2] = jnp.sum(g_gain3[...], axis=1, keepdims=True)
            gw_conv[:, 3 * inner + 2 : 3 * inner + 3] = jnp.sum(g_shift3[...], axis=1, keepdims=True)
            twice = width // inner
            for r in range(count):
                parts = [gw_conv[r * few : (r + 1) * few, : 3 * inner + 3]]
                for h in range(r * twice, (r + 1) * twice):
                    parts.append(gw_out[h * few : (h + 1) * few, : inner + 1])
                chunks[r] = jnp.concatenate(parts, axis=1).astype(bf16)


def middle(prompts, group, scalars, mids, x, cot, tails, weights, before=None, chunks=0):
    batches, _, width, length = x.shape
    inner = mids[0].shape[1]
    block = lambda a: blocks(a.shape, a.shape[-1], group, 0)
    args = list(scalars) + mids + [x, cot, tails] + list(weights) + list(before or ())
    in_specs = [pl.BlockSpec(memory_space=pltpu.SMEM)] * len(scalars)
    in_specs += [block(a) for a in mids + [x, cot]]
    in_specs += [WHOLE] * (len(args) - len(in_specs))
    out_like = [shape_of(*x.shape, kind=bf16)]
    out_like += [shape_of(*mid.shape, kind=bf16) for mid in mids]
    sums = [
        shape_of(width, inner + 16),
        shape_of(inner, 3 * inner + 16),
        shape_of(inner, LANES),
        shape_of(inner, LANES),
        shape_of(*tails.shape, kind=bf16),
    ]
    if chunks:
        wide = 3 * inner + 3 + (width // inner) * (inner + 1)
        sums.append(shape_of(chunks, inner // chunks, wide, kind=bf16))
    total = group * length
    scratch = [
        pltpu.VMEM((3 * inner + 16, total), bf16),
        pltpu.VMEM((inner + 16, total), bf16),
        pltpu.VMEM((inner, total), bf16),
        pltpu.VMEM((2, inner, total), bf16),
        pltpu.VMEM((inner, total), f32),
        pltpu.VMEM((inner, total), f32),
        pltpu.VMEM((width, total), bf16),
    ]
    scratch.append(pltpu.VMEM(tails.shape, f32))
    return pl.pallas_call(
        functools.partial(
            middle_kernel, batches, prompts, group, len(mids), before is not None, chunks > 0
        ),
        grid=(batches // group,),
        in_specs=in_specs,
        out_specs=[block(a) for a in out_like] + [WHOLE] * len(sums),
        out_shape=out_like + sums,
        scratch_shapes=scratch,
        compiler_params=PARAMS,
        cost_estimate=cost(batches * length * 9 * inner * width, 3 * x.size * 2),
        name="middle",
    )(*args)


def inner_back_kernel(has_rim, has_before, has_after, *refs):
    (act_ref, g_ref, n2_ref, r2_ref, vec2), refs = refs[:5], refs[5:]
    if has_rim:
        rim, refs = refs[0], refs[1:]
    if has_before:
        before, refs = refs[:3], refs[3:]
    gh_ref, sums, refs = refs[0], refs[1:4], refs[4:]
    if has_after:
        in_chunks, refs = refs[0], refs[1:]
    (kept,) = refs
    gw_in, g_gain2, g_shift2 = sums
    inner = vec2.shape[1]
    step = pl.program_id(0)

    @pl.when(step == 0)
    def _():
        for k, ref in enumerate(sums):
            ref[...] = before[k][...] if has_before else jnp.zeros_like(ref)

    g, n2, r2, gh = (Columns(ref) for ref in (g_ref, n2_ref, r2_ref, gh_ref))

    def g_in(t, c):
        value = g.get(t, c)
        if has_rim:
            piece = rim[t, c * REACH : (c + 1) * REACH]
            value += jnp.concatenate([jnp.zeros((TILE, LANES - REACH), f32), piece], axis=1)
        return value

    def keep(t, c, u):
        kept[t, at(c)] = u

    totals = backward_pass(g.count, inner, n2.get, g_in, vec2, (g_gain2, g_shift2), keep)
    for c in range(g.count):
        mean_u, mean_un = totals[c]
        scale = r2.get(ROW, c)
        by_n, constant = -(scale * mean_un), -(scale * mean_u)
        for t in tiles(inner):
            gh.put(t, c, kept[t, at(c)] * scale + (n2.get(t, c) * by_n + constant))
    for q in range(act_ref.shape[0]):
        gw_in[...] += dot(gh_ref[q], act_ref[q], 1, 1)

    if has_after:

        @pl.when(step == pl.num_programs(0) - 1)
        def _():
            count, few, wide = in_chunks.shape
            gw_in[:, wide - 2 : wide - 1] = jnp.sum(g_gain2[...], axis=1, keepdims=True)
            gw_in[:, wide - 1 : wide] = jnp.sum(g_shift2[...], axis=1, keepdims=True)
            for r in range(count):
                in_chunks[r] = gw_in[r * few : (r + 1) * few, :wide].astype(bf16)


def inner_back(act, g, n2, r2, part, vec2, rim=None, before=None, chunks=0):
    inner = vec2.shape[1]
    batches, width = act.shape[0], act.shape[1] - 16
    lanes, group, first = part
    in_specs = [blocks(act.shape, lanes, group, first)]
    in_specs += [blocks(a.shape, lanes, group, 0) for a in (g, n2, r2)] + [WHOLE]
    args = [act, g, n2, r2, vec2]
    if rim is not None:
        args.append(rim)
        in_specs.append(pl.BlockSpec((inner, GROUP * REACH), lambda i: (0, i)))
    if before is not None:
        args += before
        in_specs += [WHOLE] * 3
    sums = [shape_of(inner, width + 16), shape_of(inner, LANES), shape_of(inner, LANES)]
    if chunks:
        sums.append(shape_of(chunks, inner // chunks, width + 3, kind=bf16))
    return pl.pallas_call(
        functools.partial(inner_back_kernel, rim is not None, before is not None, chunks > 0),
        grid=(batches // group,),
        in_specs=in_specs,
        out_specs=[blocks(g.shape, lanes, group, 0)] + [WHOLE] * len(sums),
        out_shape=[shape_of(*g.shape, kind=bf16)] + sums,
        scratch_shapes=[pltpu.VMEM((inner, group * lanes), f32)],
        compiler_params=PARAMS,
        cost_estimate=cost(4 * width * inner * batches * lanes, 0),
        name="inner_back",
    )(*args)


def outer_back_kernel(pieces, has_before, has_into, has_after, *refs):
    (x_ref, cot_ref, mean_ref, scale_ref), refs = refs[:4], refs[4:]
    ghs, refs = refs[:pieces], refs[pieces:]
    (w_in, vec1), refs = refs[:2], refs[2:]
    if has_before:
        before, refs = refs[:2], refs[2:]
    if has_into:
        refs = refs[1:]
    out_ref, sums, refs = refs[0], refs[1:3], refs[3:]
    if has_after:
        small, refs = refs[0], refs[1:]
    (g_act,) = refs
    width = w_in.shape[0]
    step = pl.program_id(0)

    @pl.when(step == 0)
    def _():
        for k, ref in enumerate(sums):
            ref[...] = before[k][...] if has_before else jnp.zeros_like(ref)

    first = 0
    for gh in ghs:
        length = gh.shape[-1]
        g_act[:, first : first + length] = dot(w_in[...], gh[0], 1, 0)
        first += length
    x, cot, mean, scale, out = (Columns(r) for r in (x_ref, cot_ref, mean_ref, scale_ref, out_ref))
    scales = [scale.get(ROW, c) for c in range(x.count)]
    means = [mean.get(ROW, c) for c in range(x.count)]
    shifts = [a * b for a, b in zip(means, scales)]

    def keep(t, c, u):
        g_act[t, at(c)] = u

    totals = backward_pass(
        x.count,
        width,
        lambda t, c: x.get(t, c) * scales[c] - shifts[c],
        lambda t, c: g_act[t, at(c)],
        vec1,
        sums,
        keep,
    )
    for c in range(x.count):
        mean_u, mean_un = totals[c]
        by_x = -(scales[c] * scales[c] * mean_un)
        constant = -(scales[c] * mean_u) - means[c] * by_x
        for t in tiles(width):
            change = g_act[t, at(c)] * scales[c] + (x.get(t, c) * by_x + constant)
            out.put(t, c, cot.get(t, c) + change)

    if has_after:

        @pl.when(step == pl.num_programs(0) - 1)
        def _():
            for k in range(2):
                small[:, k * width : (k + 1) * width] = down(sums[k][...].T)


def outer_back(
    x, cot, mean, scale, ghs, w_in, vec1, batches, before=None, into=None, last=False
):
    first, count = batches
    width, lanes = x.shape[2:]
    block = lambda a: blocks(a.shape, a.shape[-1], 1, 0, first)
    args = [x, cot, mean, scale] + ghs
    in_specs = [block(a) for a in args] + [WHOLE] * 2
    args += [w_in, vec1]
    if before is not None:
        args += before
        in_specs += [WHOLE] * 2
    aliases = {}
    if into is not None:
        aliases = {len(args): 0}
        args.append(into)
        in_specs.append(pl.BlockSpec(memory_space=pl.ANY))
    sums = [shape_of(width, LANES), shape_of(width, LANES)]
    if last:
        sums.append(shape_of(1, 2 * width))
    return pl.pallas_call(
        functools.partial(
            outer_back_kernel, len(ghs), before is not None, into is not None, last
        ),
        grid=(count,),
        in_specs=in_specs,
        out_specs=[block(x)] + [WHOLE] * len(sums),
        out_shape=[shape_of(*x.shape)] + sums,
        scratch_shapes=[pltpu.VMEM((width, lanes), f32)],
        input_output_aliases=aliases,
        compiler_params=PARAMS,
        cost_estimate=cost(8 * w_in.size * count * lanes, 0),
        name="outer_back",
    )(*args)


def packing_kernel(inner, ids, early_ref, late_ref, *refs):
    pieces, packed = refs[:-1], refs[-1]
    early, late = (jnp.sum(ref[...].astype(f32), axis=0) for ref in (early_ref, late_ref))
    shards = len(pieces)
    width = late.shape[1] - 3
    own, wide = inner // shards, width // shards
    conv_end = 3 * inner + 3
    firsts = range(conv_end, early.shape[1], inner + 1)
    kept = [early[:, first + inner : first + inner + 1] for first in firsts]
    kept += [early[:, 3 * inner : conv_end], late[:, width:]]
    starts = list(firsts) + [k * inner for k in range(3)]
    for j in range(shards):
        parts = [early[:, first + j * own : first + (j + 1) * own] for first in starts]
        parts += [late[:, j * wide : (j + 1) * wide]]
        packed[ids[0] ^ j] = jnp.concatenate(parts + kept, axis=1)
    for k in range(shards):
        pieces[k][...] = packed[k].astype(pieces[k].dtype)


def packing(ids, shards, inner, early, late):
    few, width = early.shape[1], late.shape[2] - 3
    wide = (2 * width + 3 * inner) // shards + width // inner + 6
    kinds = [f32] + [bf16] * (shards - 1)
    return pl.pallas_call(
        functools.partial(packing_kernel, inner),
        in_specs=[pl.BlockSpec(memory_space=pltpu.SMEM)] + [WHOLE] * 2,
        out_specs=[WHOLE] * shards,
        out_shape=[shape_of(few, wide, kind=kind) for kind in kinds],
        scratch_shapes=[pltpu.VMEM((shards, few, wide), f32)],
        compiler_params=PARAMS,
        name="packing",
    )(ids, early, late)


def unpacking_kernel(whole, by_out, by_conv, by_in, by_width, by_inner, tall, tall_in):
    reps, few, _ = whole.shape
    own, width = by_out.shape
    inner = by_conv.shape[1]
    wide = by_in.shape[0]
    twice = width // inner
    first_in = (twice + 3) * own
    small = first_in + wide
    for r in range(reps):
        piece = whole[r].astype(f32)
        for h in range(twice):
            rows = slice((r * twice + h) * few, (r * twice + h + 1) * few)
            tall[rows, :own] = piece[:, h * own : (h + 1) * own]
            tall[rows, own : own + 1] = piece[:, small + h : small + h + 1]
        rows = slice(r * few, (r + 1) * few)
        for k in range(3):
            by_conv[k, rows, :] = piece[:, (twice + k) * own : (twice + k + 1) * own]
        tall_in[rows, :wide] = piece[:, first_in : first_in + wide]
        tall_in[rows, wide : wide + 6] = piece[:, small + twice : small + twice + 6]
    turned = tall[...].T
    by_out[...] = turned[:own]
    by_width[...] = turned[own : own + 1]
    turned = tall_in[...].T
    by_in[...] = turned[:wide]
    by_inner[...] = turned[wide : wide + 6]


def unpacking(whole, shards, inner, width):
    own, wide = inner // shards, width // shards
    up = lambda n: -(-n // LANES) * LANES
    return pl.pallas_call(
        unpacking_kernel,
        in_specs=[WHOLE],
        out_specs=[WHOLE] * 5,
        out_shape=[
            shape_of(own, width),
            shape_of(3, inner, own),
            shape_of(wide, inner),
            shape_of(1, width),
            shape_of(6, inner),
        ],
        scratch_shapes=[
            pltpu.VMEM((width, up(own + 1)), f32),
            pltpu.VMEM((inner, up(wide + 6)), f32),
        ],
        compiler_params=PARAMS,
        name="unpacking",
    )(whole)


def passed_along(x, axis, by):
    size = lax.axis_size(axis)
    pairs = [(i, i + by) for i in range(size) if 0 <= i + by < size]
    return lax.ppermute(x, axis, pairs)


def swapped(x, axis, k):
    return lax.ppermute(x, axis, [(i, i ^ k) for i in range(lax.axis_size(axis))])


def gathered(x):
    size = lax.axis_size("shard")
    return jnp.stack([x] + [swapped(x, "shard", k) for k in range(1, size)])


def after(value, *others):
    return lax.optimization_barrier((value,) + others)[0]


def sent_from_last(x, axis):
    size = lax.axis_size(axis)
    me = lax.axis_index(axis)
    value = x
    for j in range(size - 1):
        piece = lax.ppermute(x, axis, [(size - 1, j)])
        value = jnp.where(me == j, piece, value)
    return value


def summed_at_last(x, axis):
    size = lax.axis_size(axis)
    total = x.astype(f32)
    for j in range(size - 1):
        total = total + lax.ppermute(x, axis, [(j, size - 1)]).astype(f32)
    return total


def dealt(x, axis):
    return lax.all_to_all(x, axis, 0, 0, tiled=True)


def collected(x, axis):
    return dealt(jnp.broadcast_to(x[None], (lax.axis_size(axis),) + x.shape), axis)


def on_device(
    prompt_x,
    cont_x,
    cont_map,
    cont_start,
    w_in,
    w_conv,
    w_out,
    norm1_gain,
    norm1_bias,
    bias_in,
    norm2_gain,
    norm2_bias,
    bias_conv,
    norm3_gain,
    norm3_bias,
    bias_out,
    prompt_cot,
    cont_cot,
):
    inner = w_conv.shape[2]
    turned = lambda a: jnp.swapaxes(a, 2, 3)
    prompt_x, cont_x, prompt_cot, cont_cot = map(turned, (prompt_x, cont_x, prompt_cot, cont_cot))
    width = prompt_x.shape[2]
    shards, reps = lax.axis_size("shard"), lax.axis_size("rep")
    is_last = lax.axis_index("shard") == shards - 1
    own = w_out.shape[0]
    parts = splits(own)
    ids = jnp.stack([lax.axis_index("shard"), lax.axis_index("rep") % 2]).astype(jnp.int32)
    rows = (norm1_gain, norm1_bias, norm2_gain, norm2_bias, norm3_gain, norm3_bias)
    in_part, rest_part, vec1, vec2, vec3 = sending(ids, w_in, w_conv, w_out, rows)
    rows_p, rows_c = prompt_x.shape[3], cont_x.shape[3]
    last = (LANES, GROUP, rows_p - LANES)
    rest = (rows_p - LANES, 1, 0)
    every = (rows_c, 1, 0)
    have_first = rows_p > LANES
    act_p, mean_p, scale_p, act_c, mean_c, scale_c = lead([prompt_x, cont_x], vec1)
    in_pieces, act_p = lax.optimization_barrier((gathered(in_part), act_p))
    half_in, w_in_t = taking_in(ids, in_pieces, bias_in)
    mid_l, n2_l, r2_l, rim = front([act_p], [last], w_in_t, vec2, with_rim=True)
    halo = passed_along(rim, "shard", 1)
    rest_pieces, act_c, rim = lax.optimization_barrier((gathered(rest_part), act_c, rim))
    if parts == 2:
        rest_pieces = jnp.stack([rest_pieces, swapped(rest_pieces, "rep", 1)])
    else:
        rest_pieces = rest_pieces[None]
    own_tail = sent_from_last(rim, "shard")
    if have_first:
        mid_f, n2_f, r2_f, mid_c, n2_c, r2_c = front([act_p, act_c], [rest, every], w_in_t, vec2)
        mids = [mid_f, mid_l]
    else:
        mid_c, n2_c, r2_c = front([act_c], [every], w_in_t, vec2)
        mids = [mid_l]
    rest_pieces, own_tail, mid_c = lax.optimization_barrier((rest_pieces, own_tail, mid_c))
    tails = collected(own_tail, "rep")

    weights = (*taking_rest(ids, rest_pieces, bias_conv, bias_out), vec3)
    prompt_out, *results = middle(True, 2, [], mids, prompt_x, prompt_cot, halo, weights)
    g_ps, results = results[: len(mids)], results[len(mids) :]
    sums, rim_out = results[:4], results[4]
    back_rim = passed_along(rim_out, "shard", -1)
    cont_out, g_c, *results = middle(
        False,
        2,
        [cont_start, cont_map],
        [mid_c],
        cont_x,
        cont_cot,
        tails,
        weights,
        before=sums,
        chunks=reps,
    )
    table, early = results[4:]
    table = dealt(table, "rep")

    sums = None
    gh_ps = []
    if have_first:
        gh_f, *sums = inner_back(act_p, g_ps[0], n2_f, r2_f, rest, vec2)
        gh_ps.append(gh_f)
    gh_c, *sums = inner_back(act_c, g_c, n2_c, r2_c, every, vec2, before=sums)
    table, gh_c = lax.optimization_barrier((table, gh_c))
    own_tail = jnp.sum(table.astype(f32), axis=0).astype(bf16)
    own_tail, early = lax.optimization_barrier((own_tail, early))
    own_tail = summed_at_last(own_tail, "shard")
    early = dealt(early, "rep")
    batches = prompt_x.shape[0]
    one, two = (0, batches // 2), (batches // 2, batches // 2)
    outer_c = functools.partial(
        outer_back, cont_x, cont_cot, mean_c, scale_c, [gh_c], half_in, vec1
    )
    outer_p = functools.partial(outer_back, prompt_x, prompt_cot, mean_p, scale_p)
    cont_grad, *sums1 = outer_c(one)
    cont_grad, own_tail = lax.optimization_barrier((cont_grad, own_tail))
    rim_in = back_rim.astype(f32) + jnp.where(is_last, own_tail, 0.0)
    gh_l, *results = inner_back(
        act_p, g_ps[-1], n2_l, r2_l, last, vec2, rim=rim_in, before=sums, chunks=reps
    )
    late, early, gh_l = lax.optimization_barrier((results[3], early, gh_l))
    gh_ps.append(gh_l)
    late = dealt(late, "rep")
    cont_grad, *sums1 = outer_c(two, before=sums1, into=after(cont_grad, gh_l))
    late, cont_grad = lax.optimization_barrier((late, cont_grad))

    mine, *others = packing(ids, shards, inner, early, late)
    others = [swapped(other, "shard", k + 1) for k, other in enumerate(others)]
    prompt_grad, *sums1 = outer_p(
        gh_ps, half_in, vec1, one, before=[after(sums1[0], mine), sums1[1]]
    )
    *others, prompt_grad = lax.optimization_barrier((*others, prompt_grad))
    mine = mine + sum(other.astype(f32) for other in others)
    whole = collected(mine, "rep")
    prompt_grad, *results = outer_p(
        gh_ps, half_in, vec1, two, before=sums1, into=after(prompt_grad, mine), last=True
    )
    ones = jnp.sum(lax.optimization_barrier(lax.all_gather(results[2], "rep")), axis=0)
    whole, ones = lax.optimization_barrier((whole, ones))
    ones = (ones + sum(swapped(ones, "shard", k) for k in range(1, shards)))[0]
    grad_w_out, grad_w_conv, grad_w_in, grad_bias_out, small = unpacking(whole, shards, inner, width)
    grad_bias_conv, grad_gain3, grad_shift3, grad_bias_in, grad_gain2, grad_shift2 = small
    return (
        turned(prompt_out),
        turned(cont_out),
        turned(prompt_grad),
        turned(cont_grad),
        grad_w_in,
        jnp.swapaxes(grad_w_conv, 1, 2),
        grad_w_out,
        ones[:width],
        ones[width:],
        grad_bias_in,
        grad_gain2,
        grad_shift2,
        grad_bias_conv,
        grad_gain3,
        grad_shift3,
        grad_bias_out[0],
    )


def solution(mesh):
    rows = P(None, "rep", "shard", None)
    buffers = P(None, ("rep", "shard"), None, None)
    in_specs = (
        rows,
        buffers,
        P(None, ("rep", "shard"), None),
        P(None, ("rep", "shard"), None),
        P("shard", None),
        P(None, "shard", None),
        P("shard", None),
    ) + (P(),) * 9 + (rows, buffers)
    out_specs = (
        rows,
        buffers,
        rows,
        buffers,
        P("shard", None),
        P(None, "shard", None),
        P("shard", None),
    ) + (P(),) * 9
    return jax.shard_map(
        on_device, mesh=mesh, in_specs=in_specs, out_specs=out_specs, check_vma=False
    )
```

```python
import functools

import jax
import jax.numpy as jnp
from jax import lax
from jax.experimental import pallas as pl
from jax.experimental.pallas import tpu as pltpu
from jax.sharding import PartitionSpec as P

STEP = 16
REACH = 2 * STEP
LANES = 128
GROUP = 4
TILE = 16
epsilon = 1e-05
bf16 = jnp.bfloat16
f32 = jnp.float32
VMEM_BYTES = 58 * 2**20
WHOLE = pl.BlockSpec(memory_space=pltpu.VMEM)
PARAMS = pltpu.CompilerParams(vmem_limit_bytes=VMEM_BYTES)


def cost(flops, moved):
    return pl.CostEstimate(flops=int(2.5 * flops), bytes_accessed=int(moved), transcendentals=0)


def dot(a, b, ca, cb):
    return lax.dot_general(a, b, (((ca,), (cb,)), ((), ())), preferred_element_type=f32)


def at(column):
    return slice(column * LANES, (column + 1) * LANES)


def tiles(depth):
    return [slice(r, r + TILE) for r in range(0, depth, TILE)]


class Columns:
    def __init__(self, ref):
        self.ref = ref
        self.per = ref.shape[-1] // LANES
        self.count = ref.shape[0] * self.per

    def key(self, rows, c):
        return (c // self.per,) + (0,) * (len(self.ref.shape) - 3) + (rows, at(c % self.per))

    def get(self, rows, c):
        return self.ref[self.key(rows, c)].astype(f32)

    def put(self, rows, c, values):
        self.ref[self.key(rows, c)] = values.astype(self.ref.dtype)


ROW = slice(0, 1)


def down(values):
    return jnp.sum(values, axis=0, keepdims=True)


def stats(load, depth, columns):
    zero = jnp.zeros((TILE, LANES), f32)
    sums = [zero] * columns
    for t in tiles(depth):
        sums = [s + load(t, c) for c, s in enumerate(sums)]
    means = [down(s) * (1.0 / depth) for s in sums]
    sums = [zero] * columns
    for t in tiles(depth):
        for c in range(columns):
            center = load(t, c) - means[c]
            sums[c] = sums[c] + center * center
    scales = [lax.rsqrt(down(s) * (1.0 / depth) + epsilon) for s in sums]
    return means, scales


def halved(vec):
    return 0.5 * vec


def backward_pass(columns, depth, normed, g_in, vec, sums, keep, act=None, kind=f32):
    g_gain, g_shift = sums
    unit = jnp.asarray(1.0, kind)
    zero = jnp.zeros((TILE, LANES), f32)
    totals = [[zero, zero] for _ in range(columns)]
    for t in tiles(depth):
        gain, shift = vec[0, t, :], vec[1, t, :]
        half_gain, half_shift = halved(gain).astype(kind), halved(shift).astype(kind)
        gains = shifts = None
        for c in range(columns):
            n = normed(t, c)
            half = n.astype(kind) * half_gain + half_shift
            tan = jnp.tanh(half)
            if act is not None:
                act(t, c, half * tan + half)
            slope = (unit + tan) * (unit + half * (unit - tan))
            g = g_in(t, c) * slope.astype(f32)
            gn = g * n
            u = g * gain
            keep(t, c, u)
            totals[c][0] = totals[c][0] + u
            totals[c][1] = totals[c][1] + gn * gain
            gains = gn if gains is None else gains + gn
            shifts = g if shifts is None else shifts + g
        g_gain[t, :] += gains
        g_shift[t, :] += shifts
    return [[down(s) * (1.0 / depth) for s in pair] for pair in totals]


def blocks(shape, lanes, group, first, batch=0):
    full = (group,) + tuple(shape[1:-1]) + (lanes,)
    zeros = (0,) * (len(shape) - 2)
    return pl.BlockSpec(full, lambda i: (i + batch // group,) + zeros + (first // lanes,))


def shape_of(*shape, kind=f32):
    return jax.ShapeDtypeStruct(shape, kind)


def splits(own):
    return 2 if own % 2 == 0 else 1


def sending_kernel(ids, w_in, w_conv_t, w_out, row, in_part, rest_part, *vecs):
    own, width = w_out.shape
    inner = w_conv_t.shape[1]
    parts = splits(own)
    few = own // parts
    some = in_part.shape[0]
    strips = [w_in[r : r + some, :] for r in range(0, w_in.shape[0], some)]
    in_part[...] = jnp.concatenate(strips, axis=1).astype(bf16)
    conv = [w_conv_t[k].T for k in range(3)]
    for h in range(parts):

        @pl.when(ids[1] % parts == h)
        def _():
            mine = slice(h * few, (h + 1) * few)
            pieces = [turn[mine] for turn in conv]
            pieces += [w_out[mine, q : q + inner] for q in range(0, width, inner)]
            rest_part[...] = jnp.concatenate(pieces, axis=1).astype(bf16)

    first = 0
    for vec in vecs:
        for k in range(2):
            depth = vec.shape[1]
            vec[k] = jnp.broadcast_to(row[:, first : first + depth], (LANES, depth)).T
            first += depth


def sending(ids, w_in, w_conv, w_out, row):
    own, width = w_out.shape
    inner = w_conv.shape[2]
    parts = splits(own)
    strips = 5 if w_in.shape[0] % 5 == 0 else 1
    return pl.pallas_call(
        sending_kernel,
        in_specs=[pl.BlockSpec(memory_space=pltpu.SMEM)] + [WHOLE] * 4,
        out_specs=[WHOLE] * 5,
        out_shape=[
            shape_of(w_in.shape[0] // strips, strips * inner, kind=bf16),
            shape_of(own // parts, (3 + width // inner) * inner, kind=bf16),
            shape_of(2, width, LANES),
            shape_of(2, inner, LANES),
            shape_of(2, inner, LANES),
        ],
        compiler_params=PARAMS,
        name="sending",
    )(ids, w_in, jnp.swapaxes(w_conv, 1, 2), w_out, row)


def with_shift(weights, shift):
    parts = []
    left = shift
    for _ in range(3):
        part = left.astype(bf16).astype(f32)
        parts.append(part)
        left = left - part
    parts.append(jnp.zeros((13, shift.shape[1]), f32))
    return jnp.concatenate([weights.T, jnp.concatenate(parts, axis=0).T], axis=1).astype(bf16)


def taking_in_kernel(where, ids, pieces, vecs, half_in, w_in_t, total):
    shards, some, wide = pieces.shape
    inner = total.shape[1]
    strips = wide // inner
    for j in range(shards):
        piece = pieces[ids[0] ^ j].astype(f32)
        for k in range(strips):
            first = (j * strips + k) * some
            total[first : first + some, :] = piece[:, k * inner : (k + 1) * inner]
    half_in[...] = (0.5 * total[...]).astype(bf16)
    w_in_t[...] = with_shift(total[...], vecs[:, where : where + inner])


def taking_in(ids, pieces, vecs, where, inner):
    shards, some, wide = pieces.shape
    width = shards * some * wide // inner
    return pl.pallas_call(
        functools.partial(taking_in_kernel, where),
        in_specs=[pl.BlockSpec(memory_space=pltpu.SMEM)] + [WHOLE] * 2,
        out_specs=[WHOLE] * 2,
        out_shape=[shape_of(width, inner, kind=bf16), shape_of(inner, width + 16, kind=bf16)],
        scratch_shapes=[pltpu.VMEM((width, inner), f32)],
        compiler_params=PARAMS,
        name="taking_in",
    )(ids, pieces, vecs)


def taking_rest_kernel(where, ids, pieces, vecs, *refs):
    (w_conv_t, half_conv, w_out_t, half_out), (conv, out) = refs[:4], refs[4:]
    parts, shards, few, _ = pieces.shape
    inner, width = out.shape
    for j in range(shards):
        for h in range(parts):
            first = (j * parts + h) * few
            piece = pieces[h ^ (ids[1] % parts), ids[0] ^ j].astype(f32)
            for k in range(3):
                strip = piece[:, k * inner : (k + 1) * inner]
                conv[k * inner + first : k * inner + first + few, :] = strip
            out[first : first + few, :] = piece[:, 3 * inner :]
    half_conv[...] = (0.5 * conv[...]).astype(bf16)
    w_conv_t[...] = with_shift(conv[...], vecs[:, where : where + inner])
    half_out[...] = (0.5 * out[...]).astype(bf16)
    w_out_t[...] = with_shift(out[...], vecs[:, where + inner : where + inner + width])


def taking_rest(ids, pieces, vecs, where, inner, width):
    return pl.pallas_call(
        functools.partial(taking_rest_kernel, where),
        in_specs=[pl.BlockSpec(memory_space=pltpu.SMEM)] + [WHOLE] * 2,
        out_specs=[WHOLE] * 4,
        out_shape=[
            shape_of(inner, 3 * inner + 16, kind=bf16),
            shape_of(3 * inner, inner, kind=bf16),
            shape_of(width, inner + 16, kind=bf16),
            shape_of(inner, width, kind=bf16),
        ],
        scratch_shapes=[pltpu.VMEM((3 * inner, inner), f32), pltpu.VMEM((inner, width), f32)],
        compiler_params=PARAMS,
        name="taking_rest",
    )(ids, pieces, vecs)


def lead_kernel(*refs):
    x_refs, vec1, outs = refs[:2], refs[2], refs[3:]
    for s in range(2):
        x, act, mean, scale = (Columns(ref) for ref in (x_refs[s],) + tuple(outs[3 * s : 3 * s + 3]))
        depth = x_refs[s].shape[-2]
        means, scales = stats(x.get, depth, x.count)
        for c in range(x.count):
            mean.put(ROW, c, means[c])
            scale.put(ROW, c, scales[c])
        shifts = [m * v for m, v in zip(means, scales)]
        for t in tiles(depth):
            gain, shift = halved(vec1[0, t, :]), halved(vec1[1, t, :])
            for c in range(x.count):
                half = (x.get(t, c) * scales[c] - shifts[c]) * gain + shift
                act.put(t, c, half * jnp.tanh(half) + half)
        for c in range(x.count):
            act.put(slice(depth, depth + 16), c, jnp.ones((16, LANES), f32))


def lead(xs, vec1):
    batches, _, width, _ = xs[0].shape
    in_specs, out_specs, out_shape = [], [], []
    for x in xs:
        lanes = x.shape[3]
        in_specs.append(blocks(x.shape, lanes, 1, 0))
        for depth, kind in ((width + 16, bf16), (1, f32), (1, f32)):
            out_specs.append(blocks((batches, depth, lanes), lanes, 1, 0))
            out_shape.append(shape_of(batches, depth, lanes, kind=kind))
    return pl.pallas_call(
        lead_kernel,
        grid=(batches,),
        in_specs=in_specs + [WHOLE],
        out_specs=out_specs,
        out_shape=out_shape,
        compiler_params=PARAMS,
        cost_estimate=cost(0, sum(x.size for x in xs) * 4),
        name="lead",
    )(*xs, vec1)


def front_kernel(streams, with_rim, *refs):
    acts, refs = refs[:streams], refs[streams:]
    (w_in_t, vec2), refs = refs[:2], refs[2:]
    outs, refs = [refs[3 * s : 3 * s + 3] for s in range(streams)], refs[3 * streams :]
    rim_ref = refs[0] if with_rim else None
    hiddens = refs[-streams:]
    inner = w_in_t.shape[0]
    for s in range(streams):
        act, hidden = acts[s], hiddens[s]
        mid, n2, r2 = (Columns(ref) for ref in outs[s])
        wide = act.shape[2]
        for q in range(act.shape[0]):
            hidden[:, q * wide : (q + 1) * wide] = dot(w_in_t[...], act[q], 1, 0)
        load = lambda t, c: hidden[t, at(c)]
        means, scales = stats(load, inner, mid.count)
        shifts = [m * v for m, v in zip(means, scales)]
        for c in range(mid.count):
            r2.put(ROW, c, scales[c])
        for t in tiles(inner):
            gain, shift = halved(vec2[0, t, :]), halved(vec2[1, t, :])
            rim = []
            for c in range(mid.count):
                n = load(t, c) * scales[c] - shifts[c]
                half = n * gain + shift
                value = half * jnp.tanh(half) + half
                mid.put(t, c, value)
                n2.put(t, c, n)
                rim.append(value[:, LANES - REACH :])
            if with_rim:
                rim_ref[t, :] = jnp.concatenate(rim, axis=1).astype(bf16)


def front(acts, parts, w_in_t, vec2, with_rim=False):
    inner = w_in_t.shape[0]
    batches = acts[0].shape[0]
    in_specs, out_specs, out_shape, scratch = [], [], [], []
    for act, (lanes, group, first) in zip(acts, parts):
        in_specs.append(blocks(act.shape, lanes, group, first))
        for depth, kind in ((inner, bf16), (inner, bf16), (1, f32)):
            out_specs.append(blocks((batches, depth, lanes), lanes, group, 0))
            out_shape.append(shape_of(batches, depth, lanes, kind=kind))
        scratch.append(pltpu.VMEM((inner, group * lanes), f32))
    if with_rim:
        out_specs.append(pl.BlockSpec((inner, GROUP * REACH), lambda i: (0, i)))
        out_shape.append(shape_of(inner, batches * REACH, kind=bf16))
    return pl.pallas_call(
        functools.partial(front_kernel, len(acts), with_rim),
        grid=(batches // parts[0][1],),
        in_specs=in_specs + [WHOLE] * 2,
        out_specs=out_specs,
        out_shape=out_shape,
        scratch_shapes=scratch,
        compiler_params=PARAMS,
        cost_estimate=cost(4 * w_in_t.size * sum(batches * part[0] for part in parts), 0),
        name="front",
    )(*acts, w_in_t, vec2)


def shifted_right(values, by):
    zeros = jnp.zeros((values.shape[0], by), values.dtype)
    return jnp.concatenate([zeros, values[:, : values.shape[1] - by]], axis=1)


def shifted_left(values, by):
    zeros = jnp.zeros((values.shape[0], by), values.dtype)
    return jnp.concatenate([values[:, by:], zeros], axis=1)


def chosen(base, position, fits, batches):
    one = jnp.where(jnp.logical_and(fits, position < STEP), base + STEP + position, -1)
    two = jnp.where(jnp.logical_and(fits, position < REACH), base + position, -1)
    target = jnp.concatenate([one, two], axis=1)
    row = lax.broadcasted_iota(jnp.int32, (batches * REACH, target.shape[1]), 0)
    return jnp.where(row == target, 1.0, 0.0).astype(bf16)


def middle_kernel(batches, prompts, group, pieces, has_before, has_after, *refs):
    if not prompts:
        (cont_start, cont_map), refs = refs[:2], refs[2:]
    mids, refs = refs[:pieces], refs[pieces:]
    (x_ref, cot_ref, tails), refs = refs[:3], refs[3:]
    (w_conv_t, w_conv, w_out_t, w_out, vec3), refs = refs[:5], refs[5:]
    if has_before:
        before, refs = refs[:4], refs[4:]
    out_ref, gs, refs = refs[0], refs[1 : 1 + pieces], refs[1 + pieces :]
    if has_after:
        (table_out, chunks), sums, refs = refs[:2], refs[2:6], refs[6:]
    else:
        sums, table_out, refs = refs[:4], refs[4], refs[5:]
    table, refs = refs[-1], refs[:-1]
    gw_out, gw_conv, g_gain3, g_shift3 = sums
    taps, act, gc, gt, conv, g_act, cots = refs
    width = w_out_t.shape[0]
    inner = w_out.shape[0]
    step = pl.program_id(0)
    length = taps.shape[1] // group
    columns = taps.shape[1] // LANES

    @pl.when(step == 0)
    def _():
        for k, ref in enumerate(sums):
            ref[...] = before[k][...] if has_before else jnp.zeros_like(ref)
        table[...] = jnp.zeros_like(table)
        taps[3 * inner :, :] = jnp.ones_like(taps[3 * inner :, :])
        act[inner:, :] = jnp.ones_like(act[inner:, :])

    reads = []
    for q in range(group):
        m = step * group + q
        base = m * REACH
        here = q * length
        span = slice(here, here + length)
        start_span = slice(here, here + LANES)
        cots[:, span] = cot_ref[q, 0]
        mid = mids[0][q] if pieces == 1 else jnp.concatenate([ref[q] for ref in mids], axis=1)
        lane = lax.broadcasted_iota(jnp.int32, (1, LANES), 1)
        if prompts:
            begin = chosen(base, lane, lane >= 0, batches)
            before_rows = tails[...]
            reads.append((begin,))
        else:
            start = cont_start[0, 1, m]
            owners = cont_map[0, 0, m], cont_map[0, 1, m]
            at_most = (length // LANES - 2) * LANES
            window = jnp.minimum(lax.shift_right_logical(start, 7) * LANES, at_most)
            wide = pl.ds(pl.multiple_of(here + window, LANES), 2 * LANES)
            begin = chosen(base, lane, lane < start, batches)
            before_rows = tails[owners[0]]
        first = dot(before_rows, begin, 1, 0).astype(bf16)
        taps[0:inner, span] = mid
        one, two = shifted_right(mid, STEP), shifted_right(mid, REACH)
        if not prompts:
            row = lax.broadcasted_iota(jnp.int32, (1, length), 1)
            since = jnp.where(row < start, row, row - start)
            near_one = jnp.where(since >= STEP, 1.0, 0.0)
            near_two = jnp.where(since >= REACH, 1.0, 0.0)
            full = lambda w: jnp.broadcast_to(w, (inner, length)).astype(bf16)
            one, two = one * full(near_one), two * full(near_two)
        taps[inner : 2 * inner, span] = one
        taps[2 * inner : 3 * inner, span] = two
        taps[inner : 2 * inner, start_span] += first[:, :LANES]
        taps[2 * inner : 3 * inner, start_span] += first[:, LANES:]
        if not prompts:
            offset = window + lax.broadcasted_iota(jnp.int32, (1, 2 * LANES), 1) - start
            later = chosen(base, offset, offset >= 0, batches)
            far = dot(tails[owners[1]], later, 1, 0).astype(bf16)
            taps[inner : 2 * inner, wide] += far[:, : 2 * LANES]
            taps[2 * inner : 3 * inner, wide] += far[:, 2 * LANES :]
            reads.append((begin, owners, wide, later, near_one, near_two))
    conv[...] = dot(w_conv_t[...], taps[...], 1, 0)
    g_act[...] = dot(w_out[...], cots[...], 1, 0)
    load = lambda t, c: conv[t, at(c)]
    means, scales = stats(load, inner, columns)
    shifts = [a * b for a, b in zip(means, scales)]

    def keep(t, c, u):
        g_act[t, at(c)] = u

    def put_act(t, c, value):
        act[t, at(c)] = value.astype(bf16)

    totals = backward_pass(
        columns,
        inner,
        lambda t, c: load(t, c) * scales[c] - shifts[c],
        lambda t, c: g_act[t, at(c)],
        vec3,
        (g_gain3, g_shift3),
        keep,
        put_act,
    )
    for c in range(columns):
        mean_u, mean_un = totals[c]
        by_x = -(scales[c] * scales[c] * mean_un)
        constant = -(scales[c] * mean_u) - means[c] * by_x
        for t in tiles(inner):
            g_in = g_act[t, at(c)] * scales[c] + (load(t, c) * by_x + constant)
            gc[t, at(c)] = g_in.astype(bf16)
    branch = dot(w_out_t[...], act[...], 1, 0)
    for q in range(group):
        span = slice(q * length, (q + 1) * length)
        out_ref[q, 0] = (x_ref[q, 0].astype(f32) + branch[:, span]).astype(bf16)
    gw_out[...] += dot(cots[...], act[...], 1, 1)
    gw_conv[...] += dot(gc[...], taps[...], 1, 1)
    g_taps = dot(w_conv[...], gc[...], 1, 0)
    for q in range(group):
        span = slice(q * length, (q + 1) * length)
        g0, g1, g2 = (g_taps[k * inner : (k + 1) * inner, span] for k in range(3))
        both = jnp.concatenate([g1[:, :LANES], g2[:, :LANES]], axis=1).astype(bf16)
        back = dot(both, reads[q][0], 1, 1)
        if prompts:
            table[...] += back
        else:
            begin, owners, wide, later, near_one, near_two = reads[q]
            table[owners[0]] += back
            gt[0, :, span] = g1.astype(bf16)
            gt[1, :, span] = g2.astype(bf16)
            both = jnp.concatenate([gt[0, :, wide], gt[1, :, wide]], axis=1)
            table[owners[1]] += dot(both, later, 1, 1)
            g1, g2 = g1 * near_one, g2 * near_two
        g_mid = (g0 + shifted_left(g1, STEP) + shifted_left(g2, REACH)).astype(bf16)
        if pieces == 1:
            gs[0][q] = g_mid
        else:
            gs[0][q] = g_mid[:, : length - LANES]
            gs[1][q] = g_mid[:, length - LANES :]

    @pl.when(step == pl.num_programs(0) - 1)
    def _():
        table_out[...] = table[...].astype(bf16)
        if has_after:
            count, few, _ = chunks.shape
            gw_conv[:, 3 * inner + 1 : 3 * inner + 2] = jnp.sum(g_gain3[...], axis=1, keepdims=True)
            gw_conv[:, 3 * inner + 2 : 3 * inner + 3] = jnp.sum(g_shift3[...], axis=1, keepdims=True)
            twice = width // inner
            for r in range(count):
                parts = [gw_conv[r * few : (r + 1) * few, : 3 * inner + 3]]
                for h in range(r * twice, (r + 1) * twice):
                    parts.append(gw_out[h * few : (h + 1) * few, : inner + 1])
                chunks[r] = jnp.concatenate(parts, axis=1).astype(bf16)


def middle(prompts, group, scalars, mids, x, cot, tails, weights, before=None, chunks=0):
    batches, _, width, length = x.shape
    inner = mids[0].shape[1]
    block = lambda a: blocks(a.shape, a.shape[-1], group, 0)
    args = list(scalars) + mids + [x, cot, tails] + list(weights) + list(before or ())
    in_specs = [pl.BlockSpec(memory_space=pltpu.SMEM)] * len(scalars)
    in_specs += [block(a) for a in mids + [x, cot]]
    in_specs += [WHOLE] * (len(args) - len(in_specs))
    out_like = [shape_of(*x.shape, kind=bf16)]
    out_like += [shape_of(*mid.shape, kind=bf16) for mid in mids]
    sums = [
        shape_of(width, inner + 16),
        shape_of(inner, 3 * inner + 16),
        shape_of(inner, LANES),
        shape_of(inner, LANES),
        shape_of(*tails.shape, kind=bf16),
    ]
    if chunks:
        wide = 3 * inner + 3 + (width // inner) * (inner + 1)
        sums.append(shape_of(chunks, inner // chunks, wide, kind=bf16))
    total = group * length
    kept, sums = (sums[:4], sums[4:]) if chunks else ([], sums)
    scratch = [pltpu.VMEM(a.shape, f32) for a in kept]
    scratch += [
        pltpu.VMEM((3 * inner + 16, total), bf16),
        pltpu.VMEM((inner + 16, total), bf16),
        pltpu.VMEM((inner, total), bf16),
        pltpu.VMEM((2, inner, total), bf16),
        pltpu.VMEM((inner, total), f32),
        pltpu.VMEM((inner, total), f32),
        pltpu.VMEM((width, total), bf16),
    ]
    scratch.append(pltpu.VMEM(tails.shape, f32))
    return pl.pallas_call(
        functools.partial(
            middle_kernel, batches, prompts, group, len(mids), before is not None, chunks > 0
        ),
        grid=(batches // group,),
        in_specs=in_specs,
        out_specs=[block(a) for a in out_like] + [WHOLE] * len(sums),
        out_shape=out_like + sums,
        scratch_shapes=scratch,
        compiler_params=PARAMS,
        cost_estimate=cost(batches * length * 9 * inner * width, 3 * x.size * 2),
        name="middle",
    )(*args)


def inner_back_kernel(has_rim, has_before, has_after, *refs):
    (act_ref, g_ref, n2_ref, r2_ref, vec2), refs = refs[:5], refs[5:]
    if has_rim:
        rim, refs = refs[0], refs[1:]
    if has_before:
        before, refs = refs[:3], refs[3:]
    gh_ref, sums, refs = refs[0], refs[1:4], refs[4:]
    if has_after:
        in_chunks, refs = refs[0], refs[1:]
    (kept,) = refs
    gw_in, g_gain2, g_shift2 = sums
    inner = vec2.shape[1]
    step = pl.program_id(0)

    @pl.when(step == 0)
    def _():
        for k, ref in enumerate(sums):
            ref[...] = before[k][...] if has_before else jnp.zeros_like(ref)

    g, n2, r2, gh = (Columns(ref) for ref in (g_ref, n2_ref, r2_ref, gh_ref))

    def g_in(t, c):
        value = g.get(t, c)
        if has_rim:
            piece = rim[t, c * REACH : (c + 1) * REACH]
            value += jnp.concatenate([jnp.zeros((TILE, LANES - REACH), f32), piece], axis=1)
        return value

    def keep(t, c, u):
        kept[t, at(c)] = u

    totals = backward_pass(g.count, inner, n2.get, g_in, vec2, (g_gain2, g_shift2), keep)
    for c in range(g.count):
        mean_u, mean_un = totals[c]
        scale = r2.get(ROW, c)
        by_n, constant = -(scale * mean_un), -(scale * mean_u)
        for t in tiles(inner):
            gh.put(t, c, kept[t, at(c)] * scale + (n2.get(t, c) * by_n + constant))
    for q in range(act_ref.shape[0]):
        gw_in[...] += dot(gh_ref[q], act_ref[q], 1, 1)

    if has_after:

        @pl.when(step == pl.num_programs(0) - 1)
        def _():
            count, few, wide = in_chunks.shape
            gw_in[:, wide - 2 : wide - 1] = jnp.sum(g_gain2[...], axis=1, keepdims=True)
            gw_in[:, wide - 1 : wide] = jnp.sum(g_shift2[...], axis=1, keepdims=True)
            for r in range(count):
                in_chunks[r] = gw_in[r * few : (r + 1) * few, :wide].astype(bf16)


def inner_back(act, g, n2, r2, part, vec2, rim=None, before=None, chunks=0):
    inner = vec2.shape[1]
    batches, width = act.shape[0], act.shape[1] - 16
    lanes, group, first = part
    in_specs = [blocks(act.shape, lanes, group, first)]
    in_specs += [blocks(a.shape, lanes, group, 0) for a in (g, n2, r2)] + [WHOLE]
    args = [act, g, n2, r2, vec2]
    if rim is not None:
        args.append(rim)
        in_specs.append(pl.BlockSpec((inner, GROUP * REACH), lambda i: (0, i)))
    if before is not None:
        args += before
        in_specs += [WHOLE] * 3
    sums = [shape_of(inner, width + 16), shape_of(inner, LANES), shape_of(inner, LANES)]
    if chunks:
        sums.append(shape_of(chunks, inner // chunks, width + 3, kind=bf16))
    return pl.pallas_call(
        functools.partial(inner_back_kernel, rim is not None, before is not None, chunks > 0),
        grid=(batches // group,),
        in_specs=in_specs,
        out_specs=[blocks(g.shape, lanes, group, 0)] + [WHOLE] * len(sums),
        out_shape=[shape_of(*g.shape, kind=bf16)] + sums,
        scratch_shapes=[pltpu.VMEM((inner, group * lanes), f32)],
        compiler_params=PARAMS,
        cost_estimate=cost(4 * width * inner * batches * lanes, 0),
        name="inner_back",
    )(*args)


def outer_back_kernel(pieces, has_before, has_into, has_after, *refs):
    (x_ref, cot_ref, mean_ref, scale_ref), refs = refs[:4], refs[4:]
    ghs, refs = refs[:pieces], refs[pieces:]
    (w_in, vec1), refs = refs[:2], refs[2:]
    if has_before:
        before, refs = refs[:2], refs[2:]
    if has_into:
        refs = refs[1:]
    out_ref, sums, refs = refs[0], refs[1:3], refs[3:]
    if has_after:
        small, refs = refs[0], refs[1:]
    (g_act,) = refs
    width = w_in.shape[0]
    step = pl.program_id(0)

    @pl.when(step == 0)
    def _():
        for k, ref in enumerate(sums):
            ref[...] = before[k][...] if has_before else jnp.zeros_like(ref)

    first = 0
    for gh in ghs:
        length = gh.shape[-1]
        g_act[:, first : first + length] = dot(w_in[...], gh[0], 1, 0)
        first += length
    x, cot, mean, scale, out = (Columns(r) for r in (x_ref, cot_ref, mean_ref, scale_ref, out_ref))
    scales = [scale.get(ROW, c) for c in range(x.count)]
    means = [mean.get(ROW, c) for c in range(x.count)]
    shifts = [a * b for a, b in zip(means, scales)]

    def keep(t, c, u):
        g_act[t, at(c)] = u

    totals = backward_pass(
        x.count,
        width,
        lambda t, c: x.get(t, c) * scales[c] - shifts[c],
        lambda t, c: g_act[t, at(c)],
        vec1,
        sums,
        keep,
        kind=bf16,
    )
    for c in range(x.count):
        mean_u, mean_un = totals[c]
        by_x = -(scales[c] * scales[c] * mean_un)
        constant = -(scales[c] * mean_u) - means[c] * by_x
        for t in tiles(width):
            change = g_act[t, at(c)] * scales[c] + (x.get(t, c) * by_x + constant)
            out.put(t, c, cot.get(t, c) + change)

    if has_after:

        @pl.when(step == pl.num_programs(0) - 1)
        def _():
            for k in range(2):
                small[:, k * width : (k + 1) * width] = down(sums[k][...].T)


def outer_back(
    x, cot, mean, scale, ghs, w_in, vec1, batches, before=None, into=None, last=False
):
    first, count = batches
    width, lanes = x.shape[2:]
    block = lambda a: blocks(a.shape, a.shape[-1], 1, 0, first)
    args = [x, cot, mean, scale] + ghs
    in_specs = [block(a) for a in args] + [WHOLE] * 2
    args += [w_in, vec1]
    if before is not None:
        args += before
        in_specs += [WHOLE] * 2
    aliases = {}
    if into is not None:
        aliases = {len(args): 0}
        args.append(into)
        in_specs.append(pl.BlockSpec(memory_space=pl.ANY))
    sums = [shape_of(width, LANES), shape_of(width, LANES)]
    if last:
        sums.append(shape_of(1, 2 * width))
    return pl.pallas_call(
        functools.partial(
            outer_back_kernel, len(ghs), before is not None, into is not None, last
        ),
        grid=(count,),
        in_specs=in_specs,
        out_specs=[block(x)] + [WHOLE] * len(sums),
        out_shape=[shape_of(*x.shape)] + sums,
        scratch_shapes=[pltpu.VMEM((width, lanes), f32)],
        input_output_aliases=aliases,
        compiler_params=PARAMS,
        cost_estimate=cost(8 * w_in.size * count * lanes, 0),
        name="outer_back",
    )(*args)


def packing_kernel(inner, ids, early_ref, late_ref, *refs):
    pieces, packed = refs[:-1], refs[-1]
    early, late = (jnp.sum(ref[...].astype(f32), axis=0) for ref in (early_ref, late_ref))
    shards = len(pieces)
    width = late.shape[1] - 3
    own, wide = inner // shards, width // shards
    conv_end = 3 * inner + 3
    firsts = range(conv_end, early.shape[1], inner + 1)
    kept = [early[:, first + inner : first + inner + 1] for first in firsts]
    kept += [early[:, 3 * inner : conv_end], late[:, width:]]
    starts = list(firsts) + [k * inner for k in range(3)]
    for j in range(shards):
        parts = [early[:, first + j * own : first + (j + 1) * own] for first in starts]
        parts += [late[:, j * wide : (j + 1) * wide]]
        packed[ids[0] ^ j] = jnp.concatenate(parts + kept, axis=1)
    for k in range(shards):
        pieces[k][...] = packed[k].astype(pieces[k].dtype)


def packing(ids, shards, inner, early, late):
    few, width = early.shape[1], late.shape[2] - 3
    wide = (2 * width + 3 * inner) // shards + width // inner + 6
    kinds = [f32] + [bf16] * (shards - 1)
    return pl.pallas_call(
        functools.partial(packing_kernel, inner),
        in_specs=[pl.BlockSpec(memory_space=pltpu.SMEM)] + [WHOLE] * 2,
        out_specs=[WHOLE] * shards,
        out_shape=[shape_of(few, wide, kind=kind) for kind in kinds],
        scratch_shapes=[pltpu.VMEM((shards, few, wide), f32)],
        compiler_params=PARAMS,
        name="packing",
    )(ids, early, late)


def unpacking_kernel(whole, by_out, by_conv, by_in, by_width, by_inner, tall, tall_in):
    reps, few, _ = whole.shape
    own, width = by_out.shape
    inner = by_conv.shape[1]
    wide = by_in.shape[0]
    twice = width // inner
    first_in = (twice + 3) * own
    small = first_in + wide
    for r in range(reps):
        piece = whole[r].astype(f32)
        for h in range(twice):
            rows = slice((r * twice + h) * few, (r * twice + h + 1) * few)
            tall[rows, :own] = piece[:, h * own : (h + 1) * own]
            tall[rows, own : own + 1] = piece[:, small + h : small + h + 1]
        rows = slice(r * few, (r + 1) * few)
        for k in range(3):
            by_conv[k, rows, :] = piece[:, (twice + k) * own : (twice + k + 1) * own]
        tall_in[rows, :wide] = piece[:, first_in : first_in + wide]
        tall_in[rows, wide : wide + 6] = piece[:, small + twice : small + twice + 6]
    turned = tall[...].T
    by_out[...] = turned[:own]
    by_width[...] = turned[own : own + 1]
    turned = tall_in[...].T
    by_in[...] = turned[:wide]
    by_inner[...] = turned[wide : wide + 6]


def unpacking(whole, shards, inner, width):
    own, wide = inner // shards, width // shards
    up = lambda n: -(-n // LANES) * LANES
    return pl.pallas_call(
        unpacking_kernel,
        in_specs=[WHOLE],
        out_specs=[WHOLE] * 5,
        out_shape=[
            shape_of(own, width),
            shape_of(3, inner, own),
            shape_of(wide, inner),
            shape_of(1, width),
            shape_of(6, inner),
        ],
        scratch_shapes=[
            pltpu.VMEM((width, up(own + 1)), f32),
            pltpu.VMEM((inner, up(wide + 6)), f32),
        ],
        compiler_params=PARAMS,
        name="unpacking",
    )(whole)


def passed_along(x, axis, by):
    size = lax.axis_size(axis)
    pairs = [(i, i + by) for i in range(size) if 0 <= i + by < size]
    return lax.ppermute(x, axis, pairs)


def swapped(x, axis, k):
    return lax.ppermute(x, axis, [(i, i ^ k) for i in range(lax.axis_size(axis))])


def gathered(x):
    size = lax.axis_size("shard")
    return jnp.stack([x] + [swapped(x, "shard", k) for k in range(1, size)])


def after(value, *others):
    return lax.optimization_barrier((value,) + others)[0]


def sent_from_last(x, axis):
    size = lax.axis_size(axis)
    me = lax.axis_index(axis)
    value = x
    for j in range(size - 1):
        piece = lax.ppermute(x, axis, [(size - 1, j)])
        value = jnp.where(me == j, piece, value)
    return value


def summed_at_last(x, axis):
    size = lax.axis_size(axis)
    total = x.astype(f32)
    for j in range(size - 1):
        total = total + lax.ppermute(x, axis, [(j, size - 1)]).astype(f32)
    return total


def dealt(x, axis):
    return lax.all_to_all(x, axis, 0, 0, tiled=True)


def collected(x, axis):
    return dealt(jnp.broadcast_to(x[None], (lax.axis_size(axis),) + x.shape), axis)


def on_device(
    prompt_x,
    cont_x,
    cont_map,
    cont_start,
    w_in,
    w_conv,
    w_out,
    norm1_gain,
    norm1_bias,
    bias_in,
    norm2_gain,
    norm2_bias,
    bias_conv,
    norm3_gain,
    norm3_bias,
    bias_out,
    prompt_cot,
    cont_cot,
):
    inner = w_conv.shape[2]
    turned = lambda a: jnp.swapaxes(a, 2, 3)
    prompt_x, cont_x, prompt_cot, cont_cot = map(turned, (prompt_x, cont_x, prompt_cot, cont_cot))
    width = prompt_x.shape[2]
    shards, reps = lax.axis_size("shard"), lax.axis_size("rep")
    is_last = lax.axis_index("shard") == shards - 1
    own = w_out.shape[0]
    parts = splits(own)
    ids = jnp.stack([lax.axis_index("shard"), lax.axis_index("rep") % 2]).astype(jnp.int32)
    norms = (norm1_gain, norm1_bias, norm2_gain, norm2_bias, norm3_gain, norm3_bias)
    row = jnp.concatenate(norms + (bias_in, bias_conv, bias_out))[None]
    after_norms = 2 * width + 4 * inner
    in_part, rest_part, vec1, vec2, vec3 = sending(ids, w_in, w_conv, w_out, row)
    rows_p, rows_c = prompt_x.shape[3], cont_x.shape[3]
    last = (LANES, GROUP, rows_p - LANES)
    rest = (rows_p - LANES, 1, 0)
    every = (rows_c, 1, 0)
    have_first = rows_p > LANES
    act_p, mean_p, scale_p, act_c, mean_c, scale_c = lead([prompt_x, cont_x], vec1)
    in_pieces, act_p = lax.optimization_barrier((gathered(in_part), act_p))
    half_in, w_in_t = taking_in(ids, in_pieces, row, after_norms, inner)
    mid_l, n2_l, r2_l, rim = front([act_p], [last], w_in_t, vec2, with_rim=True)
    halo = passed_along(rim, "shard", 1)
    rest_pieces, act_c, rim = lax.optimization_barrier((gathered(rest_part), act_c, rim))
    if parts == 2:
        rest_pieces = jnp.stack([rest_pieces, swapped(rest_pieces, "rep", 1)])
    else:
        rest_pieces = rest_pieces[None]
    own_tail = sent_from_last(rim, "shard")
    if have_first:
        mid_f, n2_f, r2_f, mid_c, n2_c, r2_c = front([act_p, act_c], [rest, every], w_in_t, vec2)
        mids = [mid_f, mid_l]
    else:
        mid_c, n2_c, r2_c = front([act_c], [every], w_in_t, vec2)
        mids = [mid_l]
    rest_pieces, own_tail, mid_c = lax.optimization_barrier((rest_pieces, own_tail, mid_c))
    tails = collected(own_tail, "rep")

    weights = (*taking_rest(ids, rest_pieces, row, after_norms + inner, inner, width), vec3)
    prompt_out, *results = middle(True, 2, [], mids, prompt_x, prompt_cot, halo, weights)
    g_ps, results = results[: len(mids)], results[len(mids) :]
    sums, rim_out = results[:4], results[4]
    back_rim = passed_along(rim_out, "shard", -1)
    cont_out, g_c, *results = middle(
        False,
        2,
        [jnp.transpose(a, (1, 2, 0)) for a in (cont_start, cont_map)],
        [mid_c],
        cont_x,
        cont_cot,
        tails,
        weights,
        before=sums,
        chunks=reps,
    )
    table, early = results
    table = dealt(table, "rep")

    sums = None
    gh_ps = []
    if have_first:
        gh_f, *sums = inner_back(act_p, g_ps[0], n2_f, r2_f, rest, vec2)
        gh_ps.append(gh_f)
    gh_c, *sums = inner_back(act_c, g_c, n2_c, r2_c, every, vec2, before=sums)
    table, gh_c = lax.optimization_barrier((table, gh_c))
    own_tail = jnp.sum(table.astype(f32), axis=0).astype(bf16)
    own_tail, early = lax.optimization_barrier((own_tail, early))
    own_tail = summed_at_last(own_tail, "shard")
    early = dealt(early, "rep")
    batches = prompt_x.shape[0]
    one, two = (0, batches // 2), (batches // 2, batches // 2)
    outer_c = functools.partial(
        outer_back, cont_x, cont_cot, mean_c, scale_c, [gh_c], half_in, vec1
    )
    outer_p = functools.partial(outer_back, prompt_x, prompt_cot, mean_p, scale_p)
    cont_grad, *sums1 = outer_c(one)
    cont_grad, own_tail = lax.optimization_barrier((cont_grad, own_tail))
    rim_in = back_rim.astype(f32) + jnp.where(is_last, own_tail, 0.0)
    gh_l, *results = inner_back(
        act_p, g_ps[-1], n2_l, r2_l, last, vec2, rim=rim_in, before=sums, chunks=reps
    )
    late, early, gh_l = lax.optimization_barrier((results[3], early, gh_l))
    gh_ps.append(gh_l)
    late = dealt(late, "rep")
    cont_grad, *sums1 = outer_c(two, before=sums1, into=after(cont_grad, gh_l))
    late, cont_grad = lax.optimization_barrier((late, cont_grad))

    mine, *others = packing(ids, shards, inner, early, late)
    others = [swapped(other, "shard", k + 1) for k, other in enumerate(others)]
    prompt_grad, *sums1 = outer_p(
        gh_ps, half_in, vec1, one, before=[after(sums1[0], mine), sums1[1]]
    )
    *others, prompt_grad = lax.optimization_barrier((*others, prompt_grad))
    mine = mine + sum(other.astype(f32) for other in others)
    whole = collected(mine, "rep")
    prompt_grad, *results = outer_p(
        gh_ps, half_in, vec1, two, before=sums1, into=after(prompt_grad, mine), last=True
    )
    ones = jnp.sum(lax.optimization_barrier(lax.all_gather(results[2], "rep")), axis=0)
    whole, ones = lax.optimization_barrier((whole, ones))
    ones = (ones + sum(swapped(ones, "shard", k) for k in range(1, shards)))[0]
    grad_w_out, grad_w_conv, grad_w_in, grad_bias_out, small = unpacking(whole, shards, inner, width)
    grad_bias_conv, grad_gain3, grad_shift3, grad_bias_in, grad_gain2, grad_shift2 = small
    return (
        turned(prompt_out),
        turned(cont_out),
        turned(prompt_grad),
        turned(cont_grad),
        grad_w_in,
        jnp.swapaxes(grad_w_conv, 1, 2),
        grad_w_out,
        ones[:width],
        ones[width:],
        grad_bias_in,
        grad_gain2,
        grad_shift2,
        grad_bias_conv,
        grad_gain3,
        grad_shift3,
        grad_bias_out[0],
    )


def solution(mesh):
    rows = P(None, "rep", "shard", None)
    buffers = P(None, ("rep", "shard"), None, None)
    in_specs = (
        rows,
        buffers,
        P(None, ("rep", "shard"), None),
        P(None, ("rep", "shard"), None),
        P("shard", None),
        P(None, "shard", None),
        P("shard", None),
    ) + (P(),) * 9 + (rows, buffers)
    out_specs = (
        rows,
        buffers,
        rows,
        buffers,
        P("shard", None),
        P(None, "shard", None),
        P("shard", None),
    ) + (P(),) * 9
    return jax.shard_map(
        on_device, mesh=mesh, in_specs=in_specs, out_specs=out_specs, check_vma=False
    )
```

```python
import functools

import jax
import jax.numpy as jnp
from jax import lax
from jax.experimental import pallas as pl
from jax.experimental.pallas import tpu as pltpu
from jax.sharding import PartitionSpec as P

STEP = 16
REACH = 2 * STEP
LANES = 128
GROUP = 4
TILE = 16
epsilon = 1e-05
bf16 = jnp.bfloat16
f32 = jnp.float32
VMEM_BYTES = 58 * 2**20
WHOLE = pl.BlockSpec(memory_space=pltpu.VMEM)
PARAMS = pltpu.CompilerParams(vmem_limit_bytes=VMEM_BYTES)


def cost(flops, moved):
    return pl.CostEstimate(flops=int(2.5 * flops), bytes_accessed=int(moved), transcendentals=0)


def dot(a, b, ca, cb):
    return lax.dot_general(a, b, (((ca,), (cb,)), ((), ())), preferred_element_type=f32)


def at(column):
    return slice(column * LANES, (column + 1) * LANES)


def tiles(depth):
    return [slice(r, r + TILE) for r in range(0, depth, TILE)]


class Columns:
    def __init__(self, ref):
        self.ref = ref
        self.per = ref.shape[-1] // LANES
        self.count = ref.shape[0] * self.per

    def key(self, rows, c):
        return (c // self.per,) + (0,) * (len(self.ref.shape) - 3) + (rows, at(c % self.per))

    def get(self, rows, c):
        return self.ref[self.key(rows, c)].astype(f32)

    def put(self, rows, c, values):
        self.ref[self.key(rows, c)] = values.astype(self.ref.dtype)


ROW = slice(0, 1)


def down(values):
    return jnp.sum(values, axis=0, keepdims=True)


def stats(load, depth, columns):
    zero = jnp.zeros((TILE, LANES), f32)
    sums = [zero] * columns
    for t in tiles(depth):
        sums = [s + load(t, c) for c, s in enumerate(sums)]
    means = [down(s) * (1.0 / depth) for s in sums]
    sums = [zero] * columns
    for t in tiles(depth):
        for c in range(columns):
            center = load(t, c) - means[c]
            sums[c] = sums[c] + center * center
    scales = [lax.rsqrt(down(s) * (1.0 / depth) + epsilon) for s in sums]
    return means, scales


def halved(vec):
    return 0.5 * vec


def backward_pass(columns, depth, normed, g_in, vec, sums, keep, act=None, kind=f32):
    g_gain, g_shift = sums
    unit = jnp.asarray(1.0, kind)
    zero = jnp.zeros((TILE, LANES), f32)
    totals = [[zero, zero] for _ in range(columns)]
    for t in tiles(depth):
        gain, shift = vec[0, t, :], vec[1, t, :]
        half_gain, half_shift = halved(gain).astype(kind), halved(shift).astype(kind)
        gains = shifts = None
        for c in range(columns):
            n = normed(t, c)
            half = n.astype(kind) * half_gain + half_shift
            tan = jnp.tanh(half)
            if act is not None:
                act(t, c, half * tan + half)
            slope = (unit + tan) * (unit + half * (unit - tan))
            g = g_in(t, c) * slope.astype(f32)
            gn = g * n
            u = g * gain
            keep(t, c, u)
            totals[c][0] = totals[c][0] + u
            totals[c][1] = totals[c][1] + gn * gain
            gains = gn if gains is None else gains + gn
            shifts = g if shifts is None else shifts + g
        g_gain[t, :] += gains
        g_shift[t, :] += shifts
    return [[down(s) * (1.0 / depth) for s in pair] for pair in totals]


def blocks(shape, lanes, group, first, batch=0):
    full = (group,) + tuple(shape[1:-1]) + (lanes,)
    zeros = (0,) * (len(shape) - 2)
    return pl.BlockSpec(full, lambda i: (i + batch // group,) + zeros + (first // lanes,))


def shape_of(*shape, kind=f32):
    return jax.ShapeDtypeStruct(shape, kind)


def splits(own):
    return 2 if own % 2 == 0 else 1


def sending_kernel(ids, w_in, w_conv_t, w_out, row, in_part, rest_part, *vecs):
    own, width = w_out.shape
    inner = w_conv_t.shape[1]
    parts = splits(own)
    few = own // parts
    some = in_part.shape[0]
    strips = [w_in[r : r + some, :] for r in range(0, w_in.shape[0], some)]
    in_part[...] = jnp.concatenate(strips, axis=1).astype(bf16)
    conv = [w_conv_t[k].T for k in range(3)]
    for h in range(parts):

        @pl.when(ids[1] % parts == h)
        def _():
            mine = slice(h * few, (h + 1) * few)
            pieces = [turn[mine] for turn in conv]
            pieces += [w_out[mine, q : q + inner] for q in range(0, width, inner)]
            rest_part[...] = jnp.concatenate(pieces, axis=1).astype(bf16)

    first = 0
    for vec in vecs:
        for k in range(2):
            depth = vec.shape[1]
            vec[k] = jnp.broadcast_to(row[:, first : first + depth], (LANES, depth)).T
            first += depth


def sending(ids, w_in, w_conv, w_out, row):
    own, width = w_out.shape
    inner = w_conv.shape[2]
    parts = splits(own)
    strips = 5 if w_in.shape[0] % 5 == 0 else 1
    return pl.pallas_call(
        sending_kernel,
        in_specs=[pl.BlockSpec(memory_space=pltpu.SMEM)] + [WHOLE] * 4,
        out_specs=[WHOLE] * 5,
        out_shape=[
            shape_of(w_in.shape[0] // strips, strips * inner, kind=bf16),
            shape_of(own // parts, (3 + width // inner) * inner, kind=bf16),
            shape_of(2, width, LANES),
            shape_of(2, inner, LANES),
            shape_of(2, inner, LANES),
        ],
        compiler_params=PARAMS,
        name="sending",
    )(ids, w_in, jnp.swapaxes(w_conv, 1, 2), w_out, row)


def with_shift(weights, shift):
    parts = []
    left = shift
    for _ in range(3):
        part = left.astype(bf16).astype(f32)
        parts.append(part)
        left = left - part
    parts.append(jnp.zeros((13, shift.shape[1]), f32))
    return jnp.concatenate([weights.T, jnp.concatenate(parts, axis=0).T], axis=1).astype(bf16)


def taking_in_kernel(where, ids, pieces, vecs, half_in, w_in_t, total):
    shards, some, wide = pieces.shape
    inner = total.shape[1]
    strips = wide // inner
    for j in range(shards):
        piece = pieces[ids[0] ^ j].astype(f32)
        for k in range(strips):
            first = (j * strips + k) * some
            total[first : first + some, :] = piece[:, k * inner : (k + 1) * inner]
    half_in[...] = (0.5 * total[...]).astype(bf16)
    w_in_t[...] = with_shift(total[...], vecs[:, where : where + inner])


def taking_in(ids, pieces, vecs, where, inner):
    shards, some, wide = pieces.shape
    width = shards * some * wide // inner
    return pl.pallas_call(
        functools.partial(taking_in_kernel, where),
        in_specs=[pl.BlockSpec(memory_space=pltpu.SMEM)] + [WHOLE] * 2,
        out_specs=[WHOLE] * 2,
        out_shape=[shape_of(width, inner, kind=bf16), shape_of(inner, width + 16, kind=bf16)],
        scratch_shapes=[pltpu.VMEM((width, inner), f32)],
        compiler_params=PARAMS,
        name="taking_in",
    )(ids, pieces, vecs)


def taking_rest_kernel(where, ids, pieces, vecs, *refs):
    (w_conv_t, half_conv, w_out_t, half_out), (conv, out) = refs[:4], refs[4:]
    parts, shards, few, _ = pieces.shape
    inner, width = out.shape
    for j in range(shards):
        for h in range(parts):
            first = (j * parts + h) * few
            piece = pieces[h ^ (ids[1] % parts), ids[0] ^ j].astype(f32)
            for k in range(3):
                strip = piece[:, k * inner : (k + 1) * inner]
                conv[k * inner + first : k * inner + first + few, :] = strip
            out[first : first + few, :] = piece[:, 3 * inner :]
    half_conv[...] = (0.5 * conv[...]).astype(bf16)
    w_conv_t[...] = with_shift(conv[...], vecs[:, where : where + inner])
    half_out[...] = (0.5 * out[...]).astype(bf16)
    w_out_t[...] = with_shift(out[...], vecs[:, where + inner : where + inner + width])


def taking_rest(ids, pieces, vecs, where, inner, width):
    return pl.pallas_call(
        functools.partial(taking_rest_kernel, where),
        in_specs=[pl.BlockSpec(memory_space=pltpu.SMEM)] + [WHOLE] * 2,
        out_specs=[WHOLE] * 4,
        out_shape=[
            shape_of(inner, 3 * inner + 16, kind=bf16),
            shape_of(3 * inner, inner, kind=bf16),
            shape_of(width, inner + 16, kind=bf16),
            shape_of(inner, width, kind=bf16),
        ],
        scratch_shapes=[pltpu.VMEM((3 * inner, inner), f32), pltpu.VMEM((inner, width), f32)],
        compiler_params=PARAMS,
        name="taking_rest",
    )(ids, pieces, vecs)


def lead_kernel(*refs):
    x_refs, vec1, outs = refs[:2], refs[2], refs[3:]
    for s in range(2):
        x, act, mean, scale = (Columns(ref) for ref in (x_refs[s],) + tuple(outs[3 * s : 3 * s + 3]))
        depth = x_refs[s].shape[-2]
        means, scales = stats(x.get, depth, x.count)
        for c in range(x.count):
            mean.put(ROW, c, means[c])
            scale.put(ROW, c, scales[c])
        shifts = [m * v for m, v in zip(means, scales)]
        for t in tiles(depth):
            gain, shift = halved(vec1[0, t, :]), halved(vec1[1, t, :])
            for c in range(x.count):
                half = (x.get(t, c) * scales[c] - shifts[c]) * gain + shift
                act.put(t, c, half * jnp.tanh(half) + half)
        for c in range(x.count):
            act.put(slice(depth, depth + 16), c, jnp.ones((16, LANES), f32))


def lead(xs, vec1):
    batches, _, width, _ = xs[0].shape
    in_specs, out_specs, out_shape = [], [], []
    for x in xs:
        lanes = x.shape[3]
        in_specs.append(blocks(x.shape, lanes, 1, 0))
        for depth, kind in ((width + 16, bf16), (1, f32), (1, f32)):
            out_specs.append(blocks((batches, depth, lanes), lanes, 1, 0))
            out_shape.append(shape_of(batches, depth, lanes, kind=kind))
    return pl.pallas_call(
        lead_kernel,
        grid=(batches,),
        in_specs=in_specs + [WHOLE],
        out_specs=out_specs,
        out_shape=out_shape,
        compiler_params=PARAMS,
        cost_estimate=cost(0, sum(x.size for x in xs) * 4),
        name="lead",
    )(*xs, vec1)


def front_kernel(streams, with_rim, *refs):
    acts, refs = refs[:streams], refs[streams:]
    (w_in_t, vec2), refs = refs[:2], refs[2:]
    outs, refs = [refs[3 * s : 3 * s + 3] for s in range(streams)], refs[3 * streams :]
    rim_ref = refs[0] if with_rim else None
    hiddens = refs[-streams:]
    inner = w_in_t.shape[0]
    for s in range(streams):
        act, hidden = acts[s], hiddens[s]
        mid, n2, r2 = (Columns(ref) for ref in outs[s])
        wide = act.shape[2]
        for q in range(act.shape[0]):
            hidden[:, q * wide : (q + 1) * wide] = dot(w_in_t[...], act[q], 1, 0)
        load = lambda t, c: hidden[t, at(c)]
        means, scales = stats(load, inner, mid.count)
        shifts = [m * v for m, v in zip(means, scales)]
        for c in range(mid.count):
            r2.put(ROW, c, scales[c])
        for t in tiles(inner):
            gain, shift = halved(vec2[0, t, :]), halved(vec2[1, t, :])
            rim = []
            for c in range(mid.count):
                n = load(t, c) * scales[c] - shifts[c]
                half = n * gain + shift
                value = half * jnp.tanh(half) + half
                mid.put(t, c, value)
                n2.put(t, c, n)
                rim.append(value[:, LANES - REACH :])
            if with_rim:
                rim_ref[t, :] = jnp.concatenate(rim, axis=1).astype(bf16)


def front(acts, parts, w_in_t, vec2, with_rim=False):
    inner = w_in_t.shape[0]
    batches = acts[0].shape[0]
    in_specs, out_specs, out_shape, scratch = [], [], [], []
    for act, (lanes, group, first) in zip(acts, parts):
        in_specs.append(blocks(act.shape, lanes, group, first))
        for depth, kind in ((inner, bf16), (inner, bf16), (1, f32)):
            out_specs.append(blocks((batches, depth, lanes), lanes, group, 0))
            out_shape.append(shape_of(batches, depth, lanes, kind=kind))
        scratch.append(pltpu.VMEM((inner, group * lanes), f32))
    if with_rim:
        out_specs.append(pl.BlockSpec((inner, GROUP * REACH), lambda i: (0, i)))
        out_shape.append(shape_of(inner, batches * REACH, kind=bf16))
    return pl.pallas_call(
        functools.partial(front_kernel, len(acts), with_rim),
        grid=(batches // parts[0][1],),
        in_specs=in_specs + [WHOLE] * 2,
        out_specs=out_specs,
        out_shape=out_shape,
        scratch_shapes=scratch,
        compiler_params=PARAMS,
        cost_estimate=cost(4 * w_in_t.size * sum(batches * part[0] for part in parts), 0),
        name="front",
    )(*acts, w_in_t, vec2)


def shifted_right(values, by):
    zeros = jnp.zeros((values.shape[0], by), values.dtype)
    return jnp.concatenate([zeros, values[:, : values.shape[1] - by]], axis=1)


def shifted_left(values, by):
    zeros = jnp.zeros((values.shape[0], by), values.dtype)
    return jnp.concatenate([values[:, by:], zeros], axis=1)


def chosen(base, position, fits, batches):
    one = jnp.where(jnp.logical_and(fits, position < STEP), base + STEP + position, -1)
    two = jnp.where(jnp.logical_and(fits, position < REACH), base + position, -1)
    target = jnp.concatenate([one, two], axis=1)
    row = lax.broadcasted_iota(jnp.int32, (batches * REACH, target.shape[1]), 0)
    return jnp.where(row == target, 1.0, 0.0).astype(bf16)


def middle_kernel(batches, prompts, group, pieces, has_before, has_after, *refs):
    if not prompts:
        (cont_start, cont_map), refs = refs[:2], refs[2:]
    mids, refs = refs[:pieces], refs[pieces:]
    (x_ref, cot_ref, tails), refs = refs[:3], refs[3:]
    (w_conv_t, w_conv, w_out_t, w_out, vec3), refs = refs[:5], refs[5:]
    if has_before:
        before, refs = refs[:4], refs[4:]
    out_ref, gs, refs = refs[0], refs[1 : 1 + pieces], refs[1 + pieces :]
    if has_after:
        (table_out, chunks), sums, refs = refs[:2], refs[2:6], refs[6:]
    else:
        sums, table_out, refs = refs[:4], refs[4], refs[5:]
    table, refs = refs[-1], refs[:-1]
    gw_out, gw_conv, g_gain3, g_shift3 = sums
    taps, act, gc, gt, conv, g_act, cots = refs
    width = w_out_t.shape[0]
    inner = w_out.shape[0]
    step = pl.program_id(0)
    length = taps.shape[1] // group
    columns = taps.shape[1] // LANES

    @pl.when(step == 0)
    def _():
        for k, ref in enumerate(sums):
            ref[...] = before[k][...] if has_before else jnp.zeros_like(ref)
        table[...] = jnp.zeros_like(table)
        taps[3 * inner :, :] = jnp.ones_like(taps[3 * inner :, :])
        act[inner:, :] = jnp.ones_like(act[inner:, :])

    reads = []
    for q in range(group):
        m = step * group + q
        base = m * REACH
        here = q * length
        span = slice(here, here + length)
        start_span = slice(here, here + LANES)
        cots[:, span] = cot_ref[q, 0]
        mid = mids[0][q] if pieces == 1 else jnp.concatenate([ref[q] for ref in mids], axis=1)
        lane = lax.broadcasted_iota(jnp.int32, (1, LANES), 1)
        if prompts:
            begin = chosen(base, lane, lane >= 0, batches)
            before_rows = tails[...]
            reads.append((begin,))
        else:
            start = cont_start[0, 1, m]
            owners = cont_map[0, 0, m], cont_map[0, 1, m]
            at_most = (length // LANES - 2) * LANES
            window = jnp.minimum(lax.shift_right_logical(start, 7) * LANES, at_most)
            wide = pl.ds(pl.multiple_of(here + window, LANES), 2 * LANES)
            begin = chosen(base, lane, lane < start, batches)
            before_rows = tails[owners[0]]
        first = dot(before_rows, begin, 1, 0).astype(bf16)
        taps[0:inner, span] = mid
        one, two = shifted_right(mid, STEP), shifted_right(mid, REACH)
        if not prompts:
            row = lax.broadcasted_iota(jnp.int32, (1, length), 1)
            since = jnp.where(row < start, row, row - start)
            near_one = jnp.where(since >= STEP, 1.0, 0.0)
            near_two = jnp.where(since >= REACH, 1.0, 0.0)
            full = lambda w: jnp.broadcast_to(w, (inner, length)).astype(bf16)
            one, two = one * full(near_one), two * full(near_two)
        taps[inner : 2 * inner, span] = one
        taps[2 * inner : 3 * inner, span] = two
        taps[inner : 2 * inner, start_span] += first[:, :LANES]
        taps[2 * inner : 3 * inner, start_span] += first[:, LANES:]
        if not prompts:
            offset = window + lax.broadcasted_iota(jnp.int32, (1, 2 * LANES), 1) - start
            later = chosen(base, offset, offset >= 0, batches)
            far = dot(tails[owners[1]], later, 1, 0).astype(bf16)
            taps[inner : 2 * inner, wide] += far[:, : 2 * LANES]
            taps[2 * inner : 3 * inner, wide] += far[:, 2 * LANES :]
            reads.append((begin, owners, wide, later, near_one, near_two))
    conv[...] = dot(w_conv_t[...], taps[...], 1, 0)
    g_act[...] = dot(w_out[...], cots[...], 1, 0)
    load = lambda t, c: conv[t, at(c)]
    means, scales = stats(load, inner, columns)
    shifts = [a * b for a, b in zip(means, scales)]

    def keep(t, c, u):
        g_act[t, at(c)] = u

    def put_act(t, c, value):
        act[t, at(c)] = value.astype(bf16)

    totals = backward_pass(
        columns,
        inner,
        lambda t, c: load(t, c) * scales[c] - shifts[c],
        lambda t, c: g_act[t, at(c)],
        vec3,
        (g_gain3, g_shift3),
        keep,
        put_act,
    )
    for c in range(columns):
        mean_u, mean_un = totals[c]
        by_x = -(scales[c] * scales[c] * mean_un)
        constant = -(scales[c] * mean_u) - means[c] * by_x
        for t in tiles(inner):
            g_in = g_act[t, at(c)] * scales[c] + (load(t, c) * by_x + constant)
            gc[t, at(c)] = g_in.astype(bf16)
    branch = dot(w_out_t[...], act[...], 1, 0)
    for q in range(group):
        span = slice(q * length, (q + 1) * length)
        out_ref[q, 0] = (x_ref[q, 0].astype(f32) + branch[:, span]).astype(bf16)
    gw_out[...] += dot(cots[...], act[...], 1, 1)
    gw_conv[...] += dot(gc[...], taps[...], 1, 1)
    g_taps = dot(w_conv[...], gc[...], 1, 0)
    for q in range(group):
        span = slice(q * length, (q + 1) * length)
        g0, g1, g2 = (g_taps[k * inner : (k + 1) * inner, span] for k in range(3))
        both = jnp.concatenate([g1[:, :LANES], g2[:, :LANES]], axis=1).astype(bf16)
        back = dot(both, reads[q][0], 1, 1)
        if prompts:
            table[...] += back
        else:
            begin, owners, wide, later, near_one, near_two = reads[q]
            table[owners[0]] += back
            gt[0, :, span] = g1.astype(bf16)
            gt[1, :, span] = g2.astype(bf16)
            both = jnp.concatenate([gt[0, :, wide], gt[1, :, wide]], axis=1)
            table[owners[1]] += dot(both, later, 1, 1)
            g1, g2 = g1 * near_one, g2 * near_two
        g_mid = (g0 + shifted_left(g1, STEP) + shifted_left(g2, REACH)).astype(bf16)
        if pieces == 1:
            gs[0][q] = g_mid
        else:
            gs[0][q] = g_mid[:, : length - LANES]
            gs[1][q] = g_mid[:, length - LANES :]

    @pl.when(step == pl.num_programs(0) - 1)
    def _():
        table_out[...] = table[...].astype(bf16)
        if has_after:
            count, few, _ = chunks.shape
            gw_conv[:, 3 * inner + 1 : 3 * inner + 2] = jnp.sum(g_gain3[...], axis=1, keepdims=True)
            gw_conv[:, 3 * inner + 2 : 3 * inner + 3] = jnp.sum(g_shift3[...], axis=1, keepdims=True)
            twice = width // inner
            for r in range(count):
                parts = [gw_conv[r * few : (r + 1) * few, : 3 * inner + 3]]
                for h in range(r * twice, (r + 1) * twice):
                    parts.append(gw_out[h * few : (h + 1) * few, : inner + 1])
                chunks[r] = jnp.concatenate(parts, axis=1).astype(bf16)


def middle(prompts, group, scalars, mids, x, cot, tails, weights, before=None, chunks=0):
    batches, _, width, length = x.shape
    inner = mids[0].shape[1]
    block = lambda a: blocks(a.shape, a.shape[-1], group, 0)
    args = list(scalars) + mids + [x, cot, tails] + list(weights) + list(before or ())
    in_specs = [pl.BlockSpec(memory_space=pltpu.SMEM)] * len(scalars)
    in_specs += [block(a) for a in mids + [x, cot]]
    in_specs += [WHOLE] * (len(args) - len(in_specs))
    out_like = [shape_of(*x.shape, kind=bf16)]
    out_like += [shape_of(*mid.shape, kind=bf16) for mid in mids]
    sums = [
        shape_of(width, inner + 16),
        shape_of(inner, 3 * inner + 16),
        shape_of(inner, LANES),
        shape_of(inner, LANES),
        shape_of(*tails.shape, kind=bf16),
    ]
    if chunks:
        wide = 3 * inner + 3 + (width // inner) * (inner + 1)
        sums.append(shape_of(chunks, inner // chunks, wide, kind=bf16))
    total = group * length
    kept, sums = (sums[:4], sums[4:]) if chunks else ([], sums)
    scratch = [pltpu.VMEM(a.shape, f32) for a in kept]
    scratch += [
        pltpu.VMEM((3 * inner + 16, total), bf16),
        pltpu.VMEM((inner + 16, total), bf16),
        pltpu.VMEM((inner, total), bf16),
        pltpu.VMEM((2, inner, total), bf16),
        pltpu.VMEM((inner, total), f32),
        pltpu.VMEM((inner, total), f32),
        pltpu.VMEM((width, total), bf16),
    ]
    scratch.append(pltpu.VMEM(tails.shape, f32))
    return pl.pallas_call(
        functools.partial(
            middle_kernel, batches, prompts, group, len(mids), before is not None, chunks > 0
        ),
        grid=(batches // group,),
        in_specs=in_specs,
        out_specs=[block(a) for a in out_like] + [WHOLE] * len(sums),
        out_shape=out_like + sums,
        scratch_shapes=scratch,
        compiler_params=PARAMS,
        cost_estimate=cost(batches * length * 9 * inner * width, 3 * x.size * 2),
        name="middle",
    )(*args)


def inner_back_kernel(has_rim, has_before, has_after, *refs):
    (act_ref, g_ref, n2_ref, r2_ref, vec2), refs = refs[:5], refs[5:]
    if has_rim:
        rim, refs = refs[0], refs[1:]
    if has_before:
        before, refs = refs[:3], refs[3:]
    gh_ref, sums, refs = refs[0], refs[1:4], refs[4:]
    if has_after:
        in_chunks, refs = refs[0], refs[1:]
    (kept,) = refs
    gw_in, g_gain2, g_shift2 = sums
    inner = vec2.shape[1]
    step = pl.program_id(0)

    @pl.when(step == 0)
    def _():
        for k, ref in enumerate(sums):
            ref[...] = before[k][...] if has_before else jnp.zeros_like(ref)

    g, n2, r2, gh = (Columns(ref) for ref in (g_ref, n2_ref, r2_ref, gh_ref))

    def g_in(t, c):
        value = g.get(t, c)
        if has_rim:
            piece = rim[t, c * REACH : (c + 1) * REACH]
            value += jnp.concatenate([jnp.zeros((TILE, LANES - REACH), f32), piece], axis=1)
        return value

    def keep(t, c, u):
        kept[t, at(c)] = u

    totals = backward_pass(g.count, inner, n2.get, g_in, vec2, (g_gain2, g_shift2), keep)
    for c in range(g.count):
        mean_u, mean_un = totals[c]
        scale = r2.get(ROW, c)
        by_n, constant = -(scale * mean_un), -(scale * mean_u)
        for t in tiles(inner):
            gh.put(t, c, kept[t, at(c)] * scale + (n2.get(t, c) * by_n + constant))
    for q in range(act_ref.shape[0]):
        gw_in[...] += dot(gh_ref[q], act_ref[q], 1, 1)

    if has_after:

        @pl.when(step == pl.num_programs(0) - 1)
        def _():
            count, few, wide = in_chunks.shape
            gw_in[:, wide - 2 : wide - 1] = jnp.sum(g_gain2[...], axis=1, keepdims=True)
            gw_in[:, wide - 1 : wide] = jnp.sum(g_shift2[...], axis=1, keepdims=True)
            for r in range(count):
                in_chunks[r] = gw_in[r * few : (r + 1) * few, :wide].astype(bf16)


def inner_back(act, g, n2, r2, part, vec2, rim=None, before=None, chunks=0):
    inner = vec2.shape[1]
    batches, width = act.shape[0], act.shape[1] - 16
    lanes, group, first = part
    in_specs = [blocks(act.shape, lanes, group, first)]
    in_specs += [blocks(a.shape, lanes, group, 0) for a in (g, n2, r2)] + [WHOLE]
    args = [act, g, n2, r2, vec2]
    if rim is not None:
        args.append(rim)
        in_specs.append(pl.BlockSpec((inner, GROUP * REACH), lambda i: (0, i)))
    if before is not None:
        args += before
        in_specs += [WHOLE] * 3
    sums = [shape_of(inner, width + 16), shape_of(inner, LANES), shape_of(inner, LANES)]
    if chunks:
        sums.append(shape_of(chunks, inner // chunks, width + 3, kind=bf16))
    return pl.pallas_call(
        functools.partial(inner_back_kernel, rim is not None, before is not None, chunks > 0),
        grid=(batches // group,),
        in_specs=in_specs,
        out_specs=[blocks(g.shape, lanes, group, 0)] + [WHOLE] * len(sums),
        out_shape=[shape_of(*g.shape, kind=bf16)] + sums,
        scratch_shapes=[pltpu.VMEM((inner, group * lanes), f32)],
        compiler_params=PARAMS,
        cost_estimate=cost(4 * width * inner * batches * lanes, 0),
        name="inner_back",
    )(*args)


def outer_back_kernel(pieces, has_before, has_into, has_after, *refs):
    (x_ref, cot_ref, mean_ref, scale_ref), refs = refs[:4], refs[4:]
    ghs, refs = refs[:pieces], refs[pieces:]
    (w_in, vec1), refs = refs[:2], refs[2:]
    if has_before:
        before, refs = refs[:2], refs[2:]
    if has_into:
        refs = refs[1:]
    out_ref, sums, refs = refs[0], refs[1:3], refs[3:]
    if has_after:
        small, refs = refs[0], refs[1:]
    (g_act,) = refs
    width = w_in.shape[0]
    step = pl.program_id(0)

    @pl.when(step == 0)
    def _():
        for k, ref in enumerate(sums):
            ref[...] = before[k][...] if has_before else jnp.zeros_like(ref)

    first = 0
    for gh in ghs:
        length = gh.shape[-1]
        g_act[:, first : first + length] = dot(w_in[...], gh[0], 1, 0)
        first += length
    x, cot, mean, scale, out = (Columns(r) for r in (x_ref, cot_ref, mean_ref, scale_ref, out_ref))
    scales = [scale.get(ROW, c) for c in range(x.count)]
    means = [mean.get(ROW, c) for c in range(x.count)]
    shifts = [a * b for a, b in zip(means, scales)]

    def keep(t, c, u):
        g_act[t, at(c)] = u

    totals = backward_pass(
        x.count,
        width,
        lambda t, c: x.get(t, c) * scales[c] - shifts[c],
        lambda t, c: g_act[t, at(c)],
        vec1,
        sums,
        keep,
        kind=bf16,
    )
    for c in range(x.count):
        mean_u, mean_un = totals[c]
        by_x = -(scales[c] * scales[c] * mean_un)
        constant = -(scales[c] * mean_u) - means[c] * by_x
        for t in tiles(width):
            change = g_act[t, at(c)] * scales[c] + (x.get(t, c) * by_x + constant)
            out.put(t, c, cot.get(t, c) + change)

    if has_after:

        @pl.when(step == pl.num_programs(0) - 1)
        def _():
            for k in range(2):
                small[:, k * width : (k + 1) * width] = down(sums[k][...].T)


def outer_back(
    x, cot, mean, scale, ghs, w_in, vec1, batches, before=None, into=None, last=False
):
    first, count = batches
    width, lanes = x.shape[2:]
    block = lambda a: blocks(a.shape, a.shape[-1], 1, 0, first)
    args = [x, cot, mean, scale] + ghs
    in_specs = [block(a) for a in args] + [WHOLE] * 2
    args += [w_in, vec1]
    if before is not None:
        args += before
        in_specs += [WHOLE] * 2
    aliases = {}
    if into is not None:
        aliases = {len(args): 0}
        args.append(into)
        in_specs.append(pl.BlockSpec(memory_space=pl.ANY))
    sums = [shape_of(width, LANES), shape_of(width, LANES)]
    if last:
        sums.append(shape_of(1, 2 * width))
    return pl.pallas_call(
        functools.partial(
            outer_back_kernel, len(ghs), before is not None, into is not None, last
        ),
        grid=(count,),
        in_specs=in_specs,
        out_specs=[block(x)] + [WHOLE] * len(sums),
        out_shape=[shape_of(*x.shape)] + sums,
        scratch_shapes=[pltpu.VMEM((width, lanes), f32)],
        input_output_aliases=aliases,
        compiler_params=PARAMS,
        cost_estimate=cost(8 * w_in.size * count * lanes, 0),
        name="outer_back",
    )(*args)


def packing_kernel(inner, ids, early_ref, late_ref, *refs):
    pieces, packed = refs[:-1], refs[-1]
    early, late = (jnp.sum(ref[...].astype(f32), axis=0) for ref in (early_ref, late_ref))
    shards = len(pieces)
    width = late.shape[1] - 3
    own, wide = inner // shards, width // shards
    conv_end = 3 * inner + 3
    firsts = range(conv_end, early.shape[1], inner + 1)
    kept = [early[:, first + inner : first + inner + 1] for first in firsts]
    kept += [early[:, 3 * inner : conv_end], late[:, width:]]
    starts = list(firsts) + [k * inner for k in range(3)]
    for j in range(shards):
        parts = [early[:, first + j * own : first + (j + 1) * own] for first in starts]
        parts += [late[:, j * wide : (j + 1) * wide]]
        packed[ids[0] ^ j] = jnp.concatenate(parts + kept, axis=1)
    for k in range(shards):
        pieces[k][...] = packed[k].astype(pieces[k].dtype)


def packing(ids, shards, inner, early, late):
    few, width = early.shape[1], late.shape[2] - 3
    wide = (2 * width + 3 * inner) // shards + width // inner + 6
    kinds = [f32] + [bf16] * (shards - 1)
    return pl.pallas_call(
        functools.partial(packing_kernel, inner),
        in_specs=[pl.BlockSpec(memory_space=pltpu.SMEM)] + [WHOLE] * 2,
        out_specs=[WHOLE] * shards,
        out_shape=[shape_of(few, wide, kind=kind) for kind in kinds],
        scratch_shapes=[pltpu.VMEM((shards, few, wide), f32)],
        compiler_params=PARAMS,
        name="packing",
    )(ids, early, late)


def unpacking_kernel(whole, by_out, by_conv, by_in, by_width, by_inner, tall, tall_in):
    reps, few, _ = whole.shape
    own, width = by_out.shape
    inner = by_conv.shape[1]
    wide = by_in.shape[0]
    twice = width // inner
    first_in = (twice + 3) * own
    small = first_in + wide
    for r in range(reps):
        piece = whole[r].astype(f32)
        for h in range(twice):
            rows = slice((r * twice + h) * few, (r * twice + h + 1) * few)
            tall[rows, :own] = piece[:, h * own : (h + 1) * own]
            tall[rows, own : own + 1] = piece[:, small + h : small + h + 1]
        rows = slice(r * few, (r + 1) * few)
        for k in range(3):
            by_conv[k, rows, :] = piece[:, (twice + k) * own : (twice + k + 1) * own]
        tall_in[rows, :wide] = piece[:, first_in : first_in + wide]
        tall_in[rows, wide : wide + 6] = piece[:, small + twice : small + twice + 6]
    turned = tall[...].T
    by_out[...] = turned[:own]
    by_width[...] = turned[own : own + 1]
    turned = tall_in[...].T
    by_in[...] = turned[:wide]
    by_inner[...] = turned[wide : wide + 6]


def unpacking(whole, shards, inner, width):
    own, wide = inner // shards, width // shards
    up = lambda n: -(-n // LANES) * LANES
    return pl.pallas_call(
        unpacking_kernel,
        in_specs=[WHOLE],
        out_specs=[WHOLE] * 5,
        out_shape=[
            shape_of(own, width),
            shape_of(3, inner, own),
            shape_of(wide, inner),
            shape_of(1, width),
            shape_of(6, inner),
        ],
        scratch_shapes=[
            pltpu.VMEM((width, up(own + 1)), f32),
            pltpu.VMEM((inner, up(wide + 6)), f32),
        ],
        compiler_params=PARAMS,
        name="unpacking",
    )(whole)


def passed_along(x, axis, by):
    size = lax.axis_size(axis)
    pairs = [(i, i + by) for i in range(size) if 0 <= i + by < size]
    return lax.ppermute(x, axis, pairs)


def swapped(x, axis, k):
    return lax.ppermute(x, axis, [(i, i ^ k) for i in range(lax.axis_size(axis))])


def gathered(x):
    size = lax.axis_size("shard")
    return jnp.stack([x] + [swapped(x, "shard", k) for k in range(1, size)])


def after(value, *others):
    return lax.optimization_barrier((value,) + others)[0]


def sent_from_last(x, axis):
    size = lax.axis_size(axis)
    me = lax.axis_index(axis)
    value = x
    for j in range(size - 1):
        piece = lax.ppermute(x, axis, [(size - 1, j)])
        value = jnp.where(me == j, piece, value)
    return value


def summed_at_last(x, axis):
    size = lax.axis_size(axis)
    total = x.astype(f32)
    for j in range(size - 1):
        total = total + lax.ppermute(x, axis, [(j, size - 1)]).astype(f32)
    return total


def dealt(x, axis):
    return lax.all_to_all(x, axis, 0, 0, tiled=True)


def collected(x, axis):
    return dealt(jnp.broadcast_to(x[None], (lax.axis_size(axis),) + x.shape), axis)


def on_device(
    prompt_x,
    cont_x,
    cont_map,
    cont_start,
    w_in,
    w_conv,
    w_out,
    norm1_gain,
    norm1_bias,
    bias_in,
    norm2_gain,
    norm2_bias,
    bias_conv,
    norm3_gain,
    norm3_bias,
    bias_out,
    prompt_cot,
    cont_cot,
):
    inner = w_conv.shape[2]
    turned = lambda a: jnp.swapaxes(a, 2, 3)
    prompt_x, cont_x, prompt_cot, cont_cot = map(turned, (prompt_x, cont_x, prompt_cot, cont_cot))
    width = prompt_x.shape[2]
    shards, reps = lax.axis_size("shard"), lax.axis_size("rep")
    is_last = lax.axis_index("shard") == shards - 1
    own = w_out.shape[0]
    parts = splits(own)
    ids = jnp.stack([lax.axis_index("shard"), lax.axis_index("rep") % 2]).astype(jnp.int32)
    norms = (norm1_gain, norm1_bias, norm2_gain, norm2_bias, norm3_gain, norm3_bias)
    row = jnp.concatenate(norms + (bias_in, bias_conv, bias_out))[None]
    after_norms = 2 * width + 4 * inner
    in_part, rest_part, vec1, vec2, vec3 = sending(ids, w_in, w_conv, w_out, row)
    rows_p, rows_c = prompt_x.shape[3], cont_x.shape[3]
    last = (LANES, GROUP, rows_p - LANES)
    rest = (rows_p - LANES, 1, 0)
    every = (rows_c, 1, 0)
    paired = lambda part: (part[0], 2, part[2])
    have_first = rows_p > LANES
    act_p, mean_p, scale_p, act_c, mean_c, scale_c = lead([prompt_x, cont_x], vec1)
    in_pieces, act_p = lax.optimization_barrier((gathered(in_part), act_p))
    half_in, w_in_t = taking_in(ids, in_pieces, row, after_norms, inner)
    mid_l, n2_l, r2_l, rim = front([act_p], [last], w_in_t, vec2, with_rim=True)
    halo = passed_along(rim, "shard", 1)
    rest_pieces, act_c, rim = lax.optimization_barrier((gathered(rest_part), act_c, rim))
    if parts == 2:
        rest_pieces = jnp.stack([rest_pieces, swapped(rest_pieces, "rep", 1)])
    else:
        rest_pieces = rest_pieces[None]
    own_tail = sent_from_last(rim, "shard")
    if have_first:
        mid_f, n2_f, r2_f, mid_c, n2_c, r2_c = front([act_p, act_c], [paired(rest), paired(every)], w_in_t, vec2)
        mids = [mid_f, mid_l]
    else:
        mid_c, n2_c, r2_c = front([act_c], [paired(every)], w_in_t, vec2)
        mids = [mid_l]
    rest_pieces, own_tail, mid_c = lax.optimization_barrier((rest_pieces, own_tail, mid_c))
    tails = collected(own_tail, "rep")

    weights = (*taking_rest(ids, rest_pieces, row, after_norms + inner, inner, width), vec3)
    prompt_out, *results = middle(True, 2, [], mids, prompt_x, prompt_cot, halo, weights)
    g_ps, results = results[: len(mids)], results[len(mids) :]
    sums, rim_out = results[:4], results[4]
    back_rim = passed_along(rim_out, "shard", -1)
    cont_out, g_c, *results = middle(
        False,
        2,
        [jnp.transpose(a, (1, 2, 0)) for a in (cont_start, cont_map)],
        [mid_c],
        cont_x,
        cont_cot,
        tails,
        weights,
        before=sums,
        chunks=reps,
    )
    table, early = results
    table = dealt(table, "rep")

    sums = None
    gh_ps = []
    if have_first:
        gh_f, *sums = inner_back(act_p, g_ps[0], n2_f, r2_f, rest, vec2)
        gh_ps.append(gh_f)
    gh_c, *sums = inner_back(act_c, g_c, n2_c, r2_c, every, vec2, before=sums)
    table, gh_c = lax.optimization_barrier((table, gh_c))
    own_tail = jnp.sum(table.astype(f32), axis=0).astype(bf16)
    own_tail, early = lax.optimization_barrier((own_tail, early))
    own_tail = summed_at_last(own_tail, "shard")
    early = dealt(early, "rep")
    batches = prompt_x.shape[0]
    one, two = (0, batches // 2), (batches // 2, batches // 2)
    outer_c = functools.partial(
        outer_back, cont_x, cont_cot, mean_c, scale_c, [gh_c], half_in, vec1
    )
    outer_p = functools.partial(outer_back, prompt_x, prompt_cot, mean_p, scale_p)
    cont_grad, *sums1 = outer_c(one)
    cont_grad, own_tail = lax.optimization_barrier((cont_grad, own_tail))
    rim_in = back_rim.astype(f32) + jnp.where(is_last, own_tail, 0.0)
    gh_l, *results = inner_back(
        act_p, g_ps[-1], n2_l, r2_l, last, vec2, rim=rim_in, before=sums, chunks=reps
    )
    late, early, gh_l = lax.optimization_barrier((results[3], early, gh_l))
    gh_ps.append(gh_l)
    late = dealt(late, "rep")
    cont_grad, *sums1 = outer_c(two, before=sums1, into=after(cont_grad, gh_l))
    late, cont_grad = lax.optimization_barrier((late, cont_grad))

    mine, *others = packing(ids, shards, inner, early, late)
    others = [swapped(other, "shard", k + 1) for k, other in enumerate(others)]
    prompt_grad, *sums1 = outer_p(
        gh_ps, half_in, vec1, one, before=[after(sums1[0], mine), sums1[1]]
    )
    *others, prompt_grad = lax.optimization_barrier((*others, prompt_grad))
    mine = mine + sum(other.astype(f32) for other in others)
    whole = collected(mine, "rep")
    prompt_grad, *results = outer_p(
        gh_ps, half_in, vec1, two, before=sums1, into=after(prompt_grad, mine), last=True
    )
    ones = jnp.sum(lax.optimization_barrier(lax.all_gather(results[2], "rep")), axis=0)
    whole, ones = lax.optimization_barrier((whole, ones))
    ones = (ones + sum(swapped(ones, "shard", k) for k in range(1, shards)))[0]
    grad_w_out, grad_w_conv, grad_w_in, grad_bias_out, small = unpacking(whole, shards, inner, width)
    grad_bias_conv, grad_gain3, grad_shift3, grad_bias_in, grad_gain2, grad_shift2 = small
    return (
        turned(prompt_out),
        turned(cont_out),
        turned(prompt_grad),
        turned(cont_grad),
        grad_w_in,
        jnp.swapaxes(grad_w_conv, 1, 2),
        grad_w_out,
        ones[:width],
        ones[width:],
        grad_bias_in,
        grad_gain2,
        grad_shift2,
        grad_bias_conv,
        grad_gain3,
        grad_shift3,
        grad_bias_out[0],
    )


def solution(mesh):
    rows = P(None, "rep", "shard", None)
    buffers = P(None, ("rep", "shard"), None, None)
    in_specs = (
        rows,
        buffers,
        P(None, ("rep", "shard"), None),
        P(None, ("rep", "shard"), None),
        P("shard", None),
        P(None, "shard", None),
        P("shard", None),
    ) + (P(),) * 9 + (rows, buffers)
    out_specs = (
        rows,
        buffers,
        rows,
        buffers,
        P("shard", None),
        P(None, "shard", None),
        P("shard", None),
    ) + (P(),) * 9
    return jax.shard_map(
        on_device, mesh=mesh, in_specs=in_specs, out_specs=out_specs, check_vma=False
    )
```
